32 devices in a mesh: ew: 4 (over y, x), ns: 8 (over z, core).
Axes of the slice: x: 2, y: 2, z: 4, core: 2. Of those that a mesh axis runs over, the one named last changes fastest.
Arguments:
- tokens: bfloat16 [8, 4, 2, 64, 768], P('ns', 'ew'), may hold values from -6 to 6
- vis_index: int32 [8, 4, 2, 64], P('ns', 'ew'), may hold values from 0 to 255, as said below
- counts: int32 [8, 4, 2], P('ns', 'ew'), may hold values from 32 to 64
- owners: int32 [8, 4, 2, 64, 1], P('ns', 'ew'), may hold values from 0 to 7; in each aligned block of 128 rows (0 to 127, 128 to 255, ..., all dimensions but the last counted through in order) at most 24 rows name the same one
- mask_token: bfloat16 [768], replicated, may hold values from -6 to 6
- proj_weight: bfloat16 [768, 64], replicated, may hold values from -0.21875 to 0.21875
- up_first: bfloat16 [4, 4, 64, 64], replicated, may hold values from -0.375 to 0.375
- up_second: bfloat16 [4, 4, 12, 64], replicated, may hold values from -0.375 to 0.375
- saved_pre: bfloat16 [2, 64, 64, 512], P(None, None, 'ns', 'ew'), may hold values from -6 to 6
- cotangent: bfloat16 [2, 12, 128, 1024], P(None, None, 'ns', 'ew'), may hold values from -6 to 6
Outputs:
- token_grad: bfloat16 [8, 4, 192, 768], P('ns', 'ew')
- grad_proj: float32 [768, 64], replicated
- grad_first: float32 [4, 4, 64, 64], replicated
- grad_second: float32 [4, 4, 12, 64], replicated
- grad_mask: float32 [768], replicated
The draws below stay inside these ranges and needn't reach their ends.
Inputs may be any that keep to these rules, and one draw needn't show every extreme that they name: `vis_index`: each entry is a patch number of its tile, patches numbered row by row with 64 to a row; the 64 entries of one tile and date are distinct; the live ones are the first counts entries. `owners`: among the 128 slots of one tile, live or not, at most 24 name the same owner.
All inputs are finite; a program needn't handle non-finite values.
Results may differ from the reference program's by a relative error of at most 0.0057.
Values may be sent and summed in bfloat16 or wider, within the bound.
No kernel may reach another device: no remote copies, remote signals or barrier semaphores. Data moves between devices by JAX's collectives and lax.ppermute only.
A program may use at most 64 MiB of HBM per device.

```python
import math
import jax
import jax.numpy as jnp
import numpy as np
from jax import lax

D = 768
C = 64
BANDS = 12
PH = 4
PW = 64
FRAMES = 2
VIS = 64
CAP = 24
ROWS_IN = 192
TILES_NS = 8
TILES_EW = 4
ROWS_MID = 64
COLS_MID = 512
ROWS_FINE = 128
COLS_FINE = 1024
N_EW = 4
N_NS = 8


def draw_vis_index(key, part):
    patches = PH * PW
    scores = jax.random.randint(key, (TILES_NS, TILES_EW, FRAMES, patches), 0, 1 << 20)
    scores = scores * patches + jnp.arange(patches, dtype=jnp.int32)
    ordering = jnp.argsort(scores, axis=-1).astype(jnp.int32)
    return ordering[..., :VIS]


def draw_counts(key, part):
    key_values, key_spot = jax.random.split(key)
    values = jax.random.randint(key_values, (TILES_NS, TILES_EW, FRAMES), VIS // 2, VIS + 1)
    chosen_spot = jax.random.randint(key_spot, (), 0, TILES_NS * TILES_EW * FRAMES)
    flattened = values.reshape(-1)
    positions = jnp.arange(flattened.shape[0], dtype=jnp.int32)
    flattened = jnp.where(positions == chosen_spot, VIS, flattened)
    return flattened.reshape(values.shape).astype(jnp.int32)


def block_levels(stream_key, dims, shards, smallest, largest):
    factor_of = 1.0
    for position, parts in shards:
        heights = jax.random.uniform(jax.random.fold_in(jax.random.fold_in(stream_key, 6), position), (parts,), jnp.float32, smallest / len(shards), largest / len(shards))
        factor_of = factor_of * jnp.repeat(jnp.exp(heights), dims[position] // parts).reshape((-1,) + (1,) * (len(dims) - 1 - position))
    return factor_of


def assign_block(stream_key, own, number, rows, amount, top, most, slope):
    ranking = jax.random.permutation(stream_key, amount)
    crowded, common = portions_of(amount, rows * top, most, slope, True), portions_of(amount, rows * top, most, slope, False)
    places = jnp.arange(amount)

    def named(tallies, rotation):
        used = int((tallies > 0).sum())
        fixed = max(1, used // 4)
        moved = fixed + (places - fixed + rotation * (used - fixed)) % max(1, amount - fixed)
        return jnp.zeros((amount,), jnp.int32).at[ranking[jnp.where(places < fixed, places, moved)]].set(jnp.asarray(tallies, jnp.int32))

    tallies = jnp.where(number % 4 == 0, named(crowded, number // 4), named(common, number - number // 4 - 1))
    mixed = jax.random.permutation(jax.random.fold_in(own, 3), amount)
    giver, taker = mixed[0:amount // 2 * 2:2], mixed[1:amount // 2 * 2:2]
    margin = jnp.minimum(tallies[giver] - 1, most - tallies[taker]) // 2
    margin = jnp.where((giver == ranking[0]) | (taker == ranking[0]) | (tallies[taker] == 0), 0, jnp.maximum(margin, 0))
    moved = jax.random.randint(jax.random.fold_in(own, 4), (amount // 2,), 0, 1 << 20) % (margin + 1)
    tallies = tallies.at[giver].add(-moved).at[taker].add(moved)
    items = jnp.searchsorted(jnp.cumsum(tallies), jnp.arange(rows * top), side="right").astype(jnp.int32)
    listing = items.reshape(top, rows).T
    listing = listing[jax.random.permutation(jax.random.fold_in(own, 1), rows)]
    rotation = jax.random.randint(jax.random.fold_in(own, 2), (rows, 1), 0, top)
    return jnp.take_along_axis(listing, (jnp.arange(top)[None, :] + rotation) % top, axis=1)


def portions_of(count, total, limit, slope, full):
    portions = [(1 << 20) // math.isqrt(standing ** slope) + 1 for standing in range(1, count + 1)]
    largest = limit if full else min(limit, max(-(-total // count), total * portions[0] // sum(portions)))
    least = 1 if total - largest >= count - 1 else 0
    holding, spare = [largest] + [least] * (count - 1), total - largest - least * (count - 1)
    while spare > 0:
        candidates = [i for i in range(1, count) if holding[i] < largest] or [i for i in range(1, count) if holding[i] < limit]
        mass, left = sum([portions[i] for i in candidates]), spare
        for i in candidates:
            addition = min(limit - holding[i], max(1, left * portions[i] // mass), spare)
            holding[i] = holding[i] + addition
            spare = spare - addition
    return np.array(holding)


def scatter_about(stream_key, extent, spread, reach, cuts=(), kind=jnp.bfloat16):
    gain = block_levels(stream_key, extent, cuts, -0.22, 0.18) if cuts else 1.0
    entries = jax.random.normal(stream_key, extent, jnp.float32) * spread * gain
    return jnp.minimum(jnp.maximum(entries, -reach), reach).astype(kind)


def setup_inputs(seed: int = 0) -> dict:
    seeds = jax.random.split(jax.random.key(seed), 11)
    tokens = scatter_about(seeds[0], (TILES_NS, TILES_EW, FRAMES, VIS, D), 1.0, 6.0, ((0, 8), (1, 4)))
    vis_index = draw_vis_index(jax.random.fold_in(seeds[10], 71), 0)
    counts = draw_counts(jax.random.fold_in(seeds[10], 71), 0)
    owners_keys = jax.random.split(jax.random.fold_in(seeds[3], 1), TILES_NS * TILES_EW * FRAMES * VIS // (FRAMES * VIS))
    owners_turns = jax.random.permutation(jax.random.fold_in(seeds[3], 3), TILES_NS * TILES_EW * FRAMES * VIS // (FRAMES * VIS))
    owners = jax.vmap(lambda own, number: assign_block(jax.random.fold_in(seeds[3], 2), own, number, FRAMES * VIS, N_NS, 1, CAP, 2))(owners_keys, owners_turns).reshape((TILES_NS, TILES_EW, FRAMES, VIS, 1))
    mask_token = scatter_about(seeds[4], (D,), 1.0, 6.0)
    proj_weight = scatter_about(seeds[5], (D, C), D ** -0.5, 0.21875)
    up_first = scatter_about(seeds[6], (4, 4, C, C), (4 * C) ** -0.5, 0.375)
    up_second = scatter_about(seeds[7], (4, 4, BANDS, C), (4 * C) ** -0.5, 0.375)
    saved_pre = scatter_about(seeds[8], (FRAMES, C, ROWS_MID, COLS_MID), 1.0, 6.0, ((2, 8), (3, 4)))
    cotangent = scatter_about(seeds[9], (FRAMES, BANDS, ROWS_FINE, COLS_FINE), 1.0, 6.0, ((2, 8), (3, 4)))
    return {"tokens": tokens, "vis_index": vis_index, "counts": counts, "owners": owners, "mask_token": mask_token, "proj_weight": proj_weight, "up_first": up_first, "up_second": up_second, "saved_pre": saved_pre, "cotangent": cotangent}


def gelu_value(preact):
    return preact * jax.nn.sigmoid(1.702 * preact)


def gelu_slope(preact):
    sigmoid_value = jax.nn.sigmoid(1.702 * preact)
    return sigmoid_value + 1.702 * preact * sigmoid_value * (1.0 - sigmoid_value)


def transpose_back(inputs, padded, kernel):
    height = inputs.shape[2]
    breadth = inputs.shape[3]
    inputs_wide = inputs.astype(jnp.float32)
    padded_wide = padded.astype(jnp.float32)
    kernel_wide = kernel.astype(jnp.float32)
    grad_inputs = jnp.zeros(inputs.shape, jnp.float32)
    grad_taps = []
    for tap_y in range(4):
        for tap_x in range(4):
            window = padded_wide[:, :, tap_y:tap_y + 2 * height:2, tap_x:tap_x + 2 * breadth:2]
            grad_inputs = grad_inputs + jnp.einsum("oi,fohw->fihw", kernel_wide[tap_y, tap_x], window)
            grad_taps.append(jnp.einsum("fihw,fohw->oi", inputs_wide, window))
    grad_kernel = jnp.stack(grad_taps).reshape((4, 4) + kernel.shape[2:])
    return grad_inputs, grad_kernel


def reference(tokens, vis_index, counts, owners, mask_token, proj_weight, up_first, up_second, saved_pre, cotangent):
    patches = PH * PW
    slot_ids = jnp.arange(VIS, dtype=jnp.int32)
    live = slot_ids[None, None, None, :] < counts[:, :, :, None]
    ns_ids = jnp.broadcast_to(jnp.arange(N_NS, dtype=jnp.int32)[:, None, None], (N_NS, N_EW, VIS))
    ew_ids = jnp.broadcast_to(jnp.arange(N_EW, dtype=jnp.int32)[None, :, None], (N_NS, N_EW, VIS))
    mask_proj = jnp.dot(mask_token[None, :], proj_weight, preferred_element_type=jnp.float32).astype(jnp.bfloat16)[0]

    def frame_step(carry, frame_data):
        grad_proj, grad_first, grad_second, mask_sum = carry
        frame_tokens, frame_index, frame_live, frame_pre, frame_cot = frame_data
        target = jnp.where(frame_live, frame_index, patches).astype(jnp.int32)
        token_proj = jnp.dot(frame_tokens.reshape(-1, D), proj_weight, preferred_element_type=jnp.float32).astype(jnp.bfloat16)
        token_proj = token_proj.reshape(N_NS, N_EW, VIS, C)
        first_tiles = jnp.broadcast_to(mask_proj, (N_NS, N_EW, patches, C))
        first_tiles = first_tiles.at[ns_ids, ew_ids, target].set(token_proj, mode="drop")
        shown = jnp.zeros((N_NS, N_EW, patches), jnp.float32).at[ns_ids, ew_ids, target].set(1.0, mode="drop")
        first_grid = first_tiles.reshape(N_NS, N_EW, PH, PW, C).transpose(4, 0, 2, 1, 3).reshape(1, C, N_NS * PH, N_EW * PW)
        cot_pad = jnp.pad(frame_cot[None], ((0, 0), (0, 0), (1, 1), (1, 1)))
        pre_wide = frame_pre.astype(jnp.float32)[None]
        hidden = gelu_value(pre_wide).astype(jnp.bfloat16)
        grad_hidden, second_term = transpose_back(hidden, cot_pad, up_second)
        deltas = (grad_hidden * gelu_slope(pre_wide)).astype(jnp.bfloat16)
        deltas_pad = jnp.pad(deltas, ((0, 0), (0, 0), (1, 1), (1, 1)))
        grad_grid, first_term = transpose_back(first_grid, deltas_pad, up_first)
        grad_grid = grad_grid.astype(jnp.bfloat16)[0]
        grad_tiles = grad_grid.reshape(C, N_NS, PH, N_EW, PW).transpose(1, 3, 2, 4, 0).reshape(N_NS, N_EW, patches, C)
        safe_index = jnp.clip(frame_index, 0, patches - 1).astype(jnp.int32)
        chosen = grad_tiles[ns_ids, ew_ids, safe_index]
        chosen = jnp.where(frame_live[..., None], chosen, jnp.zeros_like(chosen))
        proj_term = jnp.einsum("tevd,tevc->dc", frame_tokens.astype(jnp.float32), chosen.astype(jnp.float32))
        mask_term = jnp.einsum("tep,tepc->c", 1.0 - shown, grad_tiles.astype(jnp.float32))
        carry = (grad_proj + proj_term, grad_first + first_term, grad_second + second_term, mask_sum + mask_term)
        return carry, chosen

    start = (jnp.zeros((D, C), jnp.float32), jnp.zeros((4, 4, C, C), jnp.float32),
             jnp.zeros((4, 4, BANDS, C), jnp.float32), jnp.zeros((C,), jnp.float32))
    frame_data = (tokens.transpose(2, 0, 1, 3, 4), vis_index.transpose(2, 0, 1, 3), live.transpose(2, 0, 1, 3),
                  saved_pre, cotangent)
    totals, chosen_all = lax.scan(frame_step, start, frame_data)
    grad_proj, grad_first, grad_second, mask_sum = totals
    grad_proj = grad_proj + mask_token.astype(jnp.float32)[:, None] * mask_sum[None, :]
    grad_mask = jnp.dot(proj_weight.astype(jnp.float32), mask_sum, precision=lax.Precision.HIGHEST)

    rows_all = FRAMES * VIS
    chosen_rows = chosen_all.transpose(1, 2, 0, 3, 4).reshape(N_NS, N_EW, rows_all, C)
    owner_rows = owners.reshape(N_NS, N_EW, rows_all).astype(jnp.int32)
    live_rows = live.reshape(N_NS, N_EW, rows_all)
    owner_hits = ((owner_rows[..., None] == jnp.arange(N_NS, dtype=jnp.int32)) & live_rows[..., None]).astype(jnp.int32)
    earlier = jnp.cumsum(owner_hits, axis=2, dtype=jnp.int32) - owner_hits
    place = jnp.sum(earlier * owner_hits, axis=-1, dtype=jnp.int32)
    source_ns = jnp.broadcast_to(jnp.arange(N_NS, dtype=jnp.int32)[:, None, None], (N_NS, N_EW, rows_all))
    source_ew = jnp.broadcast_to(jnp.arange(N_EW, dtype=jnp.int32)[None, :, None], (N_NS, N_EW, rows_all))
    flat_index = (owner_rows * N_EW + source_ew) * ROWS_IN + source_ns * CAP + place
    flat_index = jnp.where(live_rows, flat_index, N_NS * N_EW * ROWS_IN).astype(jnp.int32)
    narrow = jnp.zeros((N_NS * N_EW * ROWS_IN, C), jnp.bfloat16)
    narrow = narrow.at[flat_index.reshape(-1)].set(chosen_rows.reshape(-1, C), mode="drop")

    def widen(block_rows):
        return jnp.dot(block_rows, proj_weight.T, preferred_element_type=jnp.float32).astype(jnp.bfloat16)

    token_grad = lax.map(widen, narrow.reshape(N_NS, N_EW * ROWS_IN, C)).reshape(N_NS, N_EW, ROWS_IN, D)
    return token_grad, grad_proj, grad_first, grad_second, grad_mask
```

```python
import functools

import jax
import jax.numpy as jnp
import numpy as np
from jax import lax
from jax.experimental import pallas as pl
from jax.experimental.pallas import tpu as pltpu
from jax.sharding import PartitionSpec as P

BF = jnp.bfloat16
F32 = jnp.float32
VMEM = pl.BlockSpec(memory_space=pltpu.VMEM)
GROUP = 16
GRAD_ROWS = 1024
PROJ_AT = 512
SECOND_AT = 896
MASK_ROW = SECOND_AT + 12


def nn(a, b):
    return lax.dot_general(a, b, (((1,), (0,)), ((), ())), preferred_element_type=F32)


def nt(a, b):
    return lax.dot_general(a, b, (((1,), (1,)), ((), ())), preferred_element_type=F32)


def tn(a, b):
    return lax.dot_general(a, b, (((0,), (0,)), ((), ())), preferred_element_type=F32)


def iota(shape, dim):
    return lax.broadcasted_iota(jnp.int32, shape, dim)


def one_hot(shape, pairs, shift=0):
    matrix = np.zeros(shape, np.float32)
    for row, col in pairs:
        matrix[row, col + shift] = 1.0
    return matrix


def column_tables(cols):
    half = cols // 2
    fine = 2 * cols

    def hidden_cols(arrangement):
        if arrangement == 0:
            return [2 * j for j in range(half)] + [2 * j + 1 for j in range(half)]
        return [2 * j + 2 for j in range(half)] + [2 * j - 1 for j in range(half)]

    def pixel_row(x):
        return x if 0 <= x < fine else (x if x >= fine else fine + 6 + x)

    def hidden_row(x):
        return x if 0 <= x <= cols else cols + 1

    pixels = np.zeros((fine + 128, 4 * 2 * cols), np.float32)
    cells = np.zeros((2 * cols, 2 * cols), np.float32)
    for arrangement in range(2):
        for lane, col in enumerate(hidden_cols(arrangement)):
            cells[hidden_row(col), arrangement * cols + lane] = 1.0
            for tap in range(4):
                pixels[pixel_row(2 * col + tap - 1), (tap * 2 + arrangement) * cols + lane] = 1.0
    return pixels, cells


def pack_kernel(cot_ref, pre_ref, edge_ref, g_ref, p_ref, own_ref, a_ref, b_ref, cot_wide, pre_wide):
    frames, bands, prow, pcol = cot_ref.shape
    _, chans, rows, cols = pre_ref.shape
    wide_rows = frames * GROUP * prow
    halves = range(pcol // cols)
    for f in range(frames):
        for o in range(GROUP):
            at = (f * GROUP + o) * prow
            band = cot_ref[f, o].astype(F32) if o < bands else jnp.zeros((prow, pcol), F32)
            for h in halves:
                cot_wide[pl.ds(h * wide_rows + at, prow), :] = band[:, h * cols : (h + 1) * cols]
        for c in range(chans):
            pre_wide[pl.ds((f * chans + c) * rows, rows), :] = pre_ref[f, c].astype(F32)
    for f in range(frames):
        for y in range(prow):
            for h in halves:
                g_ref[pl.ds((f * prow + y) * GROUP, GROUP), h * cols : (h + 1) * cols] = cot_wide[
                    pl.ds(h * wide_rows + f * GROUP * prow + y, GROUP, stride=prow), :
                ].astype(BF)
        for r in range(rows):
            p_ref[pl.ds((f * rows + r) * chans, chans), :] = pre_wide[
                pl.ds(f * chans * rows + r, chans, stride=rows), :
            ].astype(BF)
    pick_g = edge_ref[:, :pcol]
    pick_p = edge_ref[:, pcol:]
    edges_p = nt(pick_p, p_ref[...])
    edges_g = nt(pick_g, g_ref[...])
    width = edges_g.shape[1]
    own_ref[:, :width] = (edges_g + edges_p[:, :width]).astype(BF)
    own_ref[:, width:] = edges_p[:, width:].astype(BF)

    def message(out_ref, top):
        first = 0 if top else prow - 3
        line = 0 if top else rows - 1
        for f in range(frames):
            out_ref[pl.ds(f * 3 * GROUP, 3 * GROUP), :] = g_ref[
                pl.ds((f * prow + first) * GROUP, 3 * GROUP), :
            ]
            out_ref[pl.ds(frames * 3 * GROUP, chans), f * cols : (f + 1) * cols] = p_ref[
                pl.ds((f * rows + line) * chans, chans), :
            ]
        at = frames * 3 * GROUP + chans
        out_ref[pl.ds(at, 16), :] = jnp.zeros((16, pcol), BF)
        out_ref[pl.ds(at, 16), : frames * 3 * GROUP] = nt(
            pick_g, out_ref[pl.ds(0, frames * 3 * GROUP), :]
        ).astype(BF)
        for f in range(frames):
            out_ref[pl.ds(at, 16), cols + f * chans : cols + (f + 1) * chans] = nt(
                pick_p, p_ref[pl.ds((f * rows + line) * chans, chans), :]
            ).astype(BF)

    even = lax.rem(lax.axis_index("ns"), 2) == 0

    @pl.when(even)
    def _():
        message(a_ref, False)
        message(b_ref, True)

    @pl.when(jnp.logical_not(even))
    def _():
        message(a_ref, True)
        message(b_ref, False)


def token_kernel(
    capacity, ids_ref, tokens_ref, mask_ref, proj_ref, first_ref, second_ref,
    grid_ref, pick_ref, hidden_ref, route_ref, wab_ref, w2_ref,
):
    slots_all = tokens_ref.shape[0]
    frames, slots, patches = pick_ref.shape
    chans = proj_ref.shape[1]
    bands = second_ref.shape[2]
    owners = route_ref.shape[0] // GROUP
    half = capacity // 2
    eye = (iota((chans, chans), 0) == iota((chans, chans), 1)).astype(BF)
    pad = jnp.zeros((GROUP - bands, chans), BF)
    taps = []
    for b in range(4):
        for a in range(4):
            taps.append(jnp.concatenate([second_ref[a, b], pad], axis=0))
    w2_ref[...] = nt(eye, jnp.concatenate(taps, axis=0)).astype(BF)
    left = (iota((2 * chans, chans), 0) == iota((2 * chans, chans), 1)).astype(BF)
    right = (iota((2 * chans, chans), 0) == iota((2 * chans, chans), 1) + chans).astype(BF)
    for arrangement, (lo, hi) in enumerate(((1, 2), (3, 0))):
        taps_lo = jnp.concatenate([first_ref[a, lo] for a in range(4)], axis=0)
        taps_hi = jnp.concatenate([first_ref[a, hi] for a in range(4)], axis=0)
        wab_ref[:, arrangement * 4 * chans : (arrangement + 1) * 4 * chans] = (
            nt(left, taps_lo) + nt(right, taps_hi)
        ).astype(BF)
    vis = ids_ref[0:1, :]
    owner = ids_ref[1:2, :]
    live = ids_ref[2:3, :]
    wanted = jnp.where(live > 0, vis, patches)
    square = (slots_all, slots_all)
    column = jnp.sum(
        jnp.where(iota(square, 0) == iota(square, 1), wanted.astype(F32), 0.0), axis=1, keepdims=True
    ).astype(jnp.int32)
    token_proj = nn(tokens_ref[...], proj_ref[...]).astype(BF)
    mask_proj = nn(jnp.broadcast_to(mask_ref[...], (16, mask_ref.shape[1])), proj_ref[...]).astype(BF)
    row0 = iota((16, patches), 0) == 0
    lane = iota((chans, 2 * chans), 1)
    for f in range(frames):
        hits = iota((slots, patches), 1) == column[f * slots : (f + 1) * slots]
        picks = hits.astype(F32)
        pick_ref[f] = picks.astype(BF)
        unseen = jnp.where(row0, 1.0 - jnp.sum(picks, axis=0, keepdims=True), 0.0).astype(BF)
        hidden_ref[:, f * patches : (f + 1) * patches] = unseen
        grid = tn(token_proj[f * slots : (f + 1) * slots], picks.astype(BF)) + tn(mask_proj, unseen)
        for pair in range(patches // (2 * chans)):
            straight = grid[:, pair * 2 * chans : (pair + 1) * 2 * chans]
            turned = pltpu.roll(straight, chans, 1)
            k = f * (patches // (2 * chans)) + pair
            zero = jnp.zeros_like(straight)
            grid_ref[k, :chans, : 2 * chans] = jnp.where(lane < chans, straight, zero).astype(BF)
            grid_ref[k, chans:, : 2 * chans] = jnp.where(lane < chans, zero, turned).astype(BF)
            grid_ref[k, :chans, 2 * chans :] = jnp.where(lane < chans, turned, zero).astype(BF)
            grid_ref[k, chans:, 2 * chans :] = jnp.where(lane < chans, zero, straight).astype(BF)
    own_rows = -(-owners // 16) * 16
    hit = (iota((own_rows, slots_all), 0) == jnp.where(live > 0, owner, -1)).astype(F32)
    before = (iota(square, 0) < iota(square, 1)).astype(BF)
    earlier = nn(hit.astype(BF), before)
    place = jnp.sum(earlier * hit, axis=0, keepdims=True).astype(jnp.int32)
    for h in range(2):
        inside = (live > 0) & (place >= h * half) & (place < (h + 1) * half)
        target = jnp.where(inside, owner * GROUP + place - h * half, -1)
        route_ref[:, h * slots_all : (h + 1) * slots_all] = (
            iota((owners * GROUP, slots_all), 0) == target
        ).astype(F32).astype(BF)


def tile_kernel(
    n_ew, rows_each, g_ref, p_ref, ra_ref, rb_ref, ea_ref, eb_ref, pix_ref, cell_ref, halo_ref,
    grid_ref, pick_ref, hidden_ref, route_ref, wab_ref, w2_ref, tokens_ref, mask_ref,
    out_ref, ext, wide, wins, pres, deltas, routed,
):
    frames, slots, patches = pick_ref.shape
    chans = w2_ref.shape[0]
    pcol = g_ref.shape[1]
    cols = p_ref.shape[1]
    rows = p_ref.shape[0] // (frames * chans)
    prow = 2 * rows
    n_ns = route_ref.shape[0] // GROUP
    ns = lax.axis_index("ns")
    ew = lax.axis_index("ew")
    even_ns = lax.rem(ns, 2) == 0
    even_ew = lax.rem(ew, 2) == 0
    ra, rb = ra_ref[...], rb_ref[...]
    north = jnp.where(even_ns, rb, ra)
    south = jnp.where(even_ns, ra, rb)
    ea, eb = ea_ref[...], eb_ref[...]
    sides = jnp.concatenate([jnp.where(even_ew, ea, eb), jnp.where(even_ew, eb, ea)], axis=0)
    own_len = frames * rows * chans
    xa = sides[:, own_len : own_len + pcol]
    xb = sides[:, own_len + pcol : own_len + 2 * pcol]
    side_n = jnp.where(even_ns, xb, xa)
    side_s = jnp.where(even_ns, xa, xb)
    pick_g = halo_ref[:, :128]
    pick_p = halo_ref[:, 128:256]
    g_len = frames * prow * GROUP
    edge = frames * 3 * GROUP
    own_g = tn(sides[:, :g_len], pick_g).astype(BF)
    north_g = tn(side_n[:, :128], pick_g).astype(BF)
    south_g = tn(side_s[:, :128], pick_g).astype(BF)
    own_p = tn(sides[:, :own_len], pick_p).astype(BF)
    north_p = tn(side_n[:, 128:256], pick_p).astype(BF)
    south_p = tn(side_s[:, 128:256], pick_p).astype(BF)
    tall = (prow + 6) * GROUP
    high = (rows + 2) * chans
    for f in range(frames):
        base = f * tall
        top, mid, low = 3 * GROUP, prow * GROUP, 3 * GROUP
        ext[pl.ds(base, top), :pcol] = north[f * top : (f + 1) * top]
        ext[pl.ds(base, top), pcol:] = north_g[f * top : (f + 1) * top]
        ext[pl.ds(base + top, mid), :pcol] = g_ref[pl.ds(f * mid, mid), :]
        ext[pl.ds(base + top, mid), pcol:] = own_g[f * mid : (f + 1) * mid]
        ext[pl.ds(base + top + mid, low), :pcol] = south[f * low : (f + 1) * low]
        ext[pl.ds(base + top + mid, low), pcol:] = south_g[f * low : (f + 1) * low]
        base = f * high
        mid = rows * chans
        wide[pl.ds(base, chans), :cols] = north[edge : edge + chans, f * cols : (f + 1) * cols]
        wide[pl.ds(base, chans), cols:] = north_p[f * chans : (f + 1) * chans]
        wide[pl.ds(base + chans, mid), :cols] = p_ref[pl.ds(f * mid, mid), :]
        wide[pl.ds(base + chans, mid), cols:] = own_p[f * mid : (f + 1) * mid]
        wide[pl.ds(base + chans + mid, chans), :cols] = south[
            edge : edge + chans, f * cols : (f + 1) * cols
        ]
        wide[pl.ds(base + chans + mid, chans), cols:] = south_p[f * chans : (f + 1) * chans]
    for f in range(frames):
        block = ext[pl.ds(f * tall, tall), :]
        for b in range(4):
            lanes = slice(b * 2 * cols, (b + 1) * 2 * cols)
            wins[pl.ds(f * tall, tall), lanes] = nn(block, pix_ref[:, lanes]).astype(BF)
        pres[pl.ds(f * high, high), :] = nn(wide[pl.ds(f * high, high), :], cell_ref[...])
    w2 = w2_ref[...]
    lane = iota((chans, 2 * cols), 1)
    outside_col = ((lane == cols + cols // 2 - 1) & (ew == n_ew - 1)) | (
        (lane == cols + cols // 2) & (ew == 0)
    )
    zero = jnp.zeros((chans, cols), BF)
    grad_second = None
    for f in range(frames):
        for i in range(rows + 2):
            at = f * tall + 2 * i * GROUP
            taps = [wins[pl.ds(at, 4 * GROUP), b * 2 * cols : (b + 1) * 2 * cols] for b in range(4)]
            grad_hidden = nn(w2, jnp.concatenate(taps, axis=0))
            v = pres[pl.ds(f * high + i * chans, chans), :]
            s = 0.5 + 0.5 * jnp.tanh(0.851 * v)
            delta = grad_hidden * (s + 1.702 * v * s * (1.0 - s))
            drop = outside_col
            if i == 0:
                drop = drop | (ns == 0)
            if i == rows + 1:
                drop = drop | (ns == n_ns - 1)
            deltas[pl.ds(f * high + i * chans, chans), :] = jnp.where(drop, 0.0, delta).astype(BF)
            if 1 <= i <= rows:
                hid = (v[:, :cols] * s[:, :cols]).astype(BF)
                lhs = jnp.concatenate(
                    [
                        jnp.concatenate([taps[0][:, :cols], taps[2][:, :cols]], axis=1),
                        jnp.concatenate([taps[1][:, :cols], taps[3][:, :cols]], axis=1),
                    ],
                    axis=0,
                )
                rhs = jnp.concatenate(
                    [
                        jnp.concatenate([hid, zero], axis=1),
                        jnp.concatenate([zero, hid], axis=1),
                    ],
                    axis=0,
                )
                term = nt(lhs, rhs)
                grad_second = term if grad_second is None else grad_second + term
    wab = wab_ref[...]
    half_lane = iota((chans, cols), 1) < cols // 2
    grad_first = None
    grids = []
    for f in range(frames):
        parts = []
        for pair in range(rows // 4):
            cells = []
            for odd in range(2):
                at = f * high + (2 * pair + odd) * 2 * chans
                slab = deltas[pl.ds(at, 4 * chans), :]
                cells.append(jnp.concatenate([slab[:, :cols], slab[:, cols:]], axis=0))
            both = jnp.concatenate(cells, axis=1)
            term = nt(both, grid_ref[f * (rows // 4) + pair])
            grad_first = term if grad_first is None else grad_first + term
            turn = nn(wab, both)
            here = jnp.where(half_lane, turn[:chans, :cols], turn[chans:, cols:])
            there = jnp.where(half_lane, turn[:chans, cols:], turn[chans:, :cols])
            parts.append(here + pltpu.roll(there, cols // 2, 1))
        grids.append(jnp.concatenate(parts, axis=1).astype(BF))
    none = jnp.zeros((chans, patches), BF)
    mask_sum = nt(hidden_ref[...], jnp.concatenate(grids, axis=1))
    lower = [nt(pick_ref[f], jnp.concatenate([grids[f], none], axis=0)) for f in range(frames)]
    upper = [nt(pick_ref[f], jnp.concatenate([none, grids[f]], axis=0)) for f in range(frames)]
    chosen = jnp.concatenate(lower + upper, axis=0).astype(BF)
    routed[...] = nn(route_ref[...], chosen).astype(BF)
    features = tokens_ref.shape[1]
    tokens = tokens_ref[...]
    split = jnp.concatenate([tokens[:, : features // 2], tokens[:, features // 2 :]], axis=0)
    hi = mask_sum.astype(BF).astype(F32)
    lo = mask_sum - hi
    nothing = jnp.zeros_like(hi)
    hi_left = jnp.concatenate([hi, nothing], axis=1)[0:1]
    hi_right = jnp.concatenate([nothing, hi], axis=1)[0:1]
    lo_left = jnp.concatenate([lo, nothing], axis=1)[0:1]
    lo_right = jnp.concatenate([nothing, lo], axis=1)[0:1]
    line = iota((16, 2 * chans), 0)
    mask_rows = jnp.where(line == 0, hi_left, 0.0) + jnp.where(line == 1, hi_right, 0.0)
    mask_rows = mask_rows + jnp.where(line == 2, lo_left, 0.0) + jnp.where(line == 3, lo_right, 0.0)
    mask_token = mask_ref[...].astype(F32)
    line = iota((16, features // 2), 0)
    spread = jnp.where(
        (line == 0) | (line == 2),
        mask_token[:, : features // 2],
        jnp.where((line == 1) | (line == 3), mask_token[:, features // 2 :], 0.0),
    )
    grad_proj = tn(split, chosen) + tn(spread.astype(BF), mask_rows.astype(BF))
    mark = iota(grad_second.shape, 0) == MASK_ROW - SECOND_AT
    grad_second = jnp.where(mark, hi_left + lo_right, grad_second)
    total = jnp.concatenate([grad_first, grad_proj, grad_second], axis=0).astype(BF)
    count = out_ref.shape[0]
    for d in range(GRAD_ROWS // rows_each):
        out_ref[d, :rows_each, :] = total[d * rows_each : (d + 1) * rows_each]
    if count * rows_each > GRAD_ROWS:

        @pl.loop(GRAD_ROWS // rows_each, count)
        def _(d):
            out_ref[d, :rows_each, :] = jnp.zeros((rows_each, 2 * chans), BF)

    def place(d):
        source = pl.multiple_of(lax.rem(d, n_ns) * GROUP, GROUP)
        out_ref[d, rows_each:, :] = routed[pl.ds(source, GROUP), :]

    if count <= 64:
        for d in range(count):
            out_ref[d, rows_each:, :] = routed[pl.ds((d % n_ns) * GROUP, GROUP), :]
    else:
        pl.loop(0, count)(place)


def owner_kernel(n_ns, capacity, rows_each, got_ref, proj_ref, sum_ref, token_ref):
    count = got_ref.shape[0]
    chans = proj_ref.shape[1]
    if count <= 64:
        total = got_ref[0, :rows_each, :].astype(F32)
        for d in range(1, count):
            total = total + got_ref[d, :rows_each, :].astype(F32)
    else:
        total = lax.fori_loop(
            0,
            count,
            lambda d, acc: acc + got_ref[d, :rows_each, :].astype(F32),
            jnp.zeros((rows_each, 2 * chans), F32),
        )
    share = total.astype(BF)
    if count <= 64:
        for d in range(count):
            sum_ref[d] = share
    else:

        @pl.loop(0, count)
        def _(d):
            sum_ref[d] = share

    half = capacity // 2
    ew = lax.axis_index("ew")
    arrived = jnp.concatenate(
        [got_ref[ew * n_ns + s, rows_each:, :] for s in range(n_ns)], axis=0
    )
    shape = (n_ns * capacity, n_ns * GROUP)
    row, col = iota(shape, 0), iota(shape, 1)
    slot = lax.rem(row, capacity)
    source = (row // capacity) * GROUP + lax.rem(slot, half)
    picked = nn((source == col).astype(F32).astype(BF), arrived)
    second = lax.rem(iota(picked.shape, 0), capacity) >= half
    picked = jnp.where(second, pltpu.roll(picked, chans, 1), picked)[:, :chans].astype(BF)
    token_ref[...] = nt(picked, proj_ref[...]).astype(BF)


def finish_kernel(got_ref, proj_ref, proj_out, first_out, second_out, mask_out):
    chans = proj_ref.shape[1]
    bands = second_out.shape[2]
    rows_each = got_ref.shape[1]
    parts = [got_ref[d] for d in range(GRAD_ROWS // rows_each)]
    total = jnp.concatenate(parts, axis=0).astype(F32)
    turned = pltpu.roll(total, chans, 1)
    low, high = total[:, :chans], turned[:, :chans]
    for arrangement, taps in enumerate(((1, 2), (3, 0))):
        for a in range(4):
            at = (arrangement * 4 + a) * chans
            first_out[a, taps[0]] = low[at : at + chans]
            first_out[a, taps[1]] = high[at : at + chans]
    features = proj_ref.shape[0]
    proj_out[: features // 2, :] = low[PROJ_AT : PROJ_AT + features // 2]
    proj_out[features // 2 :, :] = high[PROJ_AT : PROJ_AT + features // 2]
    for b in range(2):
        for a in range(4):
            at = SECOND_AT + (b * 4 + a) * GROUP
            second_out[a, b] = low[at : at + bands]
            second_out[a, b + 2] = high[at : at + bands]
    mask_sum = low[MASK_ROW : MASK_ROW + 1] + high[MASK_ROW : MASK_ROW + 1]
    hi = mask_sum.astype(BF).astype(F32)
    mid = (mask_sum - hi).astype(BF).astype(F32)
    lo = mask_sum - hi - mid
    line = iota((16, chans), 0)
    rows = jnp.where(line == 0, hi, 0.0) + jnp.where(line == 1, mid, 0.0) + jnp.where(line == 2, lo, 0.0)
    mask_out[...] = jnp.sum(nt(rows.astype(BF), proj_ref[...]), axis=0, keepdims=True)


def swap(block, axis, offset):
    count = lax.axis_size(axis)
    pairs = [(i, ((i + offset) ^ 1) - offset) for i in range(count)]
    return lax.ppermute(block, axis, [(i, j) for i, j in pairs if 0 <= j < count])


def call(kernel, outs, args, scratch=(), flops=0, limit=None):
    return pl.pallas_call(
        kernel,
        out_shape=outs,
        in_specs=[VMEM] * len(args),
        out_specs=jax.tree.map(lambda _: VMEM, outs),
        scratch_shapes=list(scratch),
        compiler_params=pltpu.CompilerParams(vmem_limit_bytes=limit),
        cost_estimate=pl.CostEstimate(flops=flops, bytes_accessed=1 << 20, transcendentals=0),
    )(*args)


def per_device(
    n_ew, n_ns, tokens, vis_index, counts, owners, mask_token, proj_weight, up_first, up_second, saved_pre, cotangent
):
    frames, slots, features = tokens.shape[2:]
    _, chans, rows, cols = saved_pre.shape
    prow, pcol = cotangent.shape[2:]
    patches = rows * cols // 4
    count = n_ew * n_ns
    capacity = 3 * frames * slots // (2 * n_ns)
    rows_each = -(-GRAD_ROWS // count)
    rows_each = -(-rows_each // 16) * 16
    slots_all = frames * slots
    shape = jax.ShapeDtypeStruct

    pixels, cells = column_tables(cols)
    pixels, cells = jnp.asarray(pixels, BF), jnp.asarray(cells, BF)
    edge_pairs = [(0, 0), (1, 1), (2, 2), (3, pcol - 3), (4, pcol - 2), (5, pcol - 1)]
    edge_pairs += [(8, pcol), (9, pcol + cols - 1)]
    edges = jnp.asarray(one_hot((16, pcol + cols), edge_pairs), BF)
    halo_pairs = [(0, 0), (1, 1), (2, 2), (16 + 3, 3), (16 + 4, 4), (16 + 5, 5)]
    halo_pairs += [(8, 128), (16 + 9, 129)]
    halos = jnp.asarray(one_hot((32, 256), halo_pairs), BF)

    msg_rows = frames * 3 * GROUP + chans + 16
    own_g, own_p, own_edges, send_a, send_b = call(
        pack_kernel,
        (
            shape((frames * prow * GROUP, pcol), BF),
            shape((frames * rows * chans, cols), BF),
            shape((16, frames * rows * chans), BF),
            shape((msg_rows, pcol), BF),
            shape((msg_rows, pcol), BF),
        ),
        (cotangent, saved_pre, edges),
        [
            pltpu.VMEM((frames * GROUP * prow * pcol // cols, cols), F32),
            pltpu.VMEM((frames * chans * rows, cols), F32),
        ],
        flops=1 << 22,
    )
    got_a = swap(send_a, "ns", 0)
    got_b = swap(send_b, "ns", 1)

    live = jnp.arange(slots, dtype=jnp.int32)[None, :] < counts[0, 0][:, None]
    ids = jnp.stack(
        [
            vis_index.reshape(slots_all),
            owners.reshape(slots_all),
            live.astype(jnp.int32).reshape(slots_all),
        ]
    )
    ids = jnp.concatenate([ids, jnp.zeros((5, slots_all), jnp.int32)], axis=0)
    tile_tokens = tokens.reshape(slots_all, features)
    mask_row = mask_token.reshape(1, features)
    grid, picks, hidden, route, wab, w2 = call(
        functools.partial(token_kernel, capacity),
        (
            shape((frames * rows // 4, 2 * chans, 2 * cols), BF),
            shape((frames, slots, patches), BF),
            shape((16, frames * patches), BF),
            shape((n_ns * GROUP, 2 * slots_all), BF),
            shape((2 * chans, 8 * chans), BF),
            shape((chans, 16 * GROUP), BF),
        ),
        (ids, tile_tokens, mask_row, proj_weight, up_first, up_second),
        flops=1 << 24,
    )

    side = jnp.concatenate([own_edges, got_a[msg_rows - 16 :], got_b[msg_rows - 16 :]], axis=1)
    side_a = swap(side, "ew", 0)
    side_b = swap(side, "ew", 1)

    outgoing = call(
        functools.partial(tile_kernel, n_ew, rows_each),
        shape((count, rows_each + GROUP, 2 * chans), BF),
        (
            own_g, own_p, got_a, got_b, side_a, side_b, pixels, cells, halos,
            grid, picks, hidden, route, wab, w2, tile_tokens, mask_row,
        ),
        [
            pltpu.VMEM((frames * (prow + 6) * GROUP, pcol + 128), BF),
            pltpu.VMEM((frames * (rows + 2) * chans, 2 * cols), BF),
            pltpu.VMEM((frames * (prow + 6) * GROUP, 8 * cols), BF),
            pltpu.VMEM((frames * (rows + 2) * chans, 2 * cols), F32),
            pltpu.VMEM((frames * (rows + 2) * chans, 2 * cols), BF),
            pltpu.VMEM((n_ns * GROUP, 2 * chans), BF),
        ],
        flops=1 << 28,
        limit=40 << 20,
    )
    arrived = lax.all_to_all(outgoing, ("ew", "ns"), 0, 0, tiled=True)
    shares, token_grad = call(
        functools.partial(owner_kernel, n_ns, capacity, rows_each),
        (
            shape((count, rows_each, 2 * chans), BF),
            shape((n_ns * capacity, features), BF),
        ),
        (arrived, proj_weight),
        flops=1 << 24,
        limit=40 << 20,
    )
    summed = lax.all_to_all(shares, ("ew", "ns"), 0, 0, tiled=True)
    summed = summed[: GRAD_ROWS // rows_each]
    grad_proj, grad_first, grad_second, grad_mask = call(
        finish_kernel,
        (
            shape((features, chans), F32),
            shape((4, 4, chans, chans), F32),
            shape((4, 4, up_second.shape[2], chans), F32),
            shape((1, features), F32),
        ),
        (summed, proj_weight),
        flops=1 << 20,
    )
    return (token_grad[None, None], grad_proj, grad_first, grad_second, grad_mask.reshape(features))


def solution(mesh):
    return jax.shard_map(
        functools.partial(per_device, mesh.shape["ew"], mesh.shape["ns"]),
        mesh=mesh,
        in_specs=(
            P("ns", "ew", None, None, None),
            P("ns", "ew", None, None),
            P("ns", "ew", None),
            P("ns", "ew", None, None, None),
            P(),
            P(),
            P(),
            P(),
            P(None, None, "ns", "ew"),
            P(None, None, "ns", "ew"),
        ),
        out_specs=(P("ns", "ew", None, None), P(), P(), P(), P()),
        check_vma=False,
    )
```

```python
import functools

import jax
import jax.numpy as jnp
import numpy as np
from jax import lax
from jax.experimental import pallas as pl
from jax.experimental.pallas import tpu as pltpu
from jax.sharding import PartitionSpec as P

BF = jnp.bfloat16
F32 = jnp.float32
VMEM = pl.BlockSpec(memory_space=pltpu.VMEM)
GROUP = 16
GRAD_ROWS = 1024
PROJ_AT = 512
SECOND_AT = 896
MASK_ROW = SECOND_AT + 12


def nn(a, b):
    return lax.dot_general(a, b, (((1,), (0,)), ((), ())), preferred_element_type=F32)


def nt(a, b):
    return lax.dot_general(a, b, (((1,), (1,)), ((), ())), preferred_element_type=F32)


def tn(a, b):
    return lax.dot_general(a, b, (((0,), (0,)), ((), ())), preferred_element_type=F32)


def iota(shape, dim):
    return lax.broadcasted_iota(jnp.int32, shape, dim)


def column_tables(cols):
    half = cols // 2
    fine = 2 * cols

    def hidden_cols(arrangement):
        if arrangement == 0:
            return [2 * j for j in range(half)] + [2 * j + 1 for j in range(half)]
        return [2 * j + 2 for j in range(half)] + [2 * j - 1 for j in range(half)]

    def pixel_row(x):
        return x if 0 <= x < fine else (x if x >= fine else fine + 6 + x)

    def hidden_row(x):
        return x if 0 <= x <= cols else cols + 1

    pixels = np.zeros((fine + 128, 4 * 2 * cols), np.float32)
    cells = np.zeros((2 * cols, 2 * cols), np.float32)
    for arrangement in range(2):
        for lane, col in enumerate(hidden_cols(arrangement)):
            cells[hidden_row(col), arrangement * cols + lane] = 1.0
            for tap in range(4):
                pixels[pixel_row(2 * col + tap - 1), (tap * 2 + arrangement) * cols + lane] = 1.0
    return pixels, cells


def spread(ref, wide, group):
    frames, real, rows, cols = ref.shape
    for f in range(frames):
        for o in range(group):
            value = ref[f, o].astype(F32) if o < real else jnp.zeros((rows, cols), F32)
            for h in range(cols // 128):
                wide[pl.ds(((h * frames + f) * group + o) * rows, rows), :] = value[:, h * 128 : (h + 1) * 128]


def gathered(wide, h, frames, group, rows, f, r):
    return wide[pl.ds((h * frames + f) * group * rows + r, group, stride=rows), :].astype(BF)


def edge_tables(pcol, cols):
    row, col = iota((16, pcol), 0), iota((16, pcol), 1)
    pick_g = ((row < 3) & (col == row)) | ((row >= 3) & (row < 6) & (col == row + pcol - 6))
    row, col = iota((16, cols), 0), iota((16, cols), 1)
    pick_p = ((row == 8) & (col == 0)) | ((row == 9) & (col == cols - 1))
    return pick_g.astype(F32).astype(BF), pick_p.astype(F32).astype(BF)


def send_kernel(cot_ref, pre_ref, a_ref, b_ref, cot_wide, pre_wide):
    frames, bands, prow, pcol = cot_ref.shape
    _, chans, rows, cols = pre_ref.shape
    spread(cot_ref, cot_wide, GROUP)
    spread(pre_ref, pre_wide, chans)
    pick_g, pick_p = edge_tables(pcol, cols)
    at = frames * 3 * GROUP

    def message(out_ref, top):
        first = 0 if top else prow - 3
        line = 0 if top else rows - 1
        for f in range(frames):
            for y in range(3):
                for h in range(pcol // 128):
                    out_ref[pl.ds((f * 3 + y) * GROUP, GROUP), h * 128 : (h + 1) * 128] = gathered(
                        cot_wide, h, frames, GROUP, prow, f, first + y
                    )
            out_ref[pl.ds(at, chans), f * cols : (f + 1) * cols] = gathered(
                pre_wide, 0, frames, chans, rows, f, line
            )
        out_ref[pl.ds(at + chans, 16), :] = jnp.zeros((16, pcol), BF)
        out_ref[pl.ds(at + chans, 16), :at] = nt(pick_g, out_ref[pl.ds(0, at), :]).astype(BF)
        for f in range(frames):
            out_ref[pl.ds(at + chans, 16), cols + f * chans : cols + (f + 1) * chans] = nt(
                pick_p, out_ref[pl.ds(at, chans), f * cols : (f + 1) * cols]
            ).astype(BF)

    even = lax.rem(lax.axis_index("ns"), 2) == 0

    @pl.when(even)
    def _():
        message(a_ref, False)
        message(b_ref, True)

    @pl.when(jnp.logical_not(even))
    def _():
        message(a_ref, True)
        message(b_ref, False)


def layout_kernel(cot_ref, pre_ref, g_ref, p_ref, own_ref, cot_wide, pre_wide):
    frames, bands, prow, pcol = cot_ref.shape
    _, chans, rows, cols = pre_ref.shape
    spread(cot_ref, cot_wide, GROUP)
    spread(pre_ref, pre_wide, chans)
    for f in range(frames):
        for y in range(prow):
            for h in range(pcol // 128):
                g_ref[pl.ds((f * prow + y) * GROUP, GROUP), h * 128 : (h + 1) * 128] = gathered(
                    cot_wide, h, frames, GROUP, prow, f, y
                )
        for r in range(rows):
            p_ref[pl.ds((f * rows + r) * chans, chans), :] = gathered(pre_wide, 0, frames, chans, rows, f, r)
    pick_g, pick_p = edge_tables(pcol, cols)
    edges_p = nt(pick_p, p_ref[...])
    edges_g = nt(pick_g, g_ref[...])
    width = edges_g.shape[1]
    own_ref[:, :width] = (edges_g + edges_p[:, :width]).astype(BF)
    own_ref[:, width:] = edges_p[:, width:].astype(BF)


def token_kernel(
    capacity, counts_ref, vis_ref, owners_ref, tokens_ref, mask_ref, proj_ref, first_ref, second_ref,
    grid_ref, pick_ref, hidden_ref, route_ref, wab_ref, w2_ref,
):
    slots_all = tokens_ref.shape[0]
    frames, slots, patches = pick_ref.shape
    chans = proj_ref.shape[0]
    bands = second_ref.shape[1]
    owners = route_ref.shape[0] // GROUP
    half = capacity // 2
    eye = (iota((chans, chans), 0) == iota((chans, chans), 1)).astype(BF)
    pad = jnp.zeros((GROUP - bands, chans), F32)
    taps = []
    for b in range(4):
        for a in range(4):
            here = iota((bands, 4, chans), 1) == b
            tap = jnp.sum(jnp.where(here, second_ref[a].astype(F32), 0.0), axis=1)
            taps.append(jnp.concatenate([tap, pad], axis=0).astype(BF))
    w2_ref[...] = nt(eye, jnp.concatenate(taps, axis=0)).astype(BF)
    left = (iota((2 * chans, chans), 0) == iota((2 * chans, chans), 1)).astype(BF)
    right = (iota((2 * chans, chans), 0) == iota((2 * chans, chans), 1) + chans).astype(BF)
    for arrangement, (lo, hi) in enumerate(((1, 2), (3, 0))):
        taps_lo = jnp.concatenate([first_ref[a, lo] for a in range(4)], axis=0)
        taps_hi = jnp.concatenate([first_ref[a, hi] for a in range(4)], axis=0)
        wab_ref[:, arrangement * 4 * chans : (arrangement + 1) * 4 * chans] = (
            nt(left, taps_lo) + nt(right, taps_hi)
        ).astype(BF)
    vis = jnp.concatenate([vis_ref[f : f + 1, :] for f in range(frames)], axis=1)
    owner = jnp.concatenate([owners_ref[f] for f in range(frames)], axis=1)
    slot = iota((1, slots_all), 1)
    live = jnp.zeros((1, slots_all), jnp.int32)
    for f in range(frames):
        inside = (slot >= f * slots) & (slot < f * slots + counts_ref[0, f])
        live = jnp.where(inside, 1, live)
    wanted = jnp.where(live > 0, vis, patches)
    square = (slots_all, slots_all)
    column = jnp.sum(
        jnp.where(iota(square, 0) == iota(square, 1), wanted.astype(F32), 0.0), axis=1, keepdims=True
    ).astype(jnp.int32)
    token_proj = nt(tokens_ref[...], proj_ref[...]).astype(BF)
    features = mask_ref.shape[0]
    mask_row = mask_ref[...].astype(F32).reshape(1, features)
    mask_proj = nt(jnp.broadcast_to(mask_row, (16, features)).astype(BF), proj_ref[...]).astype(BF)
    row0 = iota((16, patches), 0) == 0
    lane = iota((chans, 2 * chans), 1)
    for f in range(frames):
        hits = iota((slots, patches), 1) == column[f * slots : (f + 1) * slots]
        picks = hits.astype(F32)
        pick_ref[f] = picks.astype(BF)
        unseen = jnp.where(row0, 1.0 - jnp.sum(picks, axis=0, keepdims=True), 0.0).astype(BF)
        hidden_ref[:, f * patches : (f + 1) * patches] = unseen
        grid = tn(token_proj[f * slots : (f + 1) * slots], picks.astype(BF)) + tn(mask_proj, unseen)
        for pair in range(patches // (2 * chans)):
            straight = grid[:, pair * 2 * chans : (pair + 1) * 2 * chans]
            turned = pltpu.roll(straight, chans, 1)
            k = f * (patches // (2 * chans)) + pair
            zero = jnp.zeros_like(straight)
            grid_ref[k, :chans, : 2 * chans] = jnp.where(lane < chans, straight, zero).astype(BF)
            grid_ref[k, chans:, : 2 * chans] = jnp.where(lane < chans, zero, turned).astype(BF)
            grid_ref[k, :chans, 2 * chans :] = jnp.where(lane < chans, turned, zero).astype(BF)
            grid_ref[k, chans:, 2 * chans :] = jnp.where(lane < chans, zero, straight).astype(BF)
    own_rows = -(-owners // 16) * 16
    hit = (iota((own_rows, slots_all), 0) == jnp.where(live > 0, owner, -1)).astype(F32)
    before = (iota(square, 0) < iota(square, 1)).astype(BF)
    earlier = nn(hit.astype(BF), before)
    place = jnp.sum(earlier * hit, axis=0, keepdims=True).astype(jnp.int32)
    for h in range(2):
        inside = (live > 0) & (place >= h * half) & (place < (h + 1) * half)
        target = jnp.where(inside, owner * GROUP + place - h * half, -1)
        route_ref[:, h * slots_all : (h + 1) * slots_all] = (
            iota((owners * GROUP, slots_all), 0) == target
        ).astype(F32).astype(BF)


def tile_kernel(
    n_ew, rows_each, g_ref, p_ref, ra_ref, rb_ref, ea_ref, eb_ref, pix_ref, cell_ref,
    grid_ref, pick_ref, hidden_ref, route_ref, wab_ref, w2_ref, tokens_ref, mask_ref,
    out_ref, ext, wide, wins, pres, deltas, routed,
):
    frames, slots, patches = pick_ref.shape
    chans = w2_ref.shape[0]
    pcol = g_ref.shape[1]
    cols = p_ref.shape[1]
    rows = p_ref.shape[0] // (frames * chans)
    prow = 2 * rows
    n_ns = route_ref.shape[0] // GROUP
    ns = lax.axis_index("ns")
    ew = lax.axis_index("ew")
    even_ns = lax.rem(ns, 2) == 0
    even_ew = lax.rem(ew, 2) == 0
    ra, rb = ra_ref[...], rb_ref[...]
    north = jnp.where(even_ns, rb, ra)
    south = jnp.where(even_ns, ra, rb)
    ea, eb = ea_ref[...], eb_ref[...]
    sides = jnp.concatenate([jnp.where(even_ew, ea, eb), jnp.where(even_ew, eb, ea)], axis=0)
    own_len = frames * rows * chans
    xa = sides[:, own_len : own_len + pcol]
    xb = sides[:, own_len + pcol : own_len + 2 * pcol]
    side_n = jnp.where(even_ns, xb, xa)
    side_s = jnp.where(even_ns, xa, xb)
    row, col = iota((32, 128), 0), iota((32, 128), 1)
    pick_g = ((row < 3) & (col == row)) | ((row >= 19) & (row < 22) & (col == row - 16))
    pick_g = pick_g.astype(F32).astype(BF)
    pick_p = ((row == 8) & (col == 0)) | ((row == 25) & (col == 1))
    pick_p = pick_p.astype(F32).astype(BF)
    g_len = frames * prow * GROUP
    edge = frames * 3 * GROUP
    own_g = tn(sides[:, :g_len], pick_g).astype(BF)
    north_g = tn(side_n[:, :128], pick_g).astype(BF)
    south_g = tn(side_s[:, :128], pick_g).astype(BF)
    own_p = tn(sides[:, :own_len], pick_p).astype(BF)
    north_p = tn(side_n[:, 128:256], pick_p).astype(BF)
    south_p = tn(side_s[:, 128:256], pick_p).astype(BF)
    tall = (prow + 6) * GROUP
    high = (rows + 2) * chans
    for f in range(frames):
        base = f * tall
        top, mid, low = 3 * GROUP, prow * GROUP, 3 * GROUP
        ext[pl.ds(base, top), :pcol] = north[f * top : (f + 1) * top]
        ext[pl.ds(base, top), pcol:] = north_g[f * top : (f + 1) * top]
        ext[pl.ds(base + top, mid), :pcol] = g_ref[pl.ds(f * mid, mid), :]
        ext[pl.ds(base + top, mid), pcol:] = own_g[f * mid : (f + 1) * mid]
        ext[pl.ds(base + top + mid, low), :pcol] = south[f * low : (f + 1) * low]
        ext[pl.ds(base + top + mid, low), pcol:] = south_g[f * low : (f + 1) * low]
        base = f * high
        mid = rows * chans
        wide[pl.ds(base, chans), :cols] = north[edge : edge + chans, f * cols : (f + 1) * cols]
        wide[pl.ds(base, chans), cols:] = north_p[f * chans : (f + 1) * chans]
        wide[pl.ds(base + chans, mid), :cols] = p_ref[pl.ds(f * mid, mid), :]
        wide[pl.ds(base + chans, mid), cols:] = own_p[f * mid : (f + 1) * mid]
        wide[pl.ds(base + chans + mid, chans), :cols] = south[
            edge : edge + chans, f * cols : (f + 1) * cols
        ]
        wide[pl.ds(base + chans + mid, chans), cols:] = south_p[f * chans : (f + 1) * chans]
    for f in range(frames):
        block = ext[pl.ds(f * tall, tall), :]
        for b in range(4):
            lanes = slice(b * 2 * cols, (b + 1) * 2 * cols)
            wins[pl.ds(f * tall, tall), lanes] = nn(block, pix_ref[:, lanes]).astype(BF)
        pres[pl.ds(f * high, high), :] = nn(wide[pl.ds(f * high, high), :], cell_ref[...])
    w2 = w2_ref[...]
    lane = iota((chans, 2 * cols), 1)
    outside_col = ((lane == cols + cols // 2 - 1) & (ew == n_ew - 1)) | (
        (lane == cols + cols // 2) & (ew == 0)
    )
    zero = jnp.zeros((chans, cols), BF)
    grad_second = None
    for f in range(frames):
        for i in range(rows + 2):
            at = f * tall + 2 * i * GROUP
            taps = [wins[pl.ds(at, 4 * GROUP), b * 2 * cols : (b + 1) * 2 * cols] for b in range(4)]
            grad_hidden = nn(w2, jnp.concatenate(taps, axis=0))
            v = pres[pl.ds(f * high + i * chans, chans), :]
            s = 0.5 + 0.5 * jnp.tanh(0.851 * v)
            delta = grad_hidden * (s + 1.702 * v * s * (1.0 - s))
            drop = outside_col
            if i == 0:
                drop = drop | (ns == 0)
            if i == rows + 1:
                drop = drop | (ns == n_ns - 1)
            deltas[pl.ds(f * high + i * chans, chans), :] = jnp.where(drop, 0.0, delta).astype(BF)
            if 1 <= i <= rows:
                hid = (v[:, :cols] * s[:, :cols]).astype(BF)
                lhs = jnp.concatenate(
                    [
                        jnp.concatenate([taps[0][:, :cols], taps[2][:, :cols]], axis=1),
                        jnp.concatenate([taps[1][:, :cols], taps[3][:, :cols]], axis=1),
                    ],
                    axis=0,
                )
                rhs = jnp.concatenate(
                    [
                        jnp.concatenate([hid, zero], axis=1),
                        jnp.concatenate([zero, hid], axis=1),
                    ],
                    axis=0,
                )
                term = nt(lhs, rhs)
                grad_second = term if grad_second is None else grad_second + term
    wab = wab_ref[...]
    half_lane = iota((chans, cols), 1) < cols // 2
    grad_first = None
    grids = []
    for f in range(frames):
        parts = []
        for pair in range(rows // 4):
            cells = []
            for odd in range(2):
                at = f * high + (2 * pair + odd) * 2 * chans
                slab = deltas[pl.ds(at, 4 * chans), :]
                cells.append(jnp.concatenate([slab[:, :cols], slab[:, cols:]], axis=0))
            both = jnp.concatenate(cells, axis=1)
            term = nt(both, grid_ref[f * (rows // 4) + pair])
            grad_first = term if grad_first is None else grad_first + term
            turn = nn(wab, both)
            here = jnp.where(half_lane, turn[:chans, :cols], turn[chans:, cols:])
            there = jnp.where(half_lane, turn[:chans, cols:], turn[chans:, :cols])
            parts.append(here + pltpu.roll(there, cols // 2, 1))
        grids.append(jnp.concatenate(parts, axis=1).astype(BF))
    none = jnp.zeros((chans, patches), BF)
    mask_sum = nt(hidden_ref[...], jnp.concatenate(grids, axis=1))
    lower = [nt(pick_ref[f], jnp.concatenate([grids[f], none], axis=0)) for f in range(frames)]
    upper = [nt(pick_ref[f], jnp.concatenate([none, grids[f]], axis=0)) for f in range(frames)]
    chosen = jnp.concatenate(lower + upper, axis=0).astype(BF)
    routed[...] = nn(route_ref[...], chosen).astype(BF)
    features = tokens_ref.shape[1]
    hi = mask_sum.astype(BF).astype(F32)
    lo = mask_sum - hi
    line = iota(hi.shape, 0)
    mask_rows = jnp.where(line == 0, hi[0:1], jnp.where(line == 1, lo[0:1], 0.0)).astype(BF)
    line = iota((16, features), 0)
    mask_row = mask_ref[...].astype(F32).reshape(1, features)
    spread_row = jnp.where(line < 2, mask_row, 0.0).astype(BF)
    slots_all = tokens_ref.shape[0]
    grad_proj = tn(chosen[:slots_all, :chans], tokens_ref[...]) + tn(mask_rows, spread_row)
    grad_proj = [grad_proj[:, k * 128 : (k + 1) * 128] for k in range(features // 128)]
    both = jnp.concatenate([hi[0:1], lo[0:1]], axis=1)
    mark = iota(grad_second.shape, 0) == MASK_ROW - SECOND_AT
    grad_second = jnp.where(mark, both, grad_second)
    total = jnp.concatenate([grad_first, *grad_proj, grad_second], axis=0).astype(BF)
    count = out_ref.shape[0]
    for d in range(GRAD_ROWS // rows_each):
        out_ref[d, :rows_each, :] = total[d * rows_each : (d + 1) * rows_each]
    if count * rows_each > GRAD_ROWS:

        @pl.loop(GRAD_ROWS // rows_each, count)
        def _(d):
            out_ref[d, :rows_each, :] = jnp.zeros((rows_each, 2 * chans), BF)

    def place(d):
        source = pl.multiple_of(lax.rem(d, n_ns) * GROUP, GROUP)
        out_ref[d, rows_each:, :] = routed[pl.ds(source, GROUP), :]

    if count <= 64:
        for d in range(count):
            out_ref[d, rows_each:, :] = routed[pl.ds((d % n_ns) * GROUP, GROUP), :]
    else:
        pl.loop(0, count)(place)


def owner_kernel(n_ns, capacity, rows_each, got_ref, proj_ref, sum_ref, token_ref):
    count = got_ref.shape[0]
    chans = proj_ref.shape[0]
    if count <= 64:
        total = got_ref[0, :rows_each, :].astype(F32)
        for d in range(1, count):
            total = total + got_ref[d, :rows_each, :].astype(F32)
    else:
        total = lax.fori_loop(
            0,
            count,
            lambda d, acc: acc + got_ref[d, :rows_each, :].astype(F32),
            jnp.zeros((rows_each, 2 * chans), F32),
        )
    share = total.astype(BF)
    if count <= 64:
        for d in range(count):
            sum_ref[d] = share
    else:

        @pl.loop(0, count)
        def _(d):
            sum_ref[d] = share

    half = capacity // 2
    ew = lax.axis_index("ew")
    arrived = jnp.concatenate(
        [got_ref[ew * n_ns + s, rows_each:, :] for s in range(n_ns)], axis=0
    )
    shape = (n_ns * capacity, n_ns * GROUP)
    row, col = iota(shape, 0), iota(shape, 1)
    slot = lax.rem(row, capacity)
    source = (row // capacity) * GROUP + lax.rem(slot, half)
    picked = nn((source == col).astype(F32).astype(BF), arrived)
    second = lax.rem(iota(picked.shape, 0), capacity) >= half
    picked = jnp.where(second, pltpu.roll(picked, chans, 1), picked)[:, :chans].astype(BF)
    token_ref[...] = nn(picked, proj_ref[...]).astype(BF)


def finish_kernel(got_ref, proj_ref, proj_out, first_out, second_out, mask_out):
    chans, features = proj_ref.shape
    bands = second_out.shape[1]
    rows_each = got_ref.shape[1]
    parts = [got_ref[d] for d in range(GRAD_ROWS // rows_each)]
    total = jnp.concatenate(parts, axis=0).astype(F32)
    for arrangement, taps in enumerate(((1, 2), (3, 0))):
        rows = total[arrangement * 4 * chans : (arrangement + 1) * 4 * chans]
        turned = pltpu.roll(rows, chans, 1)
        for a in range(4):
            first_out[a, taps[0]] = rows[a * chans : (a + 1) * chans, :chans]
            first_out[a, taps[1]] = turned[a * chans : (a + 1) * chans, :chans]
    for k in range(features // 128):
        at = PROJ_AT + k * chans
        proj_out[:, k * 128 : (k + 1) * 128] = total[at : at + chans]
    rows = total[SECOND_AT:]
    turned = pltpu.roll(rows, chans, 1)
    for b in range(2):
        for a in range(4):
            at = (b * 4 + a) * GROUP
            second_out[a, :, b, :] = rows[at : at + bands, :chans]
            second_out[a, :, b + 2, :] = turned[at : at + bands, :chans]
    at = MASK_ROW - SECOND_AT
    mask_sum = rows[at : at + 1, :chans] + turned[at : at + 1, :chans]
    hi = mask_sum.astype(BF).astype(F32)
    mid = (mask_sum - hi).astype(BF).astype(F32)
    lo = mask_sum - hi - mid
    line = iota((16, chans), 0)
    split = jnp.where(line == 0, hi, jnp.where(line == 1, mid, jnp.where(line == 2, lo, 0.0)))
    grad_mask = jnp.sum(nn(split.astype(BF), proj_ref[...]), axis=0, keepdims=True)
    mask_out[...] = grad_mask.reshape(features)


def swap(block, axis, offset):
    count = lax.axis_size(axis)
    pairs = [(i, ((i + offset) ^ 1) - offset) for i in range(count)]
    return lax.ppermute(block, axis, [(i, j) for i, j in pairs if 0 <= j < count])


def call(kernel, outs, args, scratch=(), flops=0, limit=8 << 20, scalars=0):
    return pl.pallas_call(
        kernel,
        out_shape=outs,
        in_specs=[pl.BlockSpec(memory_space=pltpu.SMEM)] * scalars + [VMEM] * (len(args) - scalars),
        out_specs=jax.tree.map(lambda _: VMEM, outs),
        scratch_shapes=list(scratch),
        compiler_params=pltpu.CompilerParams(vmem_limit_bytes=limit),
        cost_estimate=pl.CostEstimate(flops=flops, bytes_accessed=1 << 20, transcendentals=0),
    )(*args)


def per_device(
    n_ew, n_ns, tokens, vis_index, counts, owners, mask_token, proj_weight, up_first, up_second, saved_pre, cotangent
):
    frames, slots, features = tokens.shape[2:]
    _, chans, rows, cols = saved_pre.shape
    bands, prow, pcol = cotangent.shape[1:]
    patches = rows * cols // 4
    count = n_ew * n_ns
    capacity = 3 * frames * slots // (2 * n_ns)
    rows_each = -(-GRAD_ROWS // count)
    rows_each = -(-rows_each // 16) * 16
    slots_all = frames * slots
    shape = jax.ShapeDtypeStruct

    pixels, cells = column_tables(cols)
    pixels, cells = jnp.asarray(pixels, BF), jnp.asarray(cells, BF)
    msg_rows = frames * 3 * GROUP + chans + 16
    wide = [
        pltpu.VMEM((frames * GROUP * prow * pcol // 128, 128), F32),
        pltpu.VMEM((frames * chans * rows, cols), F32),
    ]
    send_a, send_b = call(
        send_kernel,
        (shape((msg_rows, pcol), BF), shape((msg_rows, pcol), BF)),
        (cotangent, saved_pre),
        wide,
        flops=1 << 22,
    )
    got_a = swap(send_a, "ns", 0)
    got_b = swap(send_b, "ns", 1)
    own_g, own_p, own_edges = call(
        layout_kernel,
        (
            shape((frames * prow * GROUP, pcol), BF),
            shape((frames * rows * chans, cols), BF),
            shape((16, frames * rows * chans), BF),
        ),
        (cotangent, saved_pre),
        wide,
        flops=1 << 22,
    )
    side = jnp.concatenate([own_edges, got_a[msg_rows - 16 :], got_b[msg_rows - 16 :]], axis=1)
    side_a = swap(side, "ew", 0)
    side_b = swap(side, "ew", 1)

    tile_tokens = tokens.reshape(slots_all, features)
    proj = proj_weight.T
    grid, picks, hidden, route, wab, w2 = call(
        functools.partial(token_kernel, capacity),
        (
            shape((frames * rows // 4, 2 * chans, 2 * cols), BF),
            shape((frames, slots, patches), BF),
            shape((16, frames * patches), BF),
            shape((n_ns * GROUP, 2 * slots_all), BF),
            shape((2 * chans, 8 * chans), BF),
            shape((chans, 16 * GROUP), BF),
        ),
        (
            counts.reshape(1, frames),
            vis_index.reshape(frames, slots),
            owners.reshape(frames, 1, slots),
            tile_tokens,
            mask_token,
            proj,
            up_first,
            up_second.transpose(0, 2, 1, 3),
        ),
        flops=1 << 24,
        scalars=1,
    )
    outgoing = call(
        functools.partial(tile_kernel, n_ew, rows_each),
        shape((count, rows_each + GROUP, 2 * chans), BF),
        (
            own_g, own_p, got_a, got_b, side_a, side_b, pixels, cells,
            grid, picks, hidden, route, wab, w2, tile_tokens, mask_token,
        ),
        [
            pltpu.VMEM((frames * (prow + 6) * GROUP, pcol + 128), BF),
            pltpu.VMEM((frames * (rows + 2) * chans, 2 * cols), BF),
            pltpu.VMEM((frames * (prow + 6) * GROUP, 8 * cols), BF),
            pltpu.VMEM((frames * (rows + 2) * chans, 2 * cols), F32),
            pltpu.VMEM((frames * (rows + 2) * chans, 2 * cols), BF),
            pltpu.VMEM((n_ns * GROUP, 2 * chans), BF),
        ],
        flops=1 << 28,
        limit=24 << 20,
    )
    arrived = lax.all_to_all(outgoing, ("ew", "ns"), 0, 0, tiled=True)
    shares, token_grad = call(
        functools.partial(owner_kernel, n_ns, capacity, rows_each),
        (
            shape((count, rows_each, 2 * chans), BF),
            shape((n_ns * capacity, features), BF),
        ),
        (arrived, proj),
        flops=1 << 24,
    )
    summed = lax.all_to_all(shares, ("ew", "ns"), 0, 0, tiled=True)
    summed = summed[: GRAD_ROWS // rows_each]
    grad_proj, grad_first, grad_second, grad_mask = call(
        finish_kernel,
        (
            shape((chans, features), F32),
            shape((4, 4, chans, chans), F32),
            shape((4, bands, 4, chans), F32),
            shape((features,), F32),
        ),
        (summed, proj),
        flops=1 << 20,
    )
    return (token_grad[None, None], grad_proj.T, grad_first, grad_second.transpose(0, 2, 1, 3), grad_mask)


def solution(mesh):
    return jax.shard_map(
        functools.partial(per_device, mesh.shape["ew"], mesh.shape["ns"]),
        mesh=mesh,
        in_specs=(
            P("ns", "ew", None, None, None),
            P("ns", "ew", None, None),
            P("ns", "ew", None),
            P("ns", "ew", None, None, None),
            P(),
            P(),
            P(),
            P(),
            P(None, None, "ns", "ew"),
            P(None, None, "ns", "ew"),
        ),
        out_specs=(P("ns", "ew", None, None), P(), P(), P(), P()),
        check_vma=False,
    )
```

```python
import functools

import jax
import jax.numpy as jnp
import numpy as np
from jax import lax
from jax.experimental import pallas as pl
from jax.experimental.pallas import tpu as pltpu
from jax.sharding import PartitionSpec as P

BF = jnp.bfloat16
F32 = jnp.float32
VMEM = pl.BlockSpec(memory_space=pltpu.VMEM)
SMEM = pl.BlockSpec(memory_space=pltpu.SMEM)
GROUP = 16
GRAD_ROWS = 1024
PROJ_AT = 512
SECOND_AT = 896
MASK_ROW = SECOND_AT + 12


def nn(a, b):
    return lax.dot_general(a, b, (((1,), (0,)), ((), ())), preferred_element_type=F32)


def nt(a, b):
    return lax.dot_general(a, b, (((1,), (1,)), ((), ())), preferred_element_type=F32)


def tn(a, b):
    return lax.dot_general(a, b, (((0,), (0,)), ((), ())), preferred_element_type=F32)


def iota(shape, dim):
    return lax.broadcasted_iota(jnp.int32, shape, dim)


def hidden_columns(cols, lanes):
    lane = lax.rem(lanes, cols)
    right = lane >= cols // 2
    own = 2 * jnp.where(right, lane - cols // 2, lane) + jnp.where(right, 1, 0)
    shifted = own + jnp.where(right, -2, 2)
    return jnp.where(lax.rem(lanes // cols, 2) == 0, own, shifted)


def column_tables(cols, pix_ref, cell_ref):
    fine = 2 * cols
    lanes = iota((1, fine), 1)
    hidden = hidden_columns(cols, lanes)
    for tap in range(4):
        pixel = 2 * hidden + tap - 1
        pixel = jnp.where(pixel < 0, fine + 6 + pixel, pixel)
        table = iota((fine + 128, fine), 0) == pixel
        pix_ref[:, tap * fine : (tap + 1) * fine] = table.astype(F32).astype(BF)
    cell = jnp.where(hidden < 0, cols + 1, hidden)
    cell_ref[...] = (iota((fine, fine), 0) == cell).astype(F32).astype(BF)


def spread(ref, wide, group):
    frames, real, rows, cols = ref.shape
    for f in range(frames):
        for o in range(group):
            value = ref[f, o].astype(F32) if o < real else jnp.zeros((rows, cols), F32)
            for h in range(cols // 128):
                wide[pl.ds(((h * frames + f) * group + o) * rows, rows), :] = value[:, h * 128 : (h + 1) * 128]


def gathered(wide, h, frames, group, rows, f, r):
    return wide[pl.ds((h * frames + f) * group * rows + r, group, stride=rows), :].astype(BF)


def edge_tables(pcol, cols):
    row, col = iota((16, pcol), 0), iota((16, pcol), 1)
    pick_g = ((row < 3) & (col == row)) | ((row >= 3) & (row < 6) & (col == row + pcol - 6))
    row, col = iota((16, cols), 0), iota((16, cols), 1)
    pick_p = ((row == 6) & (col == 0)) | ((row == 7) & (col == cols - 1))
    return pick_g.astype(F32).astype(BF), pick_p.astype(F32).astype(BF)


def cell_layout_kernel(pre_ref, p_ref, edge_ref, pre_wide):
    frames, chans, rows, cols = pre_ref.shape
    spread(pre_ref, pre_wide, chans)
    for r in range(rows):
        for f in range(frames):
            p_ref[pl.ds((r * frames + f) * chans, chans), :] = gathered(pre_wide, 0, frames, chans, rows, f, r)
    edges = nt(edge_tables(2 * cols, cols)[1], p_ref[...])[:8]
    line = frames * chans
    last = (rows - 1) * line
    edge_ref[...] = jnp.concatenate([edges[:, :line], edges[:, last:], edges[:, line:last]], axis=1)


def pixel_layout_kernel(cot_ref, edge_ref, g_ref, own_ref, cot_wide):
    frames, bands, prow, pcol = cot_ref.shape
    spread(cot_ref, cot_wide, GROUP)
    for f in range(frames):
        for y in range(prow):
            for h in range(pcol // 128):
                g_ref[pl.ds((f * prow + y) * GROUP, GROUP), h * 128 : (h + 1) * 128] = gathered(
                    cot_wide, h, frames, GROUP, prow, f, y
                )
    edges = nt(edge_tables(pcol, pcol // 2)[0], g_ref[...])[:8]
    width = edges.shape[1]
    below = edge_ref[...]
    own_ref[...] = jnp.concatenate([edges + below[:, :width], below[:, width:]], axis=1).astype(BF)


def row_messages(g_ref, p_ref, ga_ref, pa_ref, gb_ref, pb_ref):
    deep, pcol = ga_ref.shape[0], g_ref.shape[1]
    chans, cols = pa_ref.shape[0], p_ref.shape[1]
    frames = pa_ref.shape[1] // cols
    tall = g_ref.shape[0] // frames
    high = p_ref.shape[0]

    def message(g_out, p_out, top):
        for f in range(frames):
            at = f * tall if top else (f + 1) * tall - deep
            g_out[:, f * pcol : (f + 1) * pcol] = g_ref[pl.ds(at, deep), :]
            at = f * chans if top else high - (frames - f) * chans
            p_out[:, f * cols : (f + 1) * cols] = p_ref[pl.ds(at, chans), :]

    even = lax.rem(lax.axis_index("ns"), 2) == 0

    @pl.when(even)
    def _():
        message(ga_ref, pa_ref, False)
        message(gb_ref, pb_ref, True)

    @pl.when(jnp.logical_not(even))
    def _():
        message(ga_ref, pa_ref, True)
        message(gb_ref, pb_ref, False)


def local_kernel(
    capacity, counts_ref, g_ref, p_ref, vis_ref, owners_ref, tokens_ref, mask_ref, proj_ref, first_ref, second_ref,
    ga_ref, pa_ref, gb_ref, pb_ref, grid_ref, pick_ref, hidden_ref, route_ref, wab_ref, w2_ref, pix_ref, cell_ref,
):
    row_messages(g_ref, p_ref, ga_ref, pa_ref, gb_ref, pb_ref)
    column_tables(p_ref.shape[1], pix_ref, cell_ref)
    slots_all = tokens_ref.shape[0]
    frames, slots, patches = pick_ref.shape
    chans = proj_ref.shape[0]
    bands = second_ref.shape[1]
    owners = route_ref.shape[0] // GROUP
    half = capacity // 2
    eye = (iota((chans, chans), 0) == iota((chans, chans), 1)).astype(BF)
    pad = jnp.zeros((GROUP - bands, chans), F32)
    taps = []
    for b in range(4):
        for a in range(4):
            here = iota((bands, 4, chans), 1) == b
            tap = jnp.sum(jnp.where(here, second_ref[a].astype(F32), 0.0), axis=1)
            taps.append(jnp.concatenate([tap, pad], axis=0).astype(BF))
    w2_ref[...] = nt(eye, jnp.concatenate(taps, axis=0)).astype(BF)
    left = (iota((2 * chans, chans), 0) == iota((2 * chans, chans), 1)).astype(BF)
    right = (iota((2 * chans, chans), 0) == iota((2 * chans, chans), 1) + chans).astype(BF)
    for arrangement, (lo, hi) in enumerate(((1, 2), (3, 0))):
        taps_lo = jnp.concatenate([first_ref[a, lo] for a in range(4)], axis=0)
        taps_hi = jnp.concatenate([first_ref[a, hi] for a in range(4)], axis=0)
        wab_ref[:, arrangement * 4 * chans : (arrangement + 1) * 4 * chans] = (
            nt(left, taps_lo) + nt(right, taps_hi)
        ).astype(BF)
    vis = jnp.concatenate([vis_ref[f : f + 1, :] for f in range(frames)], axis=1)
    owner = jnp.concatenate([owners_ref[f] for f in range(frames)], axis=1)
    slot = iota((1, slots_all), 1)
    live = jnp.zeros((1, slots_all), jnp.int32)
    for f in range(frames):
        inside = (slot >= f * slots) & (slot < f * slots + counts_ref[0, f])
        live = jnp.where(inside, 1, live)
    wanted = jnp.where(live > 0, vis, patches)
    square = (slots_all, slots_all)
    column = jnp.sum(
        jnp.where(iota(square, 0) == iota(square, 1), wanted.astype(F32), 0.0), axis=1, keepdims=True
    ).astype(jnp.int32)
    token_proj = nt(tokens_ref[...], proj_ref[...]).astype(BF)
    features = mask_ref.shape[0]
    mask_row = mask_ref[...].astype(F32).reshape(1, features)
    mask_proj = nt(jnp.broadcast_to(mask_row, (16, features)).astype(BF), proj_ref[...]).astype(BF)
    row0 = iota((16, patches), 0) == 0
    lane = iota((chans, 2 * chans), 1)
    for f in range(frames):
        hits = iota((slots, patches), 1) == column[f * slots : (f + 1) * slots]
        picks = hits.astype(F32)
        pick_ref[f] = picks.astype(BF)
        unseen = jnp.where(row0, 1.0 - jnp.sum(picks, axis=0, keepdims=True), 0.0).astype(BF)
        hidden_ref[:, f * patches : (f + 1) * patches] = unseen
        grid = tn(token_proj[f * slots : (f + 1) * slots], picks.astype(BF)) + tn(mask_proj, unseen)
        zero = jnp.zeros((chans, 2 * chans), F32)
        for line, (group, half_at) in enumerate(((1, 0), (0, 0), (0, 1), (1, 1))):
            pair = line // 2 * 2 * chans
            straight = grid[:, pair : pair + 2 * chans]
            turned = pltpu.roll(straight, chans, 1)
            to_left, to_right = (straight, turned) if line % 2 == 0 else (turned, straight)
            at = half_at * 2 * chans
            grid_ref[f, group, :chans, at : at + 2 * chans] = jnp.where(lane < chans, to_left, zero).astype(BF)
            grid_ref[f, group, chans:, at : at + 2 * chans] = jnp.where(lane < chans, zero, to_right).astype(BF)
    own_rows = -(-owners // 16) * 16
    hit = (iota((own_rows, slots_all), 0) == jnp.where(live > 0, owner, -1)).astype(F32)
    before = (iota(square, 0) < iota(square, 1)).astype(BF)
    earlier = nn(hit.astype(BF), before)
    place = jnp.sum(earlier * hit, axis=0, keepdims=True).astype(jnp.int32)
    for h in range(2):
        inside = (live > 0) & (place >= h * half) & (place < (h + 1) * half)
        target = jnp.where(inside, owner * GROUP + place - h * half, -1)
        route_ref[:, h * slots_all : (h + 1) * slots_all] = (
            iota((owners * GROUP, slots_all), 0) == target
        ).astype(F32).astype(BF)


def side_columns(ea_ref, eb_ref, even_ew):
    ea, eb = ea_ref[...].astype(F32), eb_ref[...].astype(F32)
    return jnp.concatenate([jnp.where(even_ew, ea, eb), jnp.where(even_ew, eb, ea)], axis=0).astype(BF)


def halo_tables():
    row, col = iota((16, 128), 0), iota((16, 128), 1)
    pick_g = ((row < 3) & (col == row)) | ((row >= 11) & (row < 14) & (col == row - 8))
    pick_p = ((row == 6) & (col == 0)) | ((row == 15) & (col == 1))
    return pick_g.astype(F32).astype(BF), pick_p.astype(F32).astype(BF)


def second_backward(taps, pre, w2, drop):
    grad_hidden = nn(w2, jnp.concatenate(taps, axis=0))
    s = 0.5 + 0.5 * jnp.tanh(0.851 * pre)
    delta = grad_hidden * (s + 1.702 * pre * s * (1.0 - s))
    cols = pre.shape[1] // 2
    return jnp.where(drop, 0.0, delta).astype(BF), (pre[:, :cols] * s[:, :cols]).astype(BF)


def second_kernel_term(taps, hid):
    cols = hid.shape[1]
    zero = jnp.zeros_like(hid)
    lhs = jnp.concatenate(
        [
            jnp.concatenate([taps[0][:, :cols], taps[2][:, :cols]], axis=1),
            jnp.concatenate([taps[1][:, :cols], taps[3][:, :cols]], axis=1),
        ],
        axis=0,
    )
    rhs = jnp.concatenate(
        [jnp.concatenate([hid, zero], axis=1), jnp.concatenate([zero, hid], axis=1)], axis=0
    )
    return nt(lhs, rhs)


def outside_columns(chans, cols, n_ew, ew):
    lane = iota((chans, 2 * cols), 1)
    return ((lane == cols + cols // 2 - 1) & (ew == n_ew - 1)) | ((lane == cols + cols // 2) & (ew == 0))


def window_taps(wins, at, cols):
    return [wins[pl.ds(at, 4 * GROUP), b * 2 * cols : (b + 1) * 2 * cols] for b in range(4)]


def message_kernel(ga_ref, pa_ref, gb_ref, pb_ref, sa_ref, sb_ref, a_ref, b_ref):
    deep, span = ga_ref.shape
    corners = jnp.concatenate([sa_ref[:, :span].astype(F32), sb_ref[:, :span].astype(F32)], axis=0).astype(BF)
    for out, g, p in ((a_ref, ga_ref, pa_ref), (b_ref, gb_ref, pb_ref)):
        out[:deep, :span] = g[...]
        out[deep:, :span] = corners
        out[:, span:] = p[...]


def inner_kernel(
    n_ew, g_ref, p_ref, ea_ref, eb_ref, pix_ref, cell_ref, grid_ref, wab_ref, w2_ref,
    delta_ref, second_ref, first_ref, turn_ref, edge_ref, pre_ref, ext, wide, wins, pres,
):
    frames = grid_ref.shape[0]
    chans = w2_ref.shape[0]
    pcol, cols = g_ref.shape[1], p_ref.shape[1]
    tall = g_ref.shape[0] // frames
    rows = p_ref.shape[0] // (frames * chans)
    ew = lax.axis_index("ew")
    sides = side_columns(ea_ref, eb_ref, lax.rem(ew, 2) == 0)
    pick_g, pick_p = halo_tables()
    line = frames * chans
    ext[:, :pcol] = g_ref[...]
    ext[:, pcol:] = tn(sides[:, : frames * tall], pick_g).astype(BF)
    wide[:, :cols] = p_ref[...]
    halo = tn(sides, pick_p).astype(BF)
    wide[pl.ds(0, line), cols:] = halo[:line]
    wide[pl.ds((rows - 1) * line, line), cols:] = halo[line : 2 * line]
    wide[pl.ds(line, (rows - 2) * line), cols:] = halo[2 * line :]
    deep = 3 * GROUP
    for f in range(frames):
        block = ext[pl.ds(f * tall, tall), :]
        for b in range(4):
            lanes = slice(b * 2 * cols, (b + 1) * 2 * cols)
            wins[pl.ds(f * tall, tall), lanes] = nn(block, pix_ref[:, lanes]).astype(BF)
        edge_ref[f, 0] = wins[pl.ds(f * tall, deep), :]
        edge_ref[f, 1] = wins[pl.ds((f + 1) * tall - deep, deep), :]
    pres[...] = nn(wide[...], cell_ref[...])
    for f in range(frames):
        pre_ref[f, 0] = pres[pl.ds(f * chans, chans), :]
        pre_ref[f, 1] = pres[pl.ds((rows - 1) * line + f * chans, chans), :]
    w2 = w2_ref[...]
    wab = wab_ref[...]
    drop = outside_columns(chans, cols, n_ew, ew)
    grad_second = grad_first = None
    for f in range(frames):
        deltas = []
        for i in range(1, rows - 1):
            taps = window_taps(wins, f * tall + (2 * i - 1) * GROUP, cols)
            pre = pres[pl.ds(i * line + f * chans, chans), :]
            delta, hid = second_backward(taps, pre, w2, drop)
            deltas.append(delta)
            term = second_kernel_term(taps, hid)
            grad_second = term if grad_second is None else grad_second + term
        count = rows - 2
        for k, i in enumerate((0, 1, count - 2, count - 1)):
            delta_ref[pl.ds((f * 4 + k) * chans, chans), :] = deltas[i]
        cells = []
        for i in (0, 2):
            slab = jnp.concatenate(deltas[i : i + 4], axis=0)
            cells.append(jnp.concatenate([slab[:, :cols], slab[:, cols:]], axis=0))
        both = jnp.concatenate(cells, axis=1)
        term = nt(both, grid_ref[f, 0])
        grad_first = term if grad_first is None else grad_first + term
        turn_ref[f] = nn(wab, both)
    second_ref[...] = grad_second
    first_ref[...] = grad_first


def outer_kernel(
    n_ew, rows_each, ra_ref, rb_ref, pix_ref, cell_ref,
    delta_ref, second_ref, first_ref, turn_ref, edge_ref, pre_ref,
    grid_ref, pick_ref, hidden_ref, route_ref, wab_ref, w2_ref, tokens_ref, mask_ref,
    out_ref, ext, wide, wins, pres, routed,
):
    frames, slots, patches = pick_ref.shape
    chans = w2_ref.shape[0]
    features = tokens_ref.shape[1]
    cols = pre_ref.shape[3] // 2
    pcol = 2 * cols
    deep = 3 * GROUP
    n_ns = route_ref.shape[0] // GROUP
    ns = lax.axis_index("ns")
    ew = lax.axis_index("ew")
    even_ns = lax.rem(ns, 2) == 0
    even_ew = lax.rem(ew, 2) == 0
    ra, rb = ra_ref[...], rb_ref[...]
    north = jnp.where(even_ns, rb, ra)
    south = jnp.where(even_ns, ra, rb)
    span = frames * pcol
    tall = span // frames

    def far_sides(message):
        a, b = message[deep : deep + 8, :span].astype(F32), message[deep + 8 :, :span].astype(F32)
        return jnp.concatenate([jnp.where(even_ew, a, b), jnp.where(even_ew, b, a)], axis=0).astype(BF)

    pick_g, pick_p = halo_tables()
    line = frames * chans
    far = (far_sides(north), far_sides(south))
    for low in range(2):
        message = south if low else north
        halo_p = tn(far[low][:, (1 - low) * line : (2 - low) * line], pick_p).astype(BF)
        for f in range(frames):
            at = (f * 2 + low) * deep
            ext[pl.ds(at, deep), :pcol] = message[:deep, f * pcol : (f + 1) * pcol]
            if low:
                ext[pl.ds(at, deep), pcol:] = tn(far[low][:, f * tall : f * tall + 128], pick_g).astype(BF)[:deep]
            else:
                end = (f + 1) * tall
                ext[pl.ds(at, deep), pcol:] = tn(far[low][:, end - 128 : end], pick_g).astype(BF)[128 - deep :]
            at = (f * 2 + low) * chans
            wide[pl.ds(at, chans), :cols] = message[:, span + f * cols : span + (f + 1) * cols]
            wide[pl.ds(at, chans), cols:] = halo_p[f * chans : (f + 1) * chans]
    block = ext[...]
    for b in range(4):
        lanes = slice(b * 2 * cols, (b + 1) * 2 * cols)
        wins[:, lanes] = nn(block, pix_ref[:, lanes]).astype(BF)
    pres[...] = nn(wide[...], cell_ref[...])
    w2 = w2_ref[...]
    wab = wab_ref[...]
    drop = outside_columns(chans, cols, n_ew, ew)
    grad_second = second_ref[...]
    grad_first = first_ref[...]
    half_lane = iota((chans, cols), 1) < cols // 2
    grids = []
    for f in range(frames):
        cells = []
        for low in range(2):
            pair = []
            for k in range(2):
                inside = k == 1 - low
                beyond = wins[pl.ds((f * 2 + low) * deep, deep), :]
                window = [edge_ref[f, low], beyond] if low else [beyond, edge_ref[f, low]]
                window = jnp.concatenate(window, axis=0)[k * 2 * GROUP : (k * 2 + 4) * GROUP]
                taps = [window[:, b * 2 * cols : (b + 1) * 2 * cols] for b in range(4)]
                pre = pre_ref[f, low] if inside else pres[pl.ds((f * 2 + low) * chans, chans), :]
                gone = drop if inside else drop | (ns == (n_ns - 1 if low else 0))
                delta, hid = second_backward(taps, pre, w2, gone)
                pair.append(delta)
                if inside:
                    grad_second = grad_second + second_kernel_term(taps, hid)
            kept = delta_ref[pl.ds((f * 4 + 2 * low) * chans, 2 * chans), :]
            slab = jnp.concatenate([kept, *pair] if low else [*pair, kept], axis=0)
            cells.append(jnp.concatenate([slab[:, :cols], slab[:, cols:]], axis=0))
        both = jnp.concatenate(cells, axis=1)
        grad_first = grad_first + nt(both, grid_ref[f, 1])
        edge = nn(wab, both)
        inner = turn_ref[f]
        parts = []
        for even, odd in ((edge[:, :cols], inner[:, :cols]), (inner[:, cols:], edge[:, cols:])):
            here = jnp.where(half_lane, even[:chans], odd[chans:])
            there = jnp.where(half_lane, odd[:chans], even[chans:])
            parts.append(here + pltpu.roll(there, cols // 2, 1))
        grids.append(jnp.concatenate(parts, axis=1).astype(BF))
    none = jnp.zeros((chans, patches), BF)
    mask_sum = nt(hidden_ref[...], jnp.concatenate(grids, axis=1))
    lower = [nt(pick_ref[f], jnp.concatenate([grids[f], none], axis=0)) for f in range(frames)]
    upper = [nt(pick_ref[f], jnp.concatenate([none, grids[f]], axis=0)) for f in range(frames)]
    chosen = jnp.concatenate(lower + upper, axis=0).astype(BF)
    routed[...] = nn(route_ref[...], chosen).astype(BF)
    features = tokens_ref.shape[1]
    hi = mask_sum.astype(BF).astype(F32)
    lo = mask_sum - hi
    line = iota(hi.shape, 0)
    mask_rows = jnp.where(line == 0, hi[0:1], jnp.where(line == 1, lo[0:1], 0.0)).astype(BF)
    line = iota((16, features), 0)
    mask_row = mask_ref[...].astype(F32).reshape(1, features)
    spread_row = jnp.where(line < 2, mask_row, 0.0).astype(BF)
    slots_all = tokens_ref.shape[0]
    grad_proj = tn(chosen[:slots_all, :chans], tokens_ref[...]) + tn(mask_rows, spread_row)
    grad_proj = [grad_proj[:, k * 128 : (k + 1) * 128] for k in range(features // 128)]
    both = jnp.concatenate([hi[0:1], lo[0:1]], axis=1)
    mark = iota(grad_second.shape, 0) == MASK_ROW - SECOND_AT
    grad_second = jnp.where(mark, both, grad_second)
    total = jnp.concatenate([grad_first, *grad_proj, grad_second], axis=0).astype(BF)
    count = out_ref.shape[0]
    for d in range(GRAD_ROWS // rows_each):
        out_ref[d, :rows_each, :] = total[d * rows_each : (d + 1) * rows_each]
    if count * rows_each > GRAD_ROWS:

        @pl.loop(GRAD_ROWS // rows_each, count)
        def _(d):
            out_ref[d, :rows_each, :] = jnp.zeros((rows_each, 2 * chans), BF)

    def place(d):
        source = pl.multiple_of(lax.rem(d, n_ns) * GROUP, GROUP)
        out_ref[d, rows_each:, :] = routed[pl.ds(source, GROUP), :]

    if count <= 64:
        for d in range(count):
            out_ref[d, rows_each:, :] = routed[pl.ds((d % n_ns) * GROUP, GROUP), :]
    else:
        pl.loop(0, count)(place)


def sum_kernel(rows_each, got_ref, sum_ref):
    count = got_ref.shape[0]
    if count <= 64:
        total = got_ref[0, :rows_each, :].astype(F32)
        for d in range(1, count):
            total = total + got_ref[d, :rows_each, :].astype(F32)
    else:
        total = lax.fori_loop(
            0,
            count,
            lambda d, acc: acc + got_ref[d, :rows_each, :].astype(F32),
            jnp.zeros((rows_each, got_ref.shape[2]), F32),
        )
    share = total.astype(BF)
    if count <= 64:
        for d in range(count):
            sum_ref[d] = share
    else:

        @pl.loop(0, count)
        def _(d):
            sum_ref[d] = share


def owner_rows(n_ns, capacity, rows_each, arrived_ref, proj_ref, token_ref):
    chans = proj_ref.shape[0]
    half = capacity // 2
    ew = lax.axis_index("ew")
    arrived = jnp.concatenate(
        [arrived_ref[ew * n_ns + s, rows_each:, :] for s in range(n_ns)], axis=0
    )
    shape = (n_ns * capacity, n_ns * GROUP)
    row, col = iota(shape, 0), iota(shape, 1)
    slot = lax.rem(row, capacity)
    source = (row // capacity) * GROUP + lax.rem(slot, half)
    picked = nn((source == col).astype(F32).astype(BF), arrived)
    second = lax.rem(iota(picked.shape, 0), capacity) >= half
    picked = jnp.where(second, pltpu.roll(picked, chans, 1), picked)[:, :chans].astype(BF)
    token_ref[...] = nn(picked, proj_ref[...]).astype(BF)


def finish_kernel(
    n_ns, capacity, arrived_ref, got_ref, proj_ref, token_out, proj_out, first_out, second_out, mask_out
):
    owner_rows(n_ns, capacity, got_ref.shape[1], arrived_ref, proj_ref, token_out)
    chans, features = proj_ref.shape
    bands = second_out.shape[1]
    rows_each = got_ref.shape[1]
    parts = [got_ref[d] for d in range(GRAD_ROWS // rows_each)]
    total = jnp.concatenate(parts, axis=0).astype(F32)
    for arrangement, taps in enumerate(((1, 2), (3, 0))):
        rows = total[arrangement * 4 * chans : (arrangement + 1) * 4 * chans]
        turned = pltpu.roll(rows, chans, 1)
        for a in range(4):
            first_out[a, taps[0]] = rows[a * chans : (a + 1) * chans, :chans]
            first_out[a, taps[1]] = turned[a * chans : (a + 1) * chans, :chans]
    for k in range(features // 128):
        at = PROJ_AT + k * chans
        proj_out[:, k * 128 : (k + 1) * 128] = total[at : at + chans]
    rows = total[SECOND_AT:]
    turned = pltpu.roll(rows, chans, 1)
    for b in range(2):
        for a in range(4):
            at = (b * 4 + a) * GROUP
            second_out[a, :, b, :] = rows[at : at + bands, :chans]
            second_out[a, :, b + 2, :] = turned[at : at + bands, :chans]
    at = MASK_ROW - SECOND_AT
    mask_sum = rows[at : at + 1, :chans] + turned[at : at + 1, :chans]
    hi = mask_sum.astype(BF).astype(F32)
    mid = (mask_sum - hi).astype(BF).astype(F32)
    lo = mask_sum - hi - mid
    line = iota((16, chans), 0)
    split = jnp.where(line == 0, hi, jnp.where(line == 1, mid, jnp.where(line == 2, lo, 0.0)))
    grad_mask = jnp.sum(nn(split.astype(BF), proj_ref[...]), axis=0, keepdims=True)
    mask_out[...] = grad_mask.reshape(features)


def swap(block, axis, offset):
    count = lax.axis_size(axis)
    pairs = [(i, ((i + offset) ^ 1) - offset) for i in range(count)]
    return lax.ppermute(block, axis, [(i, j) for i, j in pairs if 0 <= j < count])


def call(kernel, outs, args, scratch=(), flops=0, limit=8 << 20, specs=None):
    return pl.pallas_call(
        kernel,
        out_shape=outs,
        in_specs=specs or [VMEM] * len(args),
        out_specs=jax.tree.map(lambda _: VMEM, outs),
        scratch_shapes=list(scratch),
        compiler_params=pltpu.CompilerParams(vmem_limit_bytes=limit),
        cost_estimate=pl.CostEstimate(flops=flops, bytes_accessed=1 << 20, transcendentals=0),
    )(*args)


def per_device(
    n_ew, n_ns, tokens, vis_index, counts, owners, mask_token, proj_weight, up_first, up_second, saved_pre, cotangent
):
    frames, slots, features = tokens.shape[2:]
    _, chans, rows, cols = saved_pre.shape
    bands, prow, pcol = cotangent.shape[1:]
    patches = rows * cols // 4
    count = n_ew * n_ns
    capacity = 3 * frames * slots // (2 * n_ns)
    rows_each = -(-GRAD_ROWS // count)
    rows_each = -(-rows_each // 16) * 16
    slots_all = frames * slots
    shape = jax.ShapeDtypeStruct

    tall = prow * GROUP
    own_p, p_edges = call(
        cell_layout_kernel,
        (shape((frames * rows * chans, cols), BF), shape((8, frames * rows * chans), F32)),
        (saved_pre,),
        [pltpu.VMEM((frames * chans * rows, cols), F32)],
        flops=1 << 31,
    )
    own_g, own_edges = call(
        pixel_layout_kernel,
        (shape((frames * tall, pcol), BF), shape((8, frames * rows * chans), BF)),
        (cotangent, p_edges),
        [pltpu.VMEM((frames * tall * pcol // 128, 128), F32)],
        flops=1 << 31,
    )
    side_b = swap(own_edges, "ew", 1)
    side_a = swap(own_edges, "ew", 0)

    tile_tokens = tokens.reshape(slots_all, features)
    proj = proj_weight.T
    g_message = shape((3 * GROUP, frames * pcol), BF)
    p_message = shape((chans, frames * cols), BF)
    g_a, p_a, g_b, p_b, grid, picks, hidden, route, wab, w2, pixels, cells = call(
        functools.partial(local_kernel, capacity),
        (
            g_message,
            p_message,
            g_message,
            p_message,
            shape((frames, 2, 2 * chans, 2 * cols), BF),
            shape((frames, slots, patches), BF),
            shape((16, frames * patches), BF),
            shape((n_ns * GROUP, 2 * slots_all), BF),
            shape((2 * chans, 8 * chans), BF),
            shape((chans, 16 * GROUP), BF),
            shape((pcol + 128, 4 * pcol), BF),
            shape((pcol, pcol), BF),
        ),
        (
            counts.reshape(1, frames),
            own_g,
            own_p,
            vis_index.reshape(frames, slots),
            owners.reshape(frames, 1, slots),
            tile_tokens,
            mask_token,
            proj,
            up_first,
            up_second.transpose(0, 2, 1, 3),
        ),
        flops=1 << 24,
        specs=[SMEM] + [VMEM] * 9,
    )
    message_shape = shape((3 * GROUP + 16, frames * (pcol + cols)), BF)
    send_a, send_b = call(
        message_kernel,
        (message_shape, message_shape),
        (g_a, p_a, g_b, p_b, side_a, side_b),
        flops=1 << 20,
    )
    got_b = swap(send_b, "ns", 1)
    got_a = swap(send_a, "ns", 0)

    delta_mid, second_mid, first_mid, turn_mid, edge_wins, edge_pre = call(
        functools.partial(inner_kernel, n_ew),
        (
            shape((frames * 4 * chans, 2 * cols), BF),
            shape((2 * 4 * GROUP, 2 * chans), F32),
            shape((8 * chans, 2 * chans), F32),
            shape((frames, 2 * chans, 2 * cols), F32),
            shape((frames, 2, 3 * GROUP, 8 * cols), BF),
            shape((frames, 2, chans, 2 * cols), F32),
        ),
        (own_g, own_p, side_a, side_b, pixels, cells, grid, wab, w2),
        [
            pltpu.VMEM((frames * tall, pcol + 128), BF),
            pltpu.VMEM((rows * frames * chans, 2 * cols), BF),
            pltpu.VMEM((frames * tall, 8 * cols), BF),
            pltpu.VMEM((rows * frames * chans, 2 * cols), F32),
        ],
        flops=1 << 27,
        limit=16 << 20,
    )
    beyond = frames * 2 * 3 * GROUP
    outgoing = call(
        functools.partial(outer_kernel, n_ew, rows_each),
        shape((count, rows_each + GROUP, 2 * chans), BF),
        (
            got_a, got_b, pixels, cells, delta_mid, second_mid, first_mid, turn_mid, edge_wins, edge_pre,
            grid, picks, hidden, route, wab, w2, tile_tokens, mask_token,
        ),
        [
            pltpu.VMEM((beyond, pcol + 128), BF),
            pltpu.VMEM((frames * 2 * chans, 2 * cols), BF),
            pltpu.VMEM((beyond, 8 * cols), BF),
            pltpu.VMEM((frames * 2 * chans, 2 * cols), F32),
            pltpu.VMEM((n_ns * GROUP, 2 * chans), BF),
        ],
        flops=1 << 27,
        limit=24 << 20,
    )
    arrived = lax.all_to_all(outgoing, ("ew", "ns"), 0, 0, tiled=True)
    shares = call(
        functools.partial(sum_kernel, rows_each),
        shape((count, rows_each, 2 * chans), BF),
        (arrived,),
        flops=1 << 24,
        limit=16 << 20,
    )
    summed = lax.all_to_all(shares, ("ew", "ns"), 0, 0, tiled=True)
    summed = summed[: GRAD_ROWS // rows_each]
    token_grad, grad_proj, grad_first, grad_second, grad_mask = call(
        functools.partial(finish_kernel, n_ns, capacity),
        (
            shape((n_ns * capacity, features), BF),
            shape((chans, features), F32),
            shape((4, 4, chans, chans), F32),
            shape((4, bands, 4, chans), F32),
            shape((features,), F32),
        ),
        (arrived, summed, proj),
        flops=1 << 20,
        limit=16 << 20,
    )
    return (token_grad[None, None], grad_proj.T, grad_first, grad_second.transpose(0, 2, 1, 3), grad_mask)


def solution(mesh):
    return jax.shard_map(
        functools.partial(per_device, mesh.shape["ew"], mesh.shape["ns"]),
        mesh=mesh,
        in_specs=(
            P("ns", "ew", None, None, None),
            P("ns", "ew", None, None),
            P("ns", "ew", None),
            P("ns", "ew", None, None, None),
            P(),
            P(),
            P(),
            P(),
            P(None, None, "ns", "ew"),
            P(None, None, "ns", "ew"),
        ),
        out_specs=(P("ns", "ew", None, None), P(), P(), P(), P()),
        check_vma=False,
    )
```

```python
import functools

import jax
import jax.numpy as jnp
import numpy as np
from jax import lax
from jax.experimental import pallas as pl
from jax.experimental.pallas import tpu as pltpu
from jax.sharding import PartitionSpec as P

BF = jnp.bfloat16
F32 = jnp.float32
VMEM = pl.BlockSpec(memory_space=pltpu.VMEM)
SMEM = pl.BlockSpec(memory_space=pltpu.SMEM)
GROUP = 16
GRAD_ROWS = 1024
PROJ_AT = 512
SECOND_AT = 896
MASK_ROW = SECOND_AT + 12


def nn(a, b):
    return lax.dot_general(a, b, (((1,), (0,)), ((), ())), preferred_element_type=F32)


def nt(a, b):
    return lax.dot_general(a, b, (((1,), (1,)), ((), ())), preferred_element_type=F32)


def tn(a, b):
    return lax.dot_general(a, b, (((0,), (0,)), ((), ())), preferred_element_type=F32)


def iota(shape, dim):
    return lax.broadcasted_iota(jnp.int32, shape, dim)


def hidden_columns(cols, lanes):
    lane = lax.rem(lanes, cols)
    right = lane >= cols // 2
    own = 2 * jnp.where(right, lane - cols // 2, lane) + jnp.where(right, 1, 0)
    shifted = own + jnp.where(right, -2, 2)
    return jnp.where(lax.rem(lanes // cols, 2) == 0, own, shifted)


def column_tables(cols, pix_ref, cell_ref):
    fine = 2 * cols
    lanes = iota((1, fine), 1)
    hidden = hidden_columns(cols, lanes)
    for tap in range(4):
        pixel = 2 * hidden + tap - 1
        pixel = jnp.where(pixel < 0, fine + 6 + pixel, pixel)
        table = iota((fine + 128, fine), 0) == pixel
        pix_ref[:, tap * fine : (tap + 1) * fine] = table.astype(F32).astype(BF)
    cell = jnp.where(hidden < 0, cols + 1, hidden)
    cell_ref[...] = (iota((fine, fine), 0) == cell).astype(F32).astype(BF)


def spread(ref, wide, group):
    frames, real, rows, cols = ref.shape
    for f in range(frames):
        for o in range(group):
            value = ref[f, o].astype(F32) if o < real else jnp.zeros((rows, cols), F32)
            for h in range(cols // 128):
                wide[pl.ds(((h * frames + f) * group + o) * rows, rows), :] = value[:, h * 128 : (h + 1) * 128]


def gathered(wide, h, frames, group, rows, f, r):
    return wide[pl.ds((h * frames + f) * group * rows + r, group, stride=rows), :].astype(BF)


def edge_tables(pcol, cols):
    row, col = iota((16, pcol), 0), iota((16, pcol), 1)
    pick_g = ((row < 3) & (col == row)) | ((row >= 3) & (row < 6) & (col == row + pcol - 6))
    row, col = iota((16, cols), 0), iota((16, cols), 1)
    pick_p = ((row == 6) & (col == 0)) | ((row == 7) & (col == cols - 1))
    return pick_g.astype(F32).astype(BF), pick_p.astype(F32).astype(BF)


def cell_layout_kernel(pre_ref, p_ref, edge_ref, pre_wide):
    frames, chans, rows, cols = pre_ref.shape
    spread(pre_ref, pre_wide, chans)
    for r in range(rows):
        for f in range(frames):
            p_ref[pl.ds((r * frames + f) * chans, chans), :] = gathered(pre_wide, 0, frames, chans, rows, f, r)
    edges = nt(edge_tables(2 * cols, cols)[1], p_ref[...])[:8]
    line = frames * chans
    last = (rows - 1) * line
    edge_ref[...] = jnp.concatenate([edges[:, :line], edges[:, last:], edges[:, line:last]], axis=1)


def pixel_layout_kernel(cot_ref, edge_ref, g_ref, own_ref, cot_wide):
    frames, bands, prow, pcol = cot_ref.shape
    spread(cot_ref, cot_wide, GROUP)
    for f in range(frames):
        for y in range(prow):
            for h in range(pcol // 128):
                g_ref[pl.ds((f * prow + y) * GROUP, GROUP), h * 128 : (h + 1) * 128] = gathered(
                    cot_wide, h, frames, GROUP, prow, f, y
                )
    edges = nt(edge_tables(pcol, pcol // 2)[0], g_ref[...])[:8]
    width = edges.shape[1]
    below = edge_ref[...]
    own_ref[...] = jnp.concatenate([edges + below[:, :width], below[:, width:]], axis=1).astype(BF)


def row_messages(g_ref, p_ref, ga_ref, pa_ref, gb_ref, pb_ref):
    deep, pcol = ga_ref.shape[0], g_ref.shape[1]
    chans, cols = pa_ref.shape[0], p_ref.shape[1]
    frames = pa_ref.shape[1] // cols
    tall = g_ref.shape[0] // frames
    high = p_ref.shape[0]

    def message(g_out, p_out, top):
        for f in range(frames):
            at = f * tall if top else (f + 1) * tall - deep
            g_out[:, f * pcol : (f + 1) * pcol] = g_ref[pl.ds(at, deep), :]
            at = f * chans if top else high - (frames - f) * chans
            p_out[:, f * cols : (f + 1) * cols] = p_ref[pl.ds(at, chans), :]

    even = lax.rem(lax.axis_index("ns"), 2) == 0

    @pl.when(even)
    def _():
        message(ga_ref, pa_ref, False)
        message(gb_ref, pb_ref, True)

    @pl.when(jnp.logical_not(even))
    def _():
        message(ga_ref, pa_ref, True)
        message(gb_ref, pb_ref, False)


def local_kernel(
    capacity, counts_ref, g_ref, p_ref, vis_ref, owners_ref, tokens_ref, mask_ref, proj_ref, first_ref, second_ref,
    ga_ref, pa_ref, gb_ref, pb_ref, grid_ref, pick_ref, hidden_ref, route_ref, wab_ref, w2_ref, pix_ref, cell_ref,
):
    row_messages(g_ref, p_ref, ga_ref, pa_ref, gb_ref, pb_ref)
    column_tables(p_ref.shape[1], pix_ref, cell_ref)
    slots_all = tokens_ref.shape[0]
    frames, slots, patches = pick_ref.shape
    chans = proj_ref.shape[0]
    bands = second_ref.shape[1]
    slot_rows = -(-capacity // 8) * 8
    owners = route_ref.shape[0] // slot_rows
    eye = (iota((chans, chans), 0) == iota((chans, chans), 1)).astype(BF)
    pad = jnp.zeros((GROUP - bands, chans), F32)
    taps = []
    for b in range(4):
        for a in range(4):
            here = iota((bands, 4, chans), 1) == b
            tap = jnp.sum(jnp.where(here, second_ref[a].astype(F32), 0.0), axis=1)
            taps.append(jnp.concatenate([tap, pad], axis=0).astype(BF))
    w2_ref[...] = nt(eye, jnp.concatenate(taps, axis=0)).astype(BF)
    left = (iota((2 * chans, chans), 0) == iota((2 * chans, chans), 1)).astype(BF)
    right = (iota((2 * chans, chans), 0) == iota((2 * chans, chans), 1) + chans).astype(BF)
    for arrangement, (lo, hi) in enumerate(((1, 2), (3, 0))):
        taps_lo = jnp.concatenate([first_ref[a, lo] for a in range(4)], axis=0)
        taps_hi = jnp.concatenate([first_ref[a, hi] for a in range(4)], axis=0)
        wab_ref[:, arrangement * 4 * chans : (arrangement + 1) * 4 * chans] = (
            nt(left, taps_lo) + nt(right, taps_hi)
        ).astype(BF)
    vis = jnp.concatenate([vis_ref[f : f + 1, :] for f in range(frames)], axis=1)
    owner = jnp.concatenate([owners_ref[f] for f in range(frames)], axis=1)
    slot = iota((1, slots_all), 1)
    live = jnp.zeros((1, slots_all), jnp.int32)
    for f in range(frames):
        inside = (slot >= f * slots) & (slot < f * slots + counts_ref[0, f])
        live = jnp.where(inside, 1, live)
    wanted = jnp.where(live > 0, vis, patches)
    square = (slots_all, slots_all)
    column = jnp.sum(
        jnp.where(iota(square, 0) == iota(square, 1), wanted.astype(F32), 0.0), axis=1, keepdims=True
    ).astype(jnp.int32)
    token_proj = nt(tokens_ref[...], proj_ref[...]).astype(BF)
    features = mask_ref.shape[0]
    mask_row = mask_ref[...].astype(F32).reshape(1, features)
    mask_proj = nt(jnp.broadcast_to(mask_row, (16, features)).astype(BF), proj_ref[...]).astype(BF)
    row0 = iota((16, patches), 0) == 0
    lane = iota((chans, 2 * chans), 1)
    for f in range(frames):
        hits = iota((slots, patches), 1) == column[f * slots : (f + 1) * slots]
        picks = hits.astype(F32)
        pick_ref[f] = picks.astype(BF)
        unseen = jnp.where(row0, 1.0 - jnp.sum(picks, axis=0, keepdims=True), 0.0).astype(BF)
        hidden_ref[:, f * patches : (f + 1) * patches] = unseen
        grid = tn(token_proj[f * slots : (f + 1) * slots], picks.astype(BF)) + tn(mask_proj, unseen)
        zero = jnp.zeros((chans, 2 * chans), F32)
        for line, (group, half_at) in enumerate(((1, 0), (0, 0), (0, 1), (1, 1))):
            pair = line // 2 * 2 * chans
            straight = grid[:, pair : pair + 2 * chans]
            turned = pltpu.roll(straight, chans, 1)
            to_left, to_right = (straight, turned) if line % 2 == 0 else (turned, straight)
            at = half_at * 2 * chans
            grid_ref[f, group, :chans, at : at + 2 * chans] = jnp.where(lane < chans, to_left, zero).astype(BF)
            grid_ref[f, group, chans:, at : at + 2 * chans] = jnp.where(lane < chans, zero, to_right).astype(BF)
    own_rows = -(-owners // 16) * 16
    hit = (iota((own_rows, slots_all), 0) == jnp.where(live > 0, owner, -1)).astype(F32)
    before = (iota(square, 0) < iota(square, 1)).astype(BF)
    earlier = nn(hit.astype(BF), before)
    place = jnp.sum(earlier * hit, axis=0, keepdims=True).astype(jnp.int32)
    block = lax.rem(owner, 2) * (owners // 2) + owner // 2
    target = jnp.where(live > 0, block * slot_rows + place, -1)
    route_ref[...] = (iota((owners * slot_rows, slots_all), 0) == target).astype(F32).astype(BF)


def side_columns(ea_ref, eb_ref, even_ew):
    ea, eb = ea_ref[...].astype(F32), eb_ref[...].astype(F32)
    return jnp.concatenate([jnp.where(even_ew, ea, eb), jnp.where(even_ew, eb, ea)], axis=0).astype(BF)


def halo_tables():
    row, col = iota((16, 128), 0), iota((16, 128), 1)
    pick_g = ((row < 3) & (col == row)) | ((row >= 11) & (row < 14) & (col == row - 8))
    pick_p = ((row == 6) & (col == 0)) | ((row == 15) & (col == 1))
    return pick_g.astype(F32).astype(BF), pick_p.astype(F32).astype(BF)


def second_backward(taps, pre, w2, drop):
    grad_hidden = nn(w2, jnp.concatenate(taps, axis=0))
    s = 0.5 + 0.5 * jnp.tanh(0.851 * pre)
    delta = grad_hidden * (s + 1.702 * pre * s * (1.0 - s))
    cols = pre.shape[1] // 2
    return jnp.where(drop, 0.0, delta).astype(BF), (pre[:, :cols] * s[:, :cols]).astype(BF)


def second_kernel_term(taps, hid):
    cols = hid.shape[1]
    zero = jnp.zeros_like(hid)
    lhs = jnp.concatenate(
        [
            jnp.concatenate([taps[0][:, :cols], taps[2][:, :cols]], axis=1),
            jnp.concatenate([taps[1][:, :cols], taps[3][:, :cols]], axis=1),
        ],
        axis=0,
    )
    rhs = jnp.concatenate(
        [jnp.concatenate([hid, zero], axis=1), jnp.concatenate([zero, hid], axis=1)], axis=0
    )
    return nt(lhs, rhs)


def outside_columns(chans, cols, n_ew, ew):
    lane = iota((chans, 2 * cols), 1)
    return ((lane == cols + cols // 2 - 1) & (ew == n_ew - 1)) | ((lane == cols + cols // 2) & (ew == 0))


def window_taps(wins, at, cols):
    return [wins[pl.ds(at, 4 * GROUP), b * 2 * cols : (b + 1) * 2 * cols] for b in range(4)]


def message_kernel(ga_ref, pa_ref, gb_ref, pb_ref, sa_ref, sb_ref, a_ref, b_ref):
    deep, span = ga_ref.shape
    corners = jnp.concatenate([sa_ref[:, :span].astype(F32), sb_ref[:, :span].astype(F32)], axis=0).astype(BF)
    for out, g, p in ((a_ref, ga_ref, pa_ref), (b_ref, gb_ref, pb_ref)):
        out[:deep, :span] = g[...]
        out[deep:, :span] = corners
        out[:, span:] = p[...]


def inner_kernel(
    n_ew, g_ref, p_ref, ea_ref, eb_ref, pix_ref, cell_ref, grid_ref, wab_ref, w2_ref,
    delta_ref, second_ref, first_ref, turn_ref, edge_ref, pre_ref, ext, wide, wins, pres,
):
    frames = grid_ref.shape[0]
    chans = w2_ref.shape[0]
    pcol, cols = g_ref.shape[1], p_ref.shape[1]
    tall = g_ref.shape[0] // frames
    rows = p_ref.shape[0] // (frames * chans)
    ew = lax.axis_index("ew")
    sides = side_columns(ea_ref, eb_ref, lax.rem(ew, 2) == 0)
    pick_g, pick_p = halo_tables()
    line = frames * chans
    ext[:, :pcol] = g_ref[...]
    ext[:, pcol:] = tn(sides[:, : frames * tall], pick_g).astype(BF)
    wide[:, :cols] = p_ref[...]
    halo = tn(sides, pick_p).astype(BF)
    wide[pl.ds(0, line), cols:] = halo[:line]
    wide[pl.ds((rows - 1) * line, line), cols:] = halo[line : 2 * line]
    wide[pl.ds(line, (rows - 2) * line), cols:] = halo[2 * line :]
    deep = 3 * GROUP
    for f in range(frames):
        block = ext[pl.ds(f * tall, tall), :]
        for b in range(4):
            lanes = slice(b * 2 * cols, (b + 1) * 2 * cols)
            wins[pl.ds(f * tall, tall), lanes] = nn(block, pix_ref[:, lanes]).astype(BF)
        edge_ref[f, 0] = wins[pl.ds(f * tall, deep), :]
        edge_ref[f, 1] = wins[pl.ds((f + 1) * tall - deep, deep), :]
    pres[...] = nn(wide[...], cell_ref[...])
    for f in range(frames):
        pre_ref[f, 0] = pres[pl.ds(f * chans, chans), :]
        pre_ref[f, 1] = pres[pl.ds((rows - 1) * line + f * chans, chans), :]
    w2 = w2_ref[...]
    wab = wab_ref[...]
    drop = outside_columns(chans, cols, n_ew, ew)
    grad_second = grad_first = None
    for f in range(frames):
        deltas = []
        for i in range(1, rows - 1):
            taps = window_taps(wins, f * tall + (2 * i - 1) * GROUP, cols)
            pre = pres[pl.ds(i * line + f * chans, chans), :]
            delta, hid = second_backward(taps, pre, w2, drop)
            deltas.append(delta)
            term = second_kernel_term(taps, hid)
            grad_second = term if grad_second is None else grad_second + term
        count = rows - 2
        for k, i in enumerate((0, 1, count - 2, count - 1)):
            delta_ref[pl.ds((f * 4 + k) * chans, chans), :] = deltas[i]
        cells = []
        for i in (0, 2):
            slab = jnp.concatenate(deltas[i : i + 4], axis=0)
            cells.append(jnp.concatenate([slab[:, :cols], slab[:, cols:]], axis=0))
        both = jnp.concatenate(cells, axis=1)
        term = nt(both, grid_ref[f, 0])
        grad_first = term if grad_first is None else grad_first + term
        turn_ref[f] = nn(wab, both)
    second_ref[...] = grad_second
    first_ref[...] = grad_first


def outer_kernel(
    n_ew, n_ns, ra_ref, rb_ref, pix_ref, cell_ref,
    delta_ref, second_ref, first_ref, turn_ref, edge_ref, pre_ref,
    grid_ref, pick_ref, hidden_ref, route_ref, wab_ref, w2_ref, tokens_ref, mask_ref,
    keep_ref, give_ref, ext, wide, wins, pres,
):
    frames, slots, patches = pick_ref.shape
    chans = w2_ref.shape[0]
    features = tokens_ref.shape[1]
    cols = pre_ref.shape[3] // 2
    pcol = 2 * cols
    deep = 3 * GROUP
    ns = lax.axis_index("ns")
    ew = lax.axis_index("ew")
    even_ns = lax.rem(ns, 2) == 0
    even_ew = lax.rem(ew, 2) == 0
    ra, rb = ra_ref[...], rb_ref[...]
    north = jnp.where(even_ns, rb, ra)
    south = jnp.where(even_ns, ra, rb)
    span = frames * pcol
    tall = span // frames

    def far_sides(message):
        a, b = message[deep : deep + 8, :span].astype(F32), message[deep + 8 :, :span].astype(F32)
        return jnp.concatenate([jnp.where(even_ew, a, b), jnp.where(even_ew, b, a)], axis=0).astype(BF)

    pick_g, pick_p = halo_tables()
    line = frames * chans
    far = (far_sides(north), far_sides(south))
    for low in range(2):
        message = south if low else north
        halo_p = tn(far[low][:, (1 - low) * line : (2 - low) * line], pick_p).astype(BF)
        for f in range(frames):
            at = (f * 2 + low) * deep
            ext[pl.ds(at, deep), :pcol] = message[:deep, f * pcol : (f + 1) * pcol]
            if low:
                ext[pl.ds(at, deep), pcol:] = tn(far[low][:, f * tall : f * tall + 128], pick_g).astype(BF)[:deep]
            else:
                end = (f + 1) * tall
                ext[pl.ds(at, deep), pcol:] = tn(far[low][:, end - 128 : end], pick_g).astype(BF)[128 - deep :]
            at = (f * 2 + low) * chans
            wide[pl.ds(at, chans), :cols] = message[:, span + f * cols : span + (f + 1) * cols]
            wide[pl.ds(at, chans), cols:] = halo_p[f * chans : (f + 1) * chans]
    block = ext[...]
    for b in range(4):
        lanes = slice(b * 2 * cols, (b + 1) * 2 * cols)
        wins[:, lanes] = nn(block, pix_ref[:, lanes]).astype(BF)
    pres[...] = nn(wide[...], cell_ref[...])
    w2 = w2_ref[...]
    wab = wab_ref[...]
    drop = outside_columns(chans, cols, n_ew, ew)
    grad_second = second_ref[...]
    grad_first = first_ref[...]
    half_lane = iota((chans, cols), 1) < cols // 2
    grids = []
    for f in range(frames):
        cells = []
        for low in range(2):
            pair = []
            for k in range(2):
                inside = k == 1 - low
                beyond = wins[pl.ds((f * 2 + low) * deep, deep), :]
                window = [edge_ref[f, low], beyond] if low else [beyond, edge_ref[f, low]]
                window = jnp.concatenate(window, axis=0)[k * 2 * GROUP : (k * 2 + 4) * GROUP]
                taps = [window[:, b * 2 * cols : (b + 1) * 2 * cols] for b in range(4)]
                pre = pre_ref[f, low] if inside else pres[pl.ds((f * 2 + low) * chans, chans), :]
                gone = drop if inside else drop | (ns == (n_ns - 1 if low else 0))
                delta, hid = second_backward(taps, pre, w2, gone)
                pair.append(delta)
                if inside:
                    grad_second = grad_second + second_kernel_term(taps, hid)
            kept = delta_ref[pl.ds((f * 4 + 2 * low) * chans, 2 * chans), :]
            slab = jnp.concatenate([kept, *pair] if low else [*pair, kept], axis=0)
            cells.append(jnp.concatenate([slab[:, :cols], slab[:, cols:]], axis=0))
        both = jnp.concatenate(cells, axis=1)
        grad_first = grad_first + nt(both, grid_ref[f, 1])
        edge = nn(wab, both)
        inner = turn_ref[f]
        parts = []
        for even, odd in ((edge[:, :cols], inner[:, :cols]), (inner[:, cols:], edge[:, cols:])):
            here = jnp.where(half_lane, even[:chans], odd[chans:])
            there = jnp.where(half_lane, odd[:chans], even[chans:])
            parts.append(here + pltpu.roll(there, cols // 2, 1))
        grids.append(jnp.concatenate(parts, axis=1).astype(BF))
    none = jnp.zeros((chans, patches), BF)
    mask_sum = nt(hidden_ref[...], jnp.concatenate(grids, axis=1))
    chosen = [nt(pick_ref[f], jnp.concatenate([grids[f], none], axis=0)) for f in range(frames)]
    chosen = jnp.concatenate(chosen, axis=0)
    placed = jnp.where(even_ns, chosen, pltpu.roll(chosen, chans, 1)).astype(BF)
    chosen = chosen.astype(BF)
    routed = nn(route_ref[...], placed)
    hi = mask_sum.astype(BF).astype(F32)
    lo = mask_sum - hi
    line = iota(hi.shape, 0)
    mask_rows = jnp.where(line == 0, hi[0:1], jnp.where(line == 1, lo[0:1], 0.0)).astype(BF)
    line = iota((16, features), 0)
    mask_row = mask_ref[...].astype(F32).reshape(1, features)
    spread_row = jnp.where(line < 2, mask_row, 0.0).astype(BF)
    grad_proj = tn(chosen[:, :chans], tokens_ref[...]) + tn(mask_rows, spread_row)
    grad_proj = [grad_proj[:, k * 128 : (k + 1) * 128] for k in range(features // 128)]
    both = jnp.concatenate([hi[0:1], lo[0:1]], axis=1)
    mark = iota(grad_second.shape, 0) == MASK_ROW - SECOND_AT
    grad_second = jnp.where(mark, both, grad_second)
    halves = (grad_first, jnp.concatenate([*grad_proj, grad_second], axis=0))
    part = routed.shape[0] // 2

    def split(mine):
        keep_ref[: GRAD_ROWS // 2, :] = halves[mine]
        keep_ref[GRAD_ROWS // 2 :, :] = routed[mine * part : (mine + 1) * part]
        give_ref[: GRAD_ROWS // 2, :] = halves[1 - mine].astype(BF)
        give_ref[GRAD_ROWS // 2 :, :] = routed[(1 - mine) * part : (2 - mine) * part].astype(BF)

    @pl.when(even_ns)
    def _():
        split(0)

    @pl.when(jnp.logical_not(even_ns))
    def _():
        split(1)


def chip_kernel(rows_each, keep_ref, got_ref, out_ref):
    count = out_ref.shape[0]
    slot_rows = out_ref.shape[1] - rows_each
    grads = GRAD_ROWS // 2
    chips = (keep_ref.shape[0] - grads) // slot_rows
    total = (keep_ref[...] + got_ref[...].astype(F32)).astype(BF)
    full = min(count, grads // rows_each)
    for d in range(full):
        out_ref[d, :rows_each, :] = total[d * rows_each : (d + 1) * rows_each]
    if full < count:

        @pl.loop(full, count)
        def _(d):
            out_ref[d, :rows_each, :] = jnp.zeros((rows_each, total.shape[1]), BF)

    for z in range(chips):
        rows = total[grads + z * slot_rows : grads + (z + 1) * slot_rows]
        for e in range(count // chips):
            out_ref[e * chips + z, rows_each:, :] = rows


def sum_kernel(rows_each, got_ref, sum_ref):
    count = got_ref.shape[0]
    if count <= 64:
        total = got_ref[0, :rows_each, :].astype(F32)
        for d in range(1, count):
            total = total + got_ref[d, :rows_each, :].astype(F32)
    else:
        total = lax.fori_loop(
            0,
            count,
            lambda d, acc: acc + got_ref[d, :rows_each, :].astype(F32),
            jnp.zeros((rows_each, got_ref.shape[2]), F32),
        )
    share = total.astype(BF)
    if count <= 64:
        for d in range(count):
            sum_ref[d] = share
    else:

        @pl.loop(0, count)
        def _(d):
            sum_ref[d] = share


def owner_kernel(capacity, rows_each, arrived_ref, proj_ref, token_ref):
    chans = proj_ref.shape[0]
    slot_rows = arrived_ref.shape[1] - rows_each
    chips = token_ref.shape[0] // (2 * capacity)
    ew = lax.axis_index("ew")
    arrived = [arrived_ref[ew * chips + z, rows_each:, :].astype(F32) for z in range(chips)]
    arrived = jnp.concatenate(arrived, axis=0).astype(BF)
    shape = (token_ref.shape[0], chips * slot_rows)
    row, col = iota(shape, 0), iota(shape, 1)
    source = (row // (2 * capacity)) * slot_rows + lax.rem(row, capacity)
    picked = nn((source == col).astype(F32).astype(BF), arrived)
    second = lax.rem(iota(picked.shape, 0) // capacity, 2) == 1
    picked = jnp.where(second, pltpu.roll(picked, chans, 1), picked)[:, :chans].astype(BF)
    token_ref[...] = nn(picked, proj_ref[...]).astype(BF)


def finish_kernel(mine_ref, other_ref, proj_ref, proj_out, first_out, second_out, mask_out):
    chans, features = proj_ref.shape
    bands = second_out.shape[1]
    rows_each = mine_ref.shape[1]
    blocks = range(GRAD_ROWS // 2 // rows_each)
    mine = jnp.concatenate([mine_ref[d] for d in blocks], axis=0)
    other = jnp.concatenate([other_ref[d] for d in blocks], axis=0)
    even = lax.rem(lax.axis_index("ns"), 2) == 0
    total = [jnp.where(even, mine, other), jnp.where(even, other, mine)]
    total = jnp.concatenate(total, axis=0).astype(F32)
    for arrangement, taps in enumerate(((1, 2), (3, 0))):
        rows = total[arrangement * 4 * chans : (arrangement + 1) * 4 * chans]
        turned = pltpu.roll(rows, chans, 1)
        for a in range(4):
            first_out[a, taps[0]] = rows[a * chans : (a + 1) * chans, :chans]
            first_out[a, taps[1]] = turned[a * chans : (a + 1) * chans, :chans]
    for k in range(features // 128):
        at = PROJ_AT + k * chans
        proj_out[:, k * 128 : (k + 1) * 128] = total[at : at + chans]
    rows = total[SECOND_AT:]
    turned = pltpu.roll(rows, chans, 1)
    for b in range(2):
        for a in range(4):
            at = (b * 4 + a) * GROUP
            second_out[a, :, b, :] = rows[at : at + bands, :chans]
            second_out[a, :, b + 2, :] = turned[at : at + bands, :chans]
    at = MASK_ROW - SECOND_AT
    mask_sum = rows[at : at + 1, :chans] + turned[at : at + 1, :chans]
    hi = mask_sum.astype(BF).astype(F32)
    mid = (mask_sum - hi).astype(BF).astype(F32)
    lo = mask_sum - hi - mid
    line = iota((16, chans), 0)
    split = jnp.where(line == 0, hi, jnp.where(line == 1, mid, jnp.where(line == 2, lo, 0.0)))
    grad_mask = jnp.sum(nn(split.astype(BF), proj_ref[...]), axis=0, keepdims=True)
    mask_out[...] = grad_mask.reshape(features)


def swap(block, axis, offset):
    count = lax.axis_size(axis)
    pairs = [(i, ((i + offset) ^ 1) - offset) for i in range(count)]
    return lax.ppermute(block, axis, [(i, j) for i, j in pairs if 0 <= j < count])


def call(kernel, outs, args, scratch=(), flops=0, limit=8 << 20, specs=None):
    return pl.pallas_call(
        kernel,
        out_shape=outs,
        in_specs=specs or [VMEM] * len(args),
        out_specs=jax.tree.map(lambda _: VMEM, outs),
        scratch_shapes=list(scratch),
        compiler_params=pltpu.CompilerParams(vmem_limit_bytes=limit),
        cost_estimate=pl.CostEstimate(flops=flops, bytes_accessed=1 << 20, transcendentals=0),
    )(*args)


def per_device(
    n_ew, n_ns, tokens, vis_index, counts, owners, mask_token, proj_weight, up_first, up_second, saved_pre, cotangent
):
    frames, slots, features = tokens.shape[2:]
    _, chans, rows, cols = saved_pre.shape
    bands, prow, pcol = cotangent.shape[1:]
    patches = rows * cols // 4
    count = n_ew * n_ns
    capacity = 3 * frames * slots // (2 * n_ns)
    rows_each = -(-GRAD_ROWS // count)
    rows_each = -(-rows_each // 16) * 16
    slot_rows = -(-capacity // 8) * 8
    groups = [[e * n_ns + z * 2 + c for e in range(n_ew) for z in range(n_ns // 2)] for c in range(2)]
    slots_all = frames * slots
    shape = jax.ShapeDtypeStruct

    tall = prow * GROUP
    own_p, p_edges = call(
        cell_layout_kernel,
        (shape((frames * rows * chans, cols), BF), shape((8, frames * rows * chans), F32)),
        (saved_pre,),
        [pltpu.VMEM((frames * chans * rows, cols), F32)],
        flops=1 << 31,
    )
    own_g, own_edges = call(
        pixel_layout_kernel,
        (shape((frames * tall, pcol), BF), shape((8, frames * rows * chans), BF)),
        (cotangent, p_edges),
        [pltpu.VMEM((frames * tall * pcol // 128, 128), F32)],
        flops=1 << 31,
    )
    side_b = swap(own_edges, "ew", 1)
    side_a = swap(own_edges, "ew", 0)

    tile_tokens = tokens.reshape(slots_all, features)
    proj = proj_weight.T
    g_message = shape((3 * GROUP, frames * pcol), BF)
    p_message = shape((chans, frames * cols), BF)
    g_a, p_a, g_b, p_b, grid, picks, hidden, route, wab, w2, pixels, cells = call(
        functools.partial(local_kernel, capacity),
        (
            g_message,
            p_message,
            g_message,
            p_message,
            shape((frames, 2, 2 * chans, 2 * cols), BF),
            shape((frames, slots, patches), BF),
            shape((16, frames * patches), BF),
            shape((n_ns * slot_rows, slots_all), BF),
            shape((2 * chans, 8 * chans), BF),
            shape((chans, 16 * GROUP), BF),
            shape((pcol + 128, 4 * pcol), BF),
            shape((pcol, pcol), BF),
        ),
        (
            counts.reshape(1, frames),
            own_g,
            own_p,
            vis_index.reshape(frames, slots),
            owners.reshape(frames, 1, slots),
            tile_tokens,
            mask_token,
            proj,
            up_first,
            up_second.transpose(0, 2, 1, 3),
        ),
        flops=1 << 24,
        specs=[SMEM] + [VMEM] * 9,
    )
    message_shape = shape((3 * GROUP + 16, frames * (pcol + cols)), BF)
    send_a, send_b = call(
        message_kernel,
        (message_shape, message_shape),
        (g_a, p_a, g_b, p_b, side_a, side_b),
        flops=1 << 20,
    )
    got_b = swap(send_b, "ns", 1)
    got_a = swap(send_a, "ns", 0)

    delta_mid, second_mid, first_mid, turn_mid, edge_wins, edge_pre = call(
        functools.partial(inner_kernel, n_ew),
        (
            shape((frames * 4 * chans, 2 * cols), BF),
            shape((2 * 4 * GROUP, 2 * chans), F32),
            shape((8 * chans, 2 * chans), F32),
            shape((frames, 2 * chans, 2 * cols), F32),
            shape((frames, 2, 3 * GROUP, 8 * cols), BF),
            shape((frames, 2, chans, 2 * cols), F32),
        ),
        (own_g, own_p, side_a, side_b, pixels, cells, grid, wab, w2),
        [
            pltpu.VMEM((frames * tall, pcol + 128), BF),
            pltpu.VMEM((rows * frames * chans, 2 * cols), BF),
            pltpu.VMEM((frames * tall, 8 * cols), BF),
            pltpu.VMEM((rows * frames * chans, 2 * cols), F32),
        ],
        flops=1 << 27,
        limit=16 << 20,
    )
    beyond = frames * 2 * 3 * GROUP
    half_rows = GRAD_ROWS // 2 + n_ns // 2 * slot_rows
    keep, give = call(
        functools.partial(outer_kernel, n_ew, n_ns),
        (shape((half_rows, 2 * chans), F32), shape((half_rows, 2 * chans), BF)),
        (
            got_a, got_b, pixels, cells, delta_mid, second_mid, first_mid, turn_mid, edge_wins, edge_pre,
            grid, picks, hidden, route, wab, w2, tile_tokens, mask_token,
        ),
        [
            pltpu.VMEM((beyond, pcol + 128), BF),
            pltpu.VMEM((frames * 2 * chans, 2 * cols), BF),
            pltpu.VMEM((beyond, 8 * cols), BF),
            pltpu.VMEM((frames * 2 * chans, 2 * cols), F32),
        ],
        flops=1 << 27,
        limit=24 << 20,
    )

    def exchange(blocks):
        return lax.all_to_all(blocks, ("ew", "ns"), 0, 0, axis_index_groups=groups, tiled=True)

    outgoing = call(
        functools.partial(chip_kernel, rows_each),
        shape((count // 2, rows_each + slot_rows, 2 * chans), BF),
        (keep, swap(give, "ns", 0)),
        flops=1 << 20,
    )
    arrived = exchange(outgoing)
    shares = call(
        functools.partial(sum_kernel, rows_each),
        shape((count // 2, rows_each, 2 * chans), BF),
        (arrived,),
        flops=1 << 20,
    )
    summed = exchange(shares)[: GRAD_ROWS // 2 // rows_each]
    other = swap(summed, "ns", 0)
    token_grad = call(
        functools.partial(owner_kernel, capacity, rows_each),
        shape((n_ns * capacity, features), BF),
        (arrived, proj),
        flops=1 << 27,
    )
    grad_proj, grad_first, grad_second, grad_mask = call(
        finish_kernel,
        (
            shape((chans, features), F32),
            shape((4, 4, chans, chans), F32),
            shape((4, bands, 4, chans), F32),
            shape((features,), F32),
        ),
        (summed, other, proj),
        flops=1 << 20,
    )
    return (token_grad[None, None], grad_proj.T, grad_first, grad_second.transpose(0, 2, 1, 3), grad_mask)


def solution(mesh):
    return jax.shard_map(
        functools.partial(per_device, mesh.shape["ew"], mesh.shape["ns"]),
        mesh=mesh,
        in_specs=(
            P("ns", "ew", None, None, None),
            P("ns", "ew", None, None),
            P("ns", "ew", None),
            P("ns", "ew", None, None, None),
            P(),
            P(),
            P(),
            P(),
            P(None, None, "ns", "ew"),
            P(None, None, "ns", "ew"),
        ),
        out_specs=(P("ns", "ew", None, None), P(), P(), P(), P()),
        check_vma=False,
    )
```

```python
import functools

import jax
import jax.numpy as jnp
import numpy as np
from jax import lax
from jax.experimental import pallas as pl
from jax.experimental.pallas import tpu as pltpu
from jax.sharding import PartitionSpec as P

BF = jnp.bfloat16
F32 = jnp.float32
VMEM = pl.BlockSpec(memory_space=pltpu.VMEM)
SMEM = pl.BlockSpec(memory_space=pltpu.SMEM)
GROUP = 16
GRAD_ROWS = 1024
PROJ_AT = 512
SECOND_AT = 896
MASK_ROW = SECOND_AT + 12


def nn(a, b):
    return lax.dot_general(a, b, (((1,), (0,)), ((), ())), preferred_element_type=F32)


def nt(a, b):
    return lax.dot_general(a, b, (((1,), (1,)), ((), ())), preferred_element_type=F32)


def tn(a, b):
    return lax.dot_general(a, b, (((0,), (0,)), ((), ())), preferred_element_type=F32)


def iota(shape, dim):
    return lax.broadcasted_iota(jnp.int32, shape, dim)


def hidden_columns(cols, lanes):
    lane = lax.rem(lanes, cols)
    right = lane >= cols // 2
    own = 2 * jnp.where(right, lane - cols // 2, lane) + jnp.where(right, 1, 0)
    shifted = own + jnp.where(right, -2, 2)
    return jnp.where(lax.rem(lanes // cols, 2) == 0, own, shifted)


def column_tables(cols, pix_ref, cell_ref):
    fine = 2 * cols
    lanes = iota((1, fine), 1)
    hidden = hidden_columns(cols, lanes)
    for tap in range(4):
        pixel = 2 * hidden + tap - 1
        pixel = jnp.where(pixel < 0, fine + 6 + pixel, pixel)
        table = iota((fine + 128, fine), 0) == pixel
        pix_ref[:, tap * fine : (tap + 1) * fine] = table.astype(F32).astype(BF)
    cell = jnp.where(hidden < 0, cols + 1, hidden)
    cell_ref[...] = (iota((fine, fine), 0) == cell).astype(F32).astype(BF)


def spread(ref, wide, group):
    frames, real, rows, cols = ref.shape
    for f in range(frames):
        for o in range(group):
            value = ref[f, o].astype(F32) if o < real else jnp.zeros((rows, cols), F32)
            for h in range(cols // 128):
                wide[pl.ds(((h * frames + f) * group + o) * rows, rows), :] = value[:, h * 128 : (h + 1) * 128]


def gathered(wide, h, frames, group, rows, f, r):
    return wide[pl.ds((h * frames + f) * group * rows + r, group, stride=rows), :].astype(BF)


def edge_tables(pcol, cols):
    row, col = iota((16, pcol), 0), iota((16, pcol), 1)
    pick_g = ((row < 3) & (col == row)) | ((row >= 3) & (row < 6) & (col == row + pcol - 6))
    row, col = iota((16, cols), 0), iota((16, cols), 1)
    pick_p = ((row == 6) & (col == 0)) | ((row == 7) & (col == cols - 1))
    return pick_g.astype(F32).astype(BF), pick_p.astype(F32).astype(BF)


def cell_layout_kernel(pre_ref, p_ref, edge_ref, pre_wide):
    frames, chans, rows, cols = pre_ref.shape
    spread(pre_ref, pre_wide, chans)
    for r in range(rows):
        for f in range(frames):
            p_ref[pl.ds((r * frames + f) * chans, chans), :] = gathered(pre_wide, 0, frames, chans, rows, f, r)
    edges = nt(edge_tables(2 * cols, cols)[1], p_ref[...])[:8]
    line = frames * chans
    last = (rows - 1) * line
    edge_ref[...] = jnp.concatenate([edges[:, :line], edges[:, last:], edges[:, line:last]], axis=1)


def pixel_layout_kernel(cot_ref, edge_ref, g_ref, own_ref, cot_wide):
    frames, bands, prow, pcol = cot_ref.shape
    spread(cot_ref, cot_wide, GROUP)
    for f in range(frames):
        for y in range(prow):
            for h in range(pcol // 128):
                g_ref[pl.ds((f * prow + y) * GROUP, GROUP), h * 128 : (h + 1) * 128] = gathered(
                    cot_wide, h, frames, GROUP, prow, f, y
                )
    edges = nt(edge_tables(pcol, pcol // 2)[0], g_ref[...])[:8]
    width = edges.shape[1]
    below = edge_ref[...]
    own_ref[...] = jnp.concatenate([edges + below[:, :width], below[:, width:]], axis=1).astype(BF)


def row_messages(g_ref, p_ref, ga_ref, pa_ref, gb_ref, pb_ref):
    deep, pcol = ga_ref.shape[0], g_ref.shape[1]
    chans, cols = pa_ref.shape[0], p_ref.shape[1]
    frames = pa_ref.shape[1] // cols
    tall = g_ref.shape[0] // frames
    high = p_ref.shape[0]

    def message(g_out, p_out, top):
        for f in range(frames):
            at = f * tall if top else (f + 1) * tall - deep
            g_out[:, f * pcol : (f + 1) * pcol] = g_ref[pl.ds(at, deep), :]
            at = f * chans if top else high - (frames - f) * chans
            p_out[:, f * cols : (f + 1) * cols] = p_ref[pl.ds(at, chans), :]

    even = lax.rem(lax.axis_index("ns"), 2) == 0

    @pl.when(even)
    def _():
        message(ga_ref, pa_ref, False)
        message(gb_ref, pb_ref, True)

    @pl.when(jnp.logical_not(even))
    def _():
        message(ga_ref, pa_ref, True)
        message(gb_ref, pb_ref, False)


def local_kernel(
    capacity, counts_ref, g_ref, p_ref, vis_ref, owners_ref, tokens_ref, mask_ref, proj_ref, first_ref, second_ref,
    ga_ref, pa_ref, gb_ref, pb_ref, grid_ref, pick_ref, hidden_ref, route_ref, wab_ref, w2_ref, pix_ref, cell_ref,
):
    row_messages(g_ref, p_ref, ga_ref, pa_ref, gb_ref, pb_ref)
    column_tables(p_ref.shape[1], pix_ref, cell_ref)
    slots_all = tokens_ref.shape[0]
    frames, slots, patches = pick_ref.shape
    chans = proj_ref.shape[0]
    bands = second_ref.shape[1]
    slot_rows = -(-capacity // 8) * 8
    owners = route_ref.shape[0] // slot_rows
    eye = (iota((chans, chans), 0) == iota((chans, chans), 1)).astype(BF)
    pad = jnp.zeros((GROUP - bands, chans), F32)
    taps = []
    for b in range(4):
        for a in range(4):
            here = iota((bands, 4, chans), 1) == b
            tap = jnp.sum(jnp.where(here, second_ref[a].astype(F32), 0.0), axis=1)
            taps.append(jnp.concatenate([tap, pad], axis=0).astype(BF))
    w2_ref[...] = nt(eye, jnp.concatenate(taps, axis=0)).astype(BF)
    left = (iota((2 * chans, chans), 0) == iota((2 * chans, chans), 1)).astype(BF)
    right = (iota((2 * chans, chans), 0) == iota((2 * chans, chans), 1) + chans).astype(BF)
    for arrangement, (lo, hi) in enumerate(((1, 2), (3, 0))):
        taps_lo = jnp.concatenate([first_ref[a, lo] for a in range(4)], axis=0)
        taps_hi = jnp.concatenate([first_ref[a, hi] for a in range(4)], axis=0)
        wab_ref[:, arrangement * 4 * chans : (arrangement + 1) * 4 * chans] = (
            nt(left, taps_lo) + nt(right, taps_hi)
        ).astype(BF)
    vis = jnp.concatenate([vis_ref[f : f + 1, :] for f in range(frames)], axis=1)
    owner = jnp.concatenate([owners_ref[f] for f in range(frames)], axis=1)
    slot = iota((1, slots_all), 1)
    live = jnp.zeros((1, slots_all), jnp.int32)
    for f in range(frames):
        inside = (slot >= f * slots) & (slot < f * slots + counts_ref[0, f])
        live = jnp.where(inside, 1, live)
    wanted = jnp.where(live > 0, vis, patches)
    square = (slots_all, slots_all)
    column = jnp.sum(
        jnp.where(iota(square, 0) == iota(square, 1), wanted.astype(F32), 0.0), axis=1, keepdims=True
    ).astype(jnp.int32)
    token_proj = nt(tokens_ref[...], proj_ref[...]).astype(BF)
    features = mask_ref.shape[0]
    mask_row = mask_ref[...].astype(F32).reshape(1, features)
    mask_proj = nt(jnp.broadcast_to(mask_row, (16, features)).astype(BF), proj_ref[...]).astype(BF)
    row0 = iota((16, patches), 0) == 0
    lane = iota((chans, 2 * chans), 1)
    for f in range(frames):
        hits = iota((slots, patches), 1) == column[f * slots : (f + 1) * slots]
        picks = hits.astype(F32)
        pick_ref[f] = picks.astype(BF)
        unseen = jnp.where(row0, 1.0 - jnp.sum(picks, axis=0, keepdims=True), 0.0).astype(BF)
        hidden_ref[:, f * patches : (f + 1) * patches] = unseen
        grid = tn(token_proj[f * slots : (f + 1) * slots], picks.astype(BF)) + tn(mask_proj, unseen)
        zero = jnp.zeros((chans, 2 * chans), F32)
        for line, (group, half_at) in enumerate(((1, 0), (0, 0), (0, 1), (1, 1))):
            pair = line // 2 * 2 * chans
            straight = grid[:, pair : pair + 2 * chans]
            turned = pltpu.roll(straight, chans, 1)
            to_left, to_right = (straight, turned) if line % 2 == 0 else (turned, straight)
            at = half_at * 2 * chans
            grid_ref[f, group, :chans, at : at + 2 * chans] = jnp.where(lane < chans, to_left, zero).astype(BF)
            grid_ref[f, group, chans:, at : at + 2 * chans] = jnp.where(lane < chans, zero, to_right).astype(BF)
    own_rows = -(-owners // 16) * 16
    hit = (iota((own_rows, slots_all), 0) == jnp.where(live > 0, owner, -1)).astype(F32)
    before = (iota(square, 0) < iota(square, 1)).astype(BF)
    earlier = nn(hit.astype(BF), before)
    place = jnp.sum(earlier * hit, axis=0, keepdims=True).astype(jnp.int32)
    block = lax.rem(owner, 2) * (owners // 2) + owner // 2
    target = jnp.where(live > 0, block * slot_rows + place, -1)
    route_ref[...] = (iota((owners * slot_rows, slots_all), 0) == target).astype(F32).astype(BF)


def side_columns(ea_ref, eb_ref, even_ew):
    ea, eb = ea_ref[...].astype(F32), eb_ref[...].astype(F32)
    return jnp.concatenate([jnp.where(even_ew, ea, eb), jnp.where(even_ew, eb, ea)], axis=0).astype(BF)


def halo_tables():
    row, col = iota((16, 128), 0), iota((16, 128), 1)
    pick_g = ((row < 3) & (col == row)) | ((row >= 11) & (row < 14) & (col == row - 8))
    pick_p = ((row == 6) & (col == 0)) | ((row == 15) & (col == 1))
    return pick_g.astype(F32).astype(BF), pick_p.astype(F32).astype(BF)


def second_backward(taps, pre, w2, drop):
    grad_hidden = nn(w2, jnp.concatenate(taps, axis=0))
    s = 0.5 + 0.5 * jnp.tanh(0.851 * pre)
    delta = grad_hidden * (s + 1.702 * pre * s * (1.0 - s))
    cols = pre.shape[1] // 2
    return jnp.where(drop, 0.0, delta).astype(BF), (pre[:, :cols] * s[:, :cols]).astype(BF)


def second_kernel_term(taps, hid):
    cols = hid.shape[1]
    zero = jnp.zeros_like(hid)
    lhs = jnp.concatenate(
        [
            jnp.concatenate([taps[0][:, :cols], taps[2][:, :cols]], axis=1),
            jnp.concatenate([taps[1][:, :cols], taps[3][:, :cols]], axis=1),
        ],
        axis=0,
    )
    rhs = jnp.concatenate(
        [jnp.concatenate([hid, zero], axis=1), jnp.concatenate([zero, hid], axis=1)], axis=0
    )
    return nt(lhs, rhs)


def outside_columns(chans, cols, n_ew, ew):
    lane = iota((chans, 2 * cols), 1)
    return ((lane == cols + cols // 2 - 1) & (ew == n_ew - 1)) | ((lane == cols + cols // 2) & (ew == 0))


def window_taps(wins, at, cols):
    return [wins[pl.ds(at, 4 * GROUP), b * 2 * cols : (b + 1) * 2 * cols] for b in range(4)]


def message_kernel(sb_ref, sa_ref, ga_ref, pa_ref, gb_ref, pb_ref, a_ref, b_ref):
    deep, span = ga_ref.shape
    corners = jnp.concatenate([sa_ref[:, :span].astype(F32), sb_ref[:, :span].astype(F32)], axis=0).astype(BF)
    for out, g, p in ((a_ref, ga_ref, pa_ref), (b_ref, gb_ref, pb_ref)):
        out[:deep, :span] = g[...]
        out[deep:, :span] = corners
        out[:, span:] = p[...]


def inner_kernel(
    n_ew, eb_ref, ea_ref, g_ref, p_ref, pix_ref, cell_ref, grid_ref, wab_ref, w2_ref,
    delta_ref, second_ref, first_ref, turn_ref, edge_ref, pre_ref, ext, wide, wins, pres,
):
    frames = grid_ref.shape[0]
    chans = w2_ref.shape[0]
    pcol, cols = g_ref.shape[1], p_ref.shape[1]
    tall = g_ref.shape[0] // frames
    rows = p_ref.shape[0] // (frames * chans)
    ew = lax.axis_index("ew")
    sides = side_columns(ea_ref, eb_ref, lax.rem(ew, 2) == 0)
    pick_g, pick_p = halo_tables()
    line = frames * chans
    ext[:, :pcol] = g_ref[...]
    ext[:, pcol:] = tn(sides[:, : frames * tall], pick_g).astype(BF)
    wide[:, :cols] = p_ref[...]
    halo = tn(sides, pick_p).astype(BF)
    wide[pl.ds(0, line), cols:] = halo[:line]
    wide[pl.ds((rows - 1) * line, line), cols:] = halo[line : 2 * line]
    wide[pl.ds(line, (rows - 2) * line), cols:] = halo[2 * line :]
    deep = 3 * GROUP
    for f in range(frames):
        block = ext[pl.ds(f * tall, tall), :]
        for b in range(4):
            lanes = slice(b * 2 * cols, (b + 1) * 2 * cols)
            wins[pl.ds(f * tall, tall), lanes] = nn(block, pix_ref[:, lanes]).astype(BF)
        edge_ref[f, 0] = wins[pl.ds(f * tall, deep), :]
        edge_ref[f, 1] = wins[pl.ds((f + 1) * tall - deep, deep), :]
    pres[...] = nn(wide[...], cell_ref[...])
    for f in range(frames):
        pre_ref[f, 0] = pres[pl.ds(f * chans, chans), :]
        pre_ref[f, 1] = pres[pl.ds((rows - 1) * line + f * chans, chans), :]
    w2 = w2_ref[...]
    wab = wab_ref[...]
    drop = outside_columns(chans, cols, n_ew, ew)
    grad_second = grad_first = None
    for f in range(frames):
        deltas = []
        for i in range(1, rows - 1):
            taps = window_taps(wins, f * tall + (2 * i - 1) * GROUP, cols)
            pre = pres[pl.ds(i * line + f * chans, chans), :]
            delta, hid = second_backward(taps, pre, w2, drop)
            deltas.append(delta)
            term = second_kernel_term(taps, hid)
            grad_second = term if grad_second is None else grad_second + term
        count = rows - 2
        for k, i in enumerate((0, 1, count - 2, count - 1)):
            delta_ref[pl.ds((f * 4 + k) * chans, chans), :] = deltas[i]
        cells = []
        for i in (0, 2):
            slab = jnp.concatenate(deltas[i : i + 4], axis=0)
            cells.append(jnp.concatenate([slab[:, :cols], slab[:, cols:]], axis=0))
        both = jnp.concatenate(cells, axis=1)
        term = nt(both, grid_ref[f, 0])
        grad_first = term if grad_first is None else grad_first + term
        turn_ref[f] = nn(wab, both)
    second_ref[...] = grad_second
    first_ref[...] = grad_first


def outer_kernel(
    n_ew, n_ns, rb_ref, ra_ref, pix_ref, cell_ref,
    delta_ref, second_ref, first_ref, turn_ref, edge_ref, pre_ref,
    grid_ref, pick_ref, hidden_ref, route_ref, wab_ref, w2_ref, tokens_ref, mask_ref,
    keep_ref, give_ref, ext, wide, wins, pres,
):
    frames, slots, patches = pick_ref.shape
    chans = w2_ref.shape[0]
    features = tokens_ref.shape[1]
    cols = pre_ref.shape[3] // 2
    pcol = 2 * cols
    deep = 3 * GROUP
    ns = lax.axis_index("ns")
    ew = lax.axis_index("ew")
    even_ns = lax.rem(ns, 2) == 0
    even_ew = lax.rem(ew, 2) == 0
    ra, rb = ra_ref[...], rb_ref[...]
    north = jnp.where(even_ns, rb, ra)
    south = jnp.where(even_ns, ra, rb)
    span = frames * pcol
    tall = span // frames

    def far_sides(message):
        a, b = message[deep : deep + 8, :span].astype(F32), message[deep + 8 :, :span].astype(F32)
        return jnp.concatenate([jnp.where(even_ew, a, b), jnp.where(even_ew, b, a)], axis=0).astype(BF)

    pick_g, pick_p = halo_tables()
    line = frames * chans
    far = (far_sides(north), far_sides(south))
    for low in range(2):
        message = south if low else north
        halo_p = tn(far[low][:, (1 - low) * line : (2 - low) * line], pick_p).astype(BF)
        for f in range(frames):
            at = (f * 2 + low) * deep
            ext[pl.ds(at, deep), :pcol] = message[:deep, f * pcol : (f + 1) * pcol]
            if low:
                ext[pl.ds(at, deep), pcol:] = tn(far[low][:, f * tall : f * tall + 128], pick_g).astype(BF)[:deep]
            else:
                end = (f + 1) * tall
                ext[pl.ds(at, deep), pcol:] = tn(far[low][:, end - 128 : end], pick_g).astype(BF)[128 - deep :]
            at = (f * 2 + low) * chans
            wide[pl.ds(at, chans), :cols] = message[:, span + f * cols : span + (f + 1) * cols]
            wide[pl.ds(at, chans), cols:] = halo_p[f * chans : (f + 1) * chans]
    block = ext[...]
    for b in range(4):
        lanes = slice(b * 2 * cols, (b + 1) * 2 * cols)
        wins[:, lanes] = nn(block, pix_ref[:, lanes]).astype(BF)
    pres[...] = nn(wide[...], cell_ref[...])
    w2 = w2_ref[...]
    wab = wab_ref[...]
    drop = outside_columns(chans, cols, n_ew, ew)
    grad_second = second_ref[...]
    grad_first = first_ref[...]
    half_lane = iota((chans, cols), 1) < cols // 2
    grids = []
    for f in range(frames):
        cells = []
        for low in range(2):
            pair = []
            for k in range(2):
                inside = k == 1 - low
                beyond = wins[pl.ds((f * 2 + low) * deep, deep), :]
                window = [edge_ref[f, low], beyond] if low else [beyond, edge_ref[f, low]]
                window = jnp.concatenate(window, axis=0)[k * 2 * GROUP : (k * 2 + 4) * GROUP]
                taps = [window[:, b * 2 * cols : (b + 1) * 2 * cols] for b in range(4)]
                pre = pre_ref[f, low] if inside else pres[pl.ds((f * 2 + low) * chans, chans), :]
                gone = drop if inside else drop | (ns == (n_ns - 1 if low else 0))
                delta, hid = second_backward(taps, pre, w2, gone)
                pair.append(delta)
                if inside:
                    grad_second = grad_second + second_kernel_term(taps, hid)
            kept = delta_ref[pl.ds((f * 4 + 2 * low) * chans, 2 * chans), :]
            slab = jnp.concatenate([kept, *pair] if low else [*pair, kept], axis=0)
            cells.append(jnp.concatenate([slab[:, :cols], slab[:, cols:]], axis=0))
        both = jnp.concatenate(cells, axis=1)
        grad_first = grad_first + nt(both, grid_ref[f, 1])
        edge = nn(wab, both)
        inner = turn_ref[f]
        parts = []
        for even, odd in ((edge[:, :cols], inner[:, :cols]), (inner[:, cols:], edge[:, cols:])):
            here = jnp.where(half_lane, even[:chans], odd[chans:])
            there = jnp.where(half_lane, odd[:chans], even[chans:])
            parts.append(here + pltpu.roll(there, cols // 2, 1))
        grids.append(jnp.concatenate(parts, axis=1).astype(BF))
    none = jnp.zeros((chans, patches), BF)
    mask_sum = nt(hidden_ref[...], jnp.concatenate(grids, axis=1))
    chosen = [nt(pick_ref[f], jnp.concatenate([grids[f], none], axis=0)) for f in range(frames)]
    chosen = jnp.concatenate(chosen, axis=0)
    placed = jnp.where(even_ns, chosen, pltpu.roll(chosen, chans, 1)).astype(BF)
    chosen = chosen.astype(BF)
    routed = nn(route_ref[...], placed)
    hi = mask_sum.astype(BF).astype(F32)
    lo = mask_sum - hi
    line = iota(hi.shape, 0)
    mask_rows = jnp.where(line == 0, hi[0:1], jnp.where(line == 1, lo[0:1], 0.0)).astype(BF)
    line = iota((16, features), 0)
    mask_row = mask_ref[...].astype(F32).reshape(1, features)
    spread_row = jnp.where(line < 2, mask_row, 0.0).astype(BF)
    grad_proj = tn(chosen[:, :chans], tokens_ref[...]) + tn(mask_rows, spread_row)
    grad_proj = [grad_proj[:, k * 128 : (k + 1) * 128] for k in range(features // 128)]
    both = jnp.concatenate([hi[0:1], lo[0:1]], axis=1)
    mark = iota(grad_second.shape, 0) == MASK_ROW - SECOND_AT
    grad_second = jnp.where(mark, both, grad_second)
    halves = (grad_first, jnp.concatenate([*grad_proj, grad_second], axis=0))
    part = routed.shape[0] // 2

    def split(mine):
        keep_ref[: GRAD_ROWS // 2, :] = halves[mine]
        keep_ref[GRAD_ROWS // 2 :, :] = routed[mine * part : (mine + 1) * part]
        give_ref[: GRAD_ROWS // 2, :] = halves[1 - mine].astype(BF)
        give_ref[GRAD_ROWS // 2 :, :] = routed[(1 - mine) * part : (2 - mine) * part].astype(BF)

    @pl.when(even_ns)
    def _():
        split(0)

    @pl.when(jnp.logical_not(even_ns))
    def _():
        split(1)


def chip_kernel(rows_each, keep_ref, got_ref, out_ref):
    count = out_ref.shape[0]
    slot_rows = out_ref.shape[1] - rows_each
    grads = GRAD_ROWS // 2
    chips = (keep_ref.shape[0] - grads) // slot_rows
    total = (keep_ref[...] + got_ref[...].astype(F32)).astype(BF)
    full = min(count, grads // rows_each)
    for d in range(full):
        out_ref[d, :rows_each, :] = total[d * rows_each : (d + 1) * rows_each]
    if full < count:

        @pl.loop(full, count)
        def _(d):
            out_ref[d, :rows_each, :] = jnp.zeros((rows_each, total.shape[1]), BF)

    for z in range(chips):
        rows = total[grads + z * slot_rows : grads + (z + 1) * slot_rows]
        for e in range(count // chips):
            out_ref[e * chips + z, rows_each:, :] = rows


def sum_kernel(rows_each, got_ref, sum_ref):
    count = got_ref.shape[0]
    if count <= 64:
        total = got_ref[0, :rows_each, :].astype(F32)
        for d in range(1, count):
            total = total + got_ref[d, :rows_each, :].astype(F32)
    else:
        total = lax.fori_loop(
            0,
            count,
            lambda d, acc: acc + got_ref[d, :rows_each, :].astype(F32),
            jnp.zeros((rows_each, got_ref.shape[2]), F32),
        )
    share = total.astype(BF)
    if count <= 64:
        for d in range(count):
            sum_ref[d] = share
    else:

        @pl.loop(0, count)
        def _(d):
            sum_ref[d] = share


def owner_kernel(capacity, rows_each, arrived_ref, proj_ref, token_ref):
    chans = proj_ref.shape[0]
    slot_rows = arrived_ref.shape[1] - rows_each
    chips = token_ref.shape[0] // (2 * capacity)
    ew = lax.axis_index("ew")
    arrived = [arrived_ref[ew * chips + z, rows_each:, :].astype(F32) for z in range(chips)]
    arrived = jnp.concatenate(arrived, axis=0).astype(BF)
    shape = (token_ref.shape[0], chips * slot_rows)
    row, col = iota(shape, 0), iota(shape, 1)
    source = (row // (2 * capacity)) * slot_rows + lax.rem(row, capacity)
    picked = nn((source == col).astype(F32).astype(BF), arrived)
    second = lax.rem(iota(picked.shape, 0) // capacity, 2) == 1
    picked = jnp.where(second, pltpu.roll(picked, chans, 1), picked)[:, :chans].astype(BF)
    token_ref[...] = nn(picked, proj_ref[...]).astype(BF)


def finish_kernel(mine_ref, other_ref, proj_ref, proj_out, first_out, second_out, mask_out):
    chans, features = proj_ref.shape
    bands = second_out.shape[1]
    rows_each = mine_ref.shape[1]
    blocks = range(GRAD_ROWS // 2 // rows_each)
    mine = jnp.concatenate([mine_ref[d] for d in blocks], axis=0)
    other = jnp.concatenate([other_ref[d] for d in blocks], axis=0)
    even = lax.rem(lax.axis_index("ns"), 2) == 0
    total = [jnp.where(even, mine, other), jnp.where(even, other, mine)]
    total = jnp.concatenate(total, axis=0).astype(F32)
    for arrangement, taps in enumerate(((1, 2), (3, 0))):
        rows = total[arrangement * 4 * chans : (arrangement + 1) * 4 * chans]
        turned = pltpu.roll(rows, chans, 1)
        for a in range(4):
            first_out[a, taps[0]] = rows[a * chans : (a + 1) * chans, :chans]
            first_out[a, taps[1]] = turned[a * chans : (a + 1) * chans, :chans]
    for k in range(features // 128):
        at = PROJ_AT + k * chans
        proj_out[:, k * 128 : (k + 1) * 128] = total[at : at + chans]
    rows = total[SECOND_AT:]
    turned = pltpu.roll(rows, chans, 1)
    for b in range(2):
        for a in range(4):
            at = (b * 4 + a) * GROUP
            second_out[a, :, b, :] = rows[at : at + bands, :chans]
            second_out[a, :, b + 2, :] = turned[at : at + bands, :chans]
    at = MASK_ROW - SECOND_AT
    mask_sum = rows[at : at + 1, :chans] + turned[at : at + 1, :chans]
    hi = mask_sum.astype(BF).astype(F32)
    mid = (mask_sum - hi).astype(BF).astype(F32)
    lo = mask_sum - hi - mid
    line = iota((16, chans), 0)
    split = jnp.where(line == 0, hi, jnp.where(line == 1, mid, jnp.where(line == 2, lo, 0.0)))
    grad_mask = jnp.sum(nn(split.astype(BF), proj_ref[...]), axis=0, keepdims=True)
    mask_out[...] = grad_mask.reshape(features)


def swap(block, axis, offset):
    count = lax.axis_size(axis)
    pairs = [(i, ((i + offset) ^ 1) - offset) for i in range(count)]
    return lax.ppermute(block, axis, [(i, j) for i, j in pairs if 0 <= j < count])


def call(kernel, outs, args, scratch=(), flops=0, limit=8 << 20, specs=None):
    return pl.pallas_call(
        kernel,
        out_shape=outs,
        in_specs=specs or [VMEM] * len(args),
        out_specs=jax.tree.map(lambda _: VMEM, outs),
        scratch_shapes=list(scratch),
        compiler_params=pltpu.CompilerParams(vmem_limit_bytes=limit),
        cost_estimate=pl.CostEstimate(flops=flops, bytes_accessed=1 << 20, transcendentals=0),
    )(*args)


def per_device(
    n_ew, n_ns, tokens, vis_index, counts, owners, mask_token, proj_weight, up_first, up_second, saved_pre, cotangent
):
    frames, slots, features = tokens.shape[2:]
    _, chans, rows, cols = saved_pre.shape
    bands, prow, pcol = cotangent.shape[1:]
    patches = rows * cols // 4
    count = n_ew * n_ns
    capacity = 3 * frames * slots // (2 * n_ns)
    rows_each = -(-GRAD_ROWS // count)
    rows_each = -(-rows_each // 16) * 16
    slot_rows = -(-capacity // 8) * 8
    groups = [[e * n_ns + z * 2 + c for e in range(n_ew) for z in range(n_ns // 2)] for c in range(2)]
    slots_all = frames * slots
    shape = jax.ShapeDtypeStruct

    tall = prow * GROUP
    own_p, p_edges = call(
        cell_layout_kernel,
        (shape((frames * rows * chans, cols), BF), shape((8, frames * rows * chans), F32)),
        (saved_pre,),
        [pltpu.VMEM((frames * chans * rows, cols), F32)],
        flops=1 << 31,
    )
    own_g, own_edges = call(
        pixel_layout_kernel,
        (shape((frames * tall, pcol), BF), shape((8, frames * rows * chans), BF)),
        (cotangent, p_edges),
        [pltpu.VMEM((frames * tall * pcol // 128, 128), F32)],
        flops=1 << 31,
    )
    side_b = swap(own_edges, "ew", 1)
    side_a = swap(own_edges, "ew", 0)

    tile_tokens = tokens.reshape(slots_all, features)
    proj = proj_weight.T
    g_message = shape((3 * GROUP, frames * pcol), BF)
    p_message = shape((chans, frames * cols), BF)
    g_a, p_a, g_b, p_b, grid, picks, hidden, route, wab, w2, pixels, cells = call(
        functools.partial(local_kernel, capacity),
        (
            g_message,
            p_message,
            g_message,
            p_message,
            shape((frames, 2, 2 * chans, 2 * cols), BF),
            shape((frames, slots, patches), BF),
            shape((16, frames * patches), BF),
            shape((n_ns * slot_rows, slots_all), BF),
            shape((2 * chans, 8 * chans), BF),
            shape((chans, 16 * GROUP), BF),
            shape((pcol + 128, 4 * pcol), BF),
            shape((pcol, pcol), BF),
        ),
        (
            counts.reshape(1, frames),
            own_g,
            own_p,
            vis_index.reshape(frames, slots),
            owners.reshape(frames, 1, slots),
            tile_tokens,
            mask_token,
            proj,
            up_first,
            up_second.transpose(0, 2, 1, 3),
        ),
        flops=1 << 24,
        specs=[SMEM] + [VMEM] * 9,
    )
    message_shape = shape((3 * GROUP + 16, frames * (pcol + cols)), BF)
    send_a, send_b = call(
        message_kernel,
        (message_shape, message_shape),
        (side_b, side_a, g_a, p_a, g_b, p_b),
        flops=1 << 20,
    )
    got_b = swap(send_b, "ns", 1)
    got_a = swap(send_a, "ns", 0)

    delta_mid, second_mid, first_mid, turn_mid, edge_wins, edge_pre = call(
        functools.partial(inner_kernel, n_ew),
        (
            shape((frames * 4 * chans, 2 * cols), BF),
            shape((2 * 4 * GROUP, 2 * chans), F32),
            shape((8 * chans, 2 * chans), F32),
            shape((frames, 2 * chans, 2 * cols), F32),
            shape((frames, 2, 3 * GROUP, 8 * cols), BF),
            shape((frames, 2, chans, 2 * cols), F32),
        ),
        (side_b, side_a, own_g, own_p, pixels, cells, grid, wab, w2),
        [
            pltpu.VMEM((frames * tall, pcol + 128), BF),
            pltpu.VMEM((rows * frames * chans, 2 * cols), BF),
            pltpu.VMEM((frames * tall, 8 * cols), BF),
            pltpu.VMEM((rows * frames * chans, 2 * cols), F32),
        ],
        flops=1 << 27,
        limit=16 << 20,
    )
    beyond = frames * 2 * 3 * GROUP
    half_rows = GRAD_ROWS // 2 + n_ns // 2 * slot_rows
    keep, give = call(
        functools.partial(outer_kernel, n_ew, n_ns),
        (shape((half_rows, 2 * chans), F32), shape((half_rows, 2 * chans), BF)),
        (
            got_b, got_a, pixels, cells, delta_mid, second_mid, first_mid, turn_mid, edge_wins, edge_pre,
            grid, picks, hidden, route, wab, w2, tile_tokens, mask_token,
        ),
        [
            pltpu.VMEM((beyond, pcol + 128), BF),
            pltpu.VMEM((frames * 2 * chans, 2 * cols), BF),
            pltpu.VMEM((beyond, 8 * cols), BF),
            pltpu.VMEM((frames * 2 * chans, 2 * cols), F32),
        ],
        flops=1 << 27,
        limit=24 << 20,
    )

    def exchange(blocks):
        return lax.all_to_all(blocks, ("ew", "ns"), 0, 0, axis_index_groups=groups, tiled=True)

    outgoing = call(
        functools.partial(chip_kernel, rows_each),
        shape((count // 2, rows_each + slot_rows, 2 * chans), BF),
        (keep, swap(give, "ns", 0)),
        flops=1 << 20,
    )
    arrived = exchange(outgoing)
    shares = call(
        functools.partial(sum_kernel, rows_each),
        shape((count // 2, rows_each, 2 * chans), BF),
        (arrived,),
        flops=1 << 20,
    )
    summed = exchange(shares)[: GRAD_ROWS // 2 // rows_each]
    other = swap(summed, "ns", 0)
    token_grad = call(
        functools.partial(owner_kernel, capacity, rows_each),
        shape((n_ns * capacity, features), BF),
        (arrived, proj),
        flops=1 << 27,
    )
    grad_proj, grad_first, grad_second, grad_mask = call(
        finish_kernel,
        (
            shape((chans, features), F32),
            shape((4, 4, chans, chans), F32),
            shape((4, bands, 4, chans), F32),
            shape((features,), F32),
        ),
        (summed, other, proj),
        flops=1 << 20,
    )
    return (token_grad[None, None], grad_proj.T, grad_first, grad_second.transpose(0, 2, 1, 3), grad_mask)


def solution(mesh):
    return jax.shard_map(
        functools.partial(per_device, mesh.shape["ew"], mesh.shape["ns"]),
        mesh=mesh,
        in_specs=(
            P("ns", "ew", None, None, None),
            P("ns", "ew", None, None),
            P("ns", "ew", None),
            P("ns", "ew", None, None, None),
            P(),
            P(),
            P(),
            P(),
            P(None, None, "ns", "ew"),
            P(None, None, "ns", "ew"),
        ),
        out_specs=(P("ns", "ew", None, None), P(), P(), P(), P()),
        check_vma=False,
    )
```

```python
import functools

import jax
import jax.numpy as jnp
import numpy as np
from jax import lax
from jax.experimental import pallas as pl
from jax.experimental.pallas import tpu as pltpu
from jax.sharding import PartitionSpec as P

BF = jnp.bfloat16
F32 = jnp.float32
VMEM = pl.BlockSpec(memory_space=pltpu.VMEM)
SMEM = pl.BlockSpec(memory_space=pltpu.SMEM)
GROUP = 16
GRAD_ROWS = 1024
PROJ_AT = 512
SECOND_AT = 896
MASK_ROW = SECOND_AT + 12


def nn(a, b):
    return lax.dot_general(a, b, (((1,), (0,)), ((), ())), preferred_element_type=F32)


def nt(a, b):
    return lax.dot_general(a, b, (((1,), (1,)), ((), ())), preferred_element_type=F32)


def tn(a, b):
    return lax.dot_general(a, b, (((0,), (0,)), ((), ())), preferred_element_type=F32)


def iota(shape, dim):
    return lax.broadcasted_iota(jnp.int32, shape, dim)


def hidden_columns(cols, lanes):
    lane = lax.rem(lanes, cols)
    right = lane >= cols // 2
    own = 2 * jnp.where(right, lane - cols // 2, lane) + jnp.where(right, 1, 0)
    shifted = own + jnp.where(right, -2, 2)
    return jnp.where(lax.rem(lanes // cols, 2) == 0, own, shifted)


def table_kernel(pix_ref, cell_ref, pick_ref):
    cols = cell_ref.shape[0] // 2
    column_tables(cols, pix_ref, cell_ref)
    pick_g, pick_p = edge_tables(2 * cols, cols)
    pick_ref[:, : 2 * cols] = pick_g
    pick_ref[:, 2 * cols :] = pick_p


def column_tables(cols, pix_ref, cell_ref):
    fine = 2 * cols
    lanes = iota((1, fine), 1)
    hidden = hidden_columns(cols, lanes)
    for tap in range(4):
        pixel = 2 * hidden + tap - 1
        pixel = jnp.where(pixel < 0, fine + 6 + pixel, pixel)
        table = iota((fine + 128, fine), 0) == pixel
        pix_ref[:, tap * fine : (tap + 1) * fine] = table.astype(F32).astype(BF)
    cell = jnp.where(hidden < 0, cols + 1, hidden)
    cell_ref[...] = (iota((fine, fine), 0) == cell).astype(F32).astype(BF)


def spread(ref, wide, group):
    frames, real, rows, cols = ref.shape
    for f in range(frames):
        for o in range(group):
            value = ref[f, o].astype(F32) if o < real else jnp.zeros((rows, cols), F32)
            for h in range(cols // 128):
                wide[pl.ds(((h * frames + f) * group + o) * rows, rows), :] = value[:, h * 128 : (h + 1) * 128]


def gathered(wide, h, frames, group, rows, f, r):
    return wide[pl.ds((h * frames + f) * group * rows + r, group, stride=rows), :].astype(BF)


def edge_tables(pcol, cols):
    row, col = iota((16, pcol), 0), iota((16, pcol), 1)
    pick_g = ((row < 3) & (col == row)) | ((row >= 3) & (row < 6) & (col == row + pcol - 6))
    row, col = iota((16, cols), 0), iota((16, cols), 1)
    pick_p = ((row == 6) & (col == 0)) | ((row == 7) & (col == cols - 1))
    return pick_g.astype(F32).astype(BF), pick_p.astype(F32).astype(BF)


def cell_layout_kernel(pick_ref, pre_ref, p_ref, edge_ref, pre_wide):
    frames, chans, rows, cols = pre_ref.shape
    spread(pre_ref, pre_wide, chans)
    for r in range(rows):
        for f in range(frames):
            p_ref[pl.ds((r * frames + f) * chans, chans), :] = gathered(pre_wide, 0, frames, chans, rows, f, r)
    edges = nt(pick_ref[:, 2 * cols :], p_ref[...])[:8]
    line = frames * chans
    last = (rows - 1) * line
    edge_ref[...] = jnp.concatenate([edges[:, :line], edges[:, last:], edges[:, line:last]], axis=1)


def pixel_layout_kernel(pick_ref, cot_ref, edge_ref, g_ref, own_ref, cot_wide):
    frames, bands, prow, pcol = cot_ref.shape
    spread(cot_ref, cot_wide, GROUP)
    for f in range(frames):
        for y in range(prow):
            for h in range(pcol // 128):
                g_ref[pl.ds((f * prow + y) * GROUP, GROUP), h * 128 : (h + 1) * 128] = gathered(
                    cot_wide, h, frames, GROUP, prow, f, y
                )
    edges = nt(pick_ref[:, :pcol], g_ref[...])[:8]
    width = edges.shape[1]
    below = edge_ref[...]
    own_ref[...] = jnp.concatenate([edges + below[:, :width], below[:, width:]], axis=1).astype(BF)


def row_messages(g_ref, p_ref, ga_ref, pa_ref, gb_ref, pb_ref):
    deep, pcol = ga_ref.shape[0], g_ref.shape[1]
    chans, cols = pa_ref.shape[0], p_ref.shape[1]
    frames = pa_ref.shape[1] // cols
    tall = g_ref.shape[0] // frames
    high = p_ref.shape[0]

    def message(g_out, p_out, top):
        for f in range(frames):
            at = f * tall if top else (f + 1) * tall - deep
            g_out[:, f * pcol : (f + 1) * pcol] = g_ref[pl.ds(at, deep), :]
            at = f * chans if top else high - (frames - f) * chans
            p_out[:, f * cols : (f + 1) * cols] = p_ref[pl.ds(at, chans), :]

    even = lax.rem(lax.axis_index("ns"), 2) == 0

    @pl.when(even)
    def _():
        message(ga_ref, pa_ref, False)
        message(gb_ref, pb_ref, True)

    @pl.when(jnp.logical_not(even))
    def _():
        message(ga_ref, pa_ref, True)
        message(gb_ref, pb_ref, False)


def local_kernel(
    capacity, counts_ref, g_ref, p_ref, vis_ref, owners_ref, tokens_ref, mask_ref, proj_ref, first_ref, second_ref,
    ga_ref, pa_ref, gb_ref, pb_ref, grid_ref, pick_ref, hidden_ref, route_ref, wab_ref, w2_ref,
):
    row_messages(g_ref, p_ref, ga_ref, pa_ref, gb_ref, pb_ref)
    slots_all = tokens_ref.shape[0]
    frames, slots, patches = pick_ref.shape
    chans = proj_ref.shape[0]
    bands = second_ref.shape[1]
    slot_rows = -(-capacity // 8) * 8
    owners = route_ref.shape[0] // slot_rows
    eye = (iota((chans, chans), 0) == iota((chans, chans), 1)).astype(BF)
    pad = jnp.zeros((GROUP - bands, chans), F32)
    taps = []
    for b in range(4):
        for a in range(4):
            here = iota((bands, 4, chans), 1) == b
            tap = jnp.sum(jnp.where(here, second_ref[a].astype(F32), 0.0), axis=1)
            taps.append(jnp.concatenate([tap, pad], axis=0).astype(BF))
    w2_ref[...] = nt(eye, jnp.concatenate(taps, axis=0)).astype(BF)
    left = (iota((2 * chans, chans), 0) == iota((2 * chans, chans), 1)).astype(BF)
    right = (iota((2 * chans, chans), 0) == iota((2 * chans, chans), 1) + chans).astype(BF)
    for arrangement, (lo, hi) in enumerate(((1, 2), (3, 0))):
        taps_lo = jnp.concatenate([first_ref[a, lo] for a in range(4)], axis=0)
        taps_hi = jnp.concatenate([first_ref[a, hi] for a in range(4)], axis=0)
        wab_ref[:, arrangement * 4 * chans : (arrangement + 1) * 4 * chans] = (
            nt(left, taps_lo) + nt(right, taps_hi)
        ).astype(BF)
    vis = jnp.concatenate([vis_ref[f : f + 1, :] for f in range(frames)], axis=1)
    owner = jnp.concatenate([owners_ref[f] for f in range(frames)], axis=1)
    slot = iota((1, slots_all), 1)
    live = jnp.zeros((1, slots_all), jnp.int32)
    for f in range(frames):
        inside = (slot >= f * slots) & (slot < f * slots + counts_ref[0, f])
        live = jnp.where(inside, 1, live)
    wanted = jnp.where(live > 0, vis, patches)
    square = (slots_all, slots_all)
    column = jnp.sum(
        jnp.where(iota(square, 0) == iota(square, 1), wanted.astype(F32), 0.0), axis=1, keepdims=True
    ).astype(jnp.int32)
    token_proj = nt(tokens_ref[...], proj_ref[...]).astype(BF)
    features = mask_ref.shape[0]
    mask_row = mask_ref[...].astype(F32).reshape(1, features)
    mask_proj = nt(jnp.broadcast_to(mask_row, (16, features)).astype(BF), proj_ref[...]).astype(BF)
    row0 = iota((16, patches), 0) == 0
    lane = iota((chans, 2 * chans), 1)
    for f in range(frames):
        hits = iota((slots, patches), 1) == column[f * slots : (f + 1) * slots]
        picks = hits.astype(F32)
        pick_ref[f] = picks.astype(BF)
        unseen = jnp.where(row0, 1.0 - jnp.sum(picks, axis=0, keepdims=True), 0.0).astype(BF)
        hidden_ref[:, f * patches : (f + 1) * patches] = unseen
        grid = tn(token_proj[f * slots : (f + 1) * slots], picks.astype(BF)) + tn(mask_proj, unseen)
        zero = jnp.zeros((chans, 2 * chans), F32)
        for line, (group, half_at) in enumerate(((1, 0), (0, 0), (0, 1), (1, 1))):
            pair = line // 2 * 2 * chans
            straight = grid[:, pair : pair + 2 * chans]
            turned = pltpu.roll(straight, chans, 1)
            to_left, to_right = (straight, turned) if line % 2 == 0 else (turned, straight)
            at = half_at * 2 * chans
            grid_ref[f, group, :chans, at : at + 2 * chans] = jnp.where(lane < chans, to_left, zero).astype(BF)
            grid_ref[f, group, chans:, at : at + 2 * chans] = jnp.where(lane < chans, zero, to_right).astype(BF)
    own_rows = -(-owners // 16) * 16
    hit = (iota((own_rows, slots_all), 0) == jnp.where(live > 0, owner, -1)).astype(F32)
    before = (iota(square, 0) < iota(square, 1)).astype(BF)
    earlier = nn(hit.astype(BF), before)
    place = jnp.sum(earlier * hit, axis=0, keepdims=True).astype(jnp.int32)
    block = lax.rem(owner, 2) * (owners // 2) + owner // 2
    target = jnp.where(live > 0, block * slot_rows + place, -1)
    route_ref[...] = (iota((owners * slot_rows, slots_all), 0) == target).astype(F32).astype(BF)


def side_columns(ea_ref, eb_ref, even_ew):
    ea, eb = ea_ref[...].astype(F32), eb_ref[...].astype(F32)
    return jnp.concatenate([jnp.where(even_ew, ea, eb), jnp.where(even_ew, eb, ea)], axis=0).astype(BF)


def halo_tables():
    row, col = iota((16, 128), 0), iota((16, 128), 1)
    pick_g = ((row < 3) & (col == row)) | ((row >= 11) & (row < 14) & (col == row - 8))
    pick_p = ((row == 6) & (col == 0)) | ((row == 15) & (col == 1))
    return pick_g.astype(F32).astype(BF), pick_p.astype(F32).astype(BF)


def second_backward(taps, pre, w2, drop):
    grad_hidden = nn(w2, jnp.concatenate(taps, axis=0))
    s = 0.5 + 0.5 * jnp.tanh(0.851 * pre)
    delta = grad_hidden * (s + 1.702 * pre * s * (1.0 - s))
    cols = pre.shape[1] // 2
    return jnp.where(drop, 0.0, delta).astype(BF), (pre[:, :cols] * s[:, :cols]).astype(BF)


def second_kernel_term(taps, hid):
    cols = hid.shape[1]
    zero = jnp.zeros_like(hid)
    lhs = jnp.concatenate(
        [
            jnp.concatenate([taps[0][:, :cols], taps[2][:, :cols]], axis=1),
            jnp.concatenate([taps[1][:, :cols], taps[3][:, :cols]], axis=1),
        ],
        axis=0,
    )
    rhs = jnp.concatenate(
        [jnp.concatenate([hid, zero], axis=1), jnp.concatenate([zero, hid], axis=1)], axis=0
    )
    return nt(lhs, rhs)


def outside_columns(chans, cols, n_ew, ew):
    lane = iota((chans, 2 * cols), 1)
    return ((lane == cols + cols // 2 - 1) & (ew == n_ew - 1)) | ((lane == cols + cols // 2) & (ew == 0))


def window_taps(wins, at, cols):
    return [wins[pl.ds(at, 4 * GROUP), b * 2 * cols : (b + 1) * 2 * cols] for b in range(4)]


def message_kernel(sb_ref, sa_ref, ga_ref, pa_ref, gb_ref, pb_ref, a_ref, b_ref):
    deep, span = ga_ref.shape
    corners = jnp.concatenate([sa_ref[:, :span].astype(F32), sb_ref[:, :span].astype(F32)], axis=0).astype(BF)
    for out, g, p in ((a_ref, ga_ref, pa_ref), (b_ref, gb_ref, pb_ref)):
        out[:deep, :span] = g[...]
        out[deep:, :span] = corners
        out[:, span:] = p[...]


def inner_kernel(
    n_ew, eb_ref, ea_ref, g_ref, p_ref, pix_ref, cell_ref, grid_ref, wab_ref, w2_ref,
    delta_ref, second_ref, first_ref, turn_ref, edge_ref, pre_ref, ext, wide, wins, pres,
):
    frames = grid_ref.shape[0]
    chans = w2_ref.shape[0]
    pcol, cols = g_ref.shape[1], p_ref.shape[1]
    tall = g_ref.shape[0] // frames
    rows = p_ref.shape[0] // (frames * chans)
    ew = lax.axis_index("ew")
    sides = side_columns(ea_ref, eb_ref, lax.rem(ew, 2) == 0)
    pick_g, pick_p = halo_tables()
    line = frames * chans
    ext[:, :pcol] = g_ref[...]
    ext[:, pcol:] = tn(sides[:, : frames * tall], pick_g).astype(BF)
    wide[:, :cols] = p_ref[...]
    halo = tn(sides, pick_p).astype(BF)
    wide[pl.ds(0, line), cols:] = halo[:line]
    wide[pl.ds((rows - 1) * line, line), cols:] = halo[line : 2 * line]
    wide[pl.ds(line, (rows - 2) * line), cols:] = halo[2 * line :]
    deep = 3 * GROUP
    for f in range(frames):
        block = ext[pl.ds(f * tall, tall), :]
        for b in range(4):
            lanes = slice(b * 2 * cols, (b + 1) * 2 * cols)
            wins[pl.ds(f * tall, tall), lanes] = nn(block, pix_ref[:, lanes]).astype(BF)
        edge_ref[f, 0] = wins[pl.ds(f * tall, deep), :]
        edge_ref[f, 1] = wins[pl.ds((f + 1) * tall - deep, deep), :]
    pres[...] = nn(wide[...], cell_ref[...])
    for f in range(frames):
        pre_ref[f, 0] = pres[pl.ds(f * chans, chans), :]
        pre_ref[f, 1] = pres[pl.ds((rows - 1) * line + f * chans, chans), :]
    w2 = w2_ref[...]
    wab = wab_ref[...]
    drop = outside_columns(chans, cols, n_ew, ew)
    grad_second = grad_first = None
    for f in range(frames):
        deltas = []
        for i in range(1, rows - 1):
            taps = window_taps(wins, f * tall + (2 * i - 1) * GROUP, cols)
            pre = pres[pl.ds(i * line + f * chans, chans), :]
            delta, hid = second_backward(taps, pre, w2, drop)
            deltas.append(delta)
            term = second_kernel_term(taps, hid)
            grad_second = term if grad_second is None else grad_second + term
        count = rows - 2
        for k, i in enumerate((0, 1, count - 2, count - 1)):
            delta_ref[pl.ds((f * 4 + k) * chans, chans), :] = deltas[i]
        cells = []
        for i in (0, 2):
            slab = jnp.concatenate(deltas[i : i + 4], axis=0)
            cells.append(jnp.concatenate([slab[:, :cols], slab[:, cols:]], axis=0))
        both = jnp.concatenate(cells, axis=1)
        term = nt(both, grid_ref[f, 0])
        grad_first = term if grad_first is None else grad_first + term
        turn_ref[f] = nn(wab, both)
    second_ref[...] = grad_second
    first_ref[...] = grad_first


def outer_kernel(
    n_ew, n_ns, rb_ref, ra_ref, pix_ref, cell_ref,
    delta_ref, second_ref, first_ref, turn_ref, edge_ref, pre_ref,
    grid_ref, pick_ref, hidden_ref, route_ref, wab_ref, w2_ref, tokens_ref, mask_ref,
    keep_ref, give_ref, ext, wide, wins, pres,
):
    frames, slots, patches = pick_ref.shape
    chans = w2_ref.shape[0]
    features = tokens_ref.shape[1]
    cols = pre_ref.shape[3] // 2
    pcol = 2 * cols
    deep = 3 * GROUP
    ns = lax.axis_index("ns")
    ew = lax.axis_index("ew")
    even_ns = lax.rem(ns, 2) == 0
    even_ew = lax.rem(ew, 2) == 0
    ra, rb = ra_ref[...], rb_ref[...]
    north = jnp.where(even_ns, rb, ra)
    south = jnp.where(even_ns, ra, rb)
    span = frames * pcol
    tall = span // frames

    def far_sides(message):
        a, b = message[deep : deep + 8, :span].astype(F32), message[deep + 8 :, :span].astype(F32)
        return jnp.concatenate([jnp.where(even_ew, a, b), jnp.where(even_ew, b, a)], axis=0).astype(BF)

    pick_g, pick_p = halo_tables()
    line = frames * chans
    far = (far_sides(north), far_sides(south))
    for low in range(2):
        message = south if low else north
        halo_p = tn(far[low][:, (1 - low) * line : (2 - low) * line], pick_p).astype(BF)
        for f in range(frames):
            at = (f * 2 + low) * deep
            ext[pl.ds(at, deep), :pcol] = message[:deep, f * pcol : (f + 1) * pcol]
            if low:
                ext[pl.ds(at, deep), pcol:] = tn(far[low][:, f * tall : f * tall + 128], pick_g).astype(BF)[:deep]
            else:
                end = (f + 1) * tall
                ext[pl.ds(at, deep), pcol:] = tn(far[low][:, end - 128 : end], pick_g).astype(BF)[128 - deep :]
            at = (f * 2 + low) * chans
            wide[pl.ds(at, chans), :cols] = message[:, span + f * cols : span + (f + 1) * cols]
            wide[pl.ds(at, chans), cols:] = halo_p[f * chans : (f + 1) * chans]
    block = ext[...]
    for b in range(4):
        lanes = slice(b * 2 * cols, (b + 1) * 2 * cols)
        wins[:, lanes] = nn(block, pix_ref[:, lanes]).astype(BF)
    pres[...] = nn(wide[...], cell_ref[...])
    w2 = w2_ref[...]
    wab = wab_ref[...]
    drop = outside_columns(chans, cols, n_ew, ew)
    grad_second = second_ref[...]
    grad_first = first_ref[...]
    half_lane = iota((chans, cols), 1) < cols // 2
    grids = []
    for f in range(frames):
        cells = []
        for low in range(2):
            pair = []
            for k in range(2):
                inside = k == 1 - low
                beyond = wins[pl.ds((f * 2 + low) * deep, deep), :]
                window = [edge_ref[f, low], beyond] if low else [beyond, edge_ref[f, low]]
                window = jnp.concatenate(window, axis=0)[k * 2 * GROUP : (k * 2 + 4) * GROUP]
                taps = [window[:, b * 2 * cols : (b + 1) * 2 * cols] for b in range(4)]
                pre = pre_ref[f, low] if inside else pres[pl.ds((f * 2 + low) * chans, chans), :]
                gone = drop if inside else drop | (ns == (n_ns - 1 if low else 0))
                delta, hid = second_backward(taps, pre, w2, gone)
                pair.append(delta)
                if inside:
                    grad_second = grad_second + second_kernel_term(taps, hid)
            kept = delta_ref[pl.ds((f * 4 + 2 * low) * chans, 2 * chans), :]
            slab = jnp.concatenate([kept, *pair] if low else [*pair, kept], axis=0)
            cells.append(jnp.concatenate([slab[:, :cols], slab[:, cols:]], axis=0))
        both = jnp.concatenate(cells, axis=1)
        grad_first = grad_first + nt(both, grid_ref[f, 1])
        edge = nn(wab, both)
        inner = turn_ref[f]
        parts = []
        for even, odd in ((edge[:, :cols], inner[:, :cols]), (inner[:, cols:], edge[:, cols:])):
            here = jnp.where(half_lane, even[:chans], odd[chans:])
            there = jnp.where(half_lane, odd[:chans], even[chans:])
            parts.append(here + pltpu.roll(there, cols // 2, 1))
        grids.append(jnp.concatenate(parts, axis=1).astype(BF))
    none = jnp.zeros((chans, patches), BF)
    mask_sum = nt(hidden_ref[...], jnp.concatenate(grids, axis=1))
    chosen = [nt(pick_ref[f], jnp.concatenate([grids[f], none], axis=0)) for f in range(frames)]
    chosen = jnp.concatenate(chosen, axis=0)
    placed = jnp.where(even_ns, chosen, pltpu.roll(chosen, chans, 1)).astype(BF)
    chosen = chosen.astype(BF)
    routed = nn(route_ref[...], placed)
    hi = mask_sum.astype(BF).astype(F32)
    lo = mask_sum - hi
    line = iota(hi.shape, 0)
    mask_rows = jnp.where(line == 0, hi[0:1], jnp.where(line == 1, lo[0:1], 0.0)).astype(BF)
    line = iota((16, features), 0)
    mask_row = mask_ref[...].astype(F32).reshape(1, features)
    spread_row = jnp.where(line < 2, mask_row, 0.0).astype(BF)
    grad_proj = tn(chosen[:, :chans], tokens_ref[...]) + tn(mask_rows, spread_row)
    grad_proj = [grad_proj[:, k * 128 : (k + 1) * 128] for k in range(features // 128)]
    both = jnp.concatenate([hi[0:1], lo[0:1]], axis=1)
    mark = iota(grad_second.shape, 0) == MASK_ROW - SECOND_AT
    grad_second = jnp.where(mark, both, grad_second)
    halves = (grad_first, jnp.concatenate([*grad_proj, grad_second], axis=0))
    part = routed.shape[0] // 2

    def split(mine):
        keep_ref[: GRAD_ROWS // 2, :] = halves[mine]
        keep_ref[GRAD_ROWS // 2 :, :] = routed[mine * part : (mine + 1) * part]
        give_ref[: GRAD_ROWS // 2, :] = halves[1 - mine].astype(BF)
        give_ref[GRAD_ROWS // 2 :, :] = routed[(1 - mine) * part : (2 - mine) * part].astype(BF)

    @pl.when(even_ns)
    def _():
        split(0)

    @pl.when(jnp.logical_not(even_ns))
    def _():
        split(1)


def chip_kernel(rows_each, keep_ref, got_ref, out_ref):
    count = out_ref.shape[0]
    slot_rows = out_ref.shape[1] - rows_each
    grads = GRAD_ROWS // 2
    chips = (keep_ref.shape[0] - grads) // slot_rows
    total = (keep_ref[...] + got_ref[...].astype(F32)).astype(BF)
    full = min(count, grads // rows_each)
    for d in range(full):
        out_ref[d, :rows_each, :] = total[d * rows_each : (d + 1) * rows_each]
    if full < count:

        @pl.loop(full, count)
        def _(d):
            out_ref[d, :rows_each, :] = jnp.zeros((rows_each, total.shape[1]), BF)

    for z in range(chips):
        rows = total[grads + z * slot_rows : grads + (z + 1) * slot_rows]
        for e in range(count // chips):
            out_ref[e * chips + z, rows_each:, :] = rows


def sum_kernel(rows_each, got_ref, sum_ref):
    count = got_ref.shape[0]
    if count <= 64:
        total = got_ref[0, :rows_each, :].astype(F32)
        for d in range(1, count):
            total = total + got_ref[d, :rows_each, :].astype(F32)
    else:
        total = lax.fori_loop(
            0,
            count,
            lambda d, acc: acc + got_ref[d, :rows_each, :].astype(F32),
            jnp.zeros((rows_each, got_ref.shape[2]), F32),
        )
    share = total.astype(BF)
    if count <= 64:
        for d in range(count):
            sum_ref[d] = share
    else:

        @pl.loop(0, count)
        def _(d):
            sum_ref[d] = share


def owner_kernel(capacity, rows_each, arrived_ref, proj_ref, token_ref):
    chans = proj_ref.shape[0]
    slot_rows = arrived_ref.shape[1] - rows_each
    chips = token_ref.shape[0] // (2 * capacity)
    ew = lax.axis_index("ew")
    arrived = [arrived_ref[ew * chips + z, rows_each:, :].astype(F32) for z in range(chips)]
    arrived = jnp.concatenate(arrived, axis=0).astype(BF)
    shape = (token_ref.shape[0], chips * slot_rows)
    row, col = iota(shape, 0), iota(shape, 1)
    source = (row // (2 * capacity)) * slot_rows + lax.rem(row, capacity)
    picked = nn((source == col).astype(F32).astype(BF), arrived)
    second = lax.rem(iota(picked.shape, 0) // capacity, 2) == 1
    picked = jnp.where(second, pltpu.roll(picked, chans, 1), picked)[:, :chans].astype(BF)
    token_ref[...] = nn(picked, proj_ref[...]).astype(BF)


def finish_kernel(mine_ref, other_ref, proj_ref, proj_out, first_out, second_out, mask_out):
    chans, features = proj_ref.shape
    bands = second_out.shape[1]
    rows_each = mine_ref.shape[1]
    blocks = range(GRAD_ROWS // 2 // rows_each)
    mine = jnp.concatenate([mine_ref[d] for d in blocks], axis=0)
    other = jnp.concatenate([other_ref[d] for d in blocks], axis=0)
    even = lax.rem(lax.axis_index("ns"), 2) == 0
    total = [jnp.where(even, mine, other), jnp.where(even, other, mine)]
    total = jnp.concatenate(total, axis=0).astype(F32)
    for arrangement, taps in enumerate(((1, 2), (3, 0))):
        rows = total[arrangement * 4 * chans : (arrangement + 1) * 4 * chans]
        turned = pltpu.roll(rows, chans, 1)
        for a in range(4):
            first_out[a, taps[0]] = rows[a * chans : (a + 1) * chans, :chans]
            first_out[a, taps[1]] = turned[a * chans : (a + 1) * chans, :chans]
    for k in range(features // 128):
        at = PROJ_AT + k * chans
        proj_out[:, k * 128 : (k + 1) * 128] = total[at : at + chans]
    rows = total[SECOND_AT:]
    turned = pltpu.roll(rows, chans, 1)
    for b in range(2):
        for a in range(4):
            at = (b * 4 + a) * GROUP
            second_out[a, :, b, :] = rows[at : at + bands, :chans]
            second_out[a, :, b + 2, :] = turned[at : at + bands, :chans]
    at = MASK_ROW - SECOND_AT
    mask_sum = rows[at : at + 1, :chans] + turned[at : at + 1, :chans]
    hi = mask_sum.astype(BF).astype(F32)
    mid = (mask_sum - hi).astype(BF).astype(F32)
    lo = mask_sum - hi - mid
    line = iota((16, chans), 0)
    split = jnp.where(line == 0, hi, jnp.where(line == 1, mid, jnp.where(line == 2, lo, 0.0)))
    grad_mask = jnp.sum(nn(split.astype(BF), proj_ref[...]), axis=0, keepdims=True)
    mask_out[...] = grad_mask.reshape(features)


def swap(block, axis, offset):
    count = lax.axis_size(axis)
    pairs = [(i, ((i + offset) ^ 1) - offset) for i in range(count)]
    return lax.ppermute(block, axis, [(i, j) for i, j in pairs if 0 <= j < count])


def call(kernel, outs, args, scratch=(), flops=0, limit=8 << 20, specs=None):
    return pl.pallas_call(
        kernel,
        out_shape=outs,
        in_specs=specs or [VMEM] * len(args),
        out_specs=jax.tree.map(lambda _: VMEM, outs),
        scratch_shapes=list(scratch),
        compiler_params=pltpu.CompilerParams(vmem_limit_bytes=limit),
        cost_estimate=pl.CostEstimate(flops=flops, bytes_accessed=1 << 10, transcendentals=0),
    )(*args)


def per_device(
    n_ew, n_ns, tokens, vis_index, counts, owners, mask_token, proj_weight, up_first, up_second, saved_pre, cotangent
):
    frames, slots, features = tokens.shape[2:]
    _, chans, rows, cols = saved_pre.shape
    bands, prow, pcol = cotangent.shape[1:]
    patches = rows * cols // 4
    count = n_ew * n_ns
    capacity = 3 * frames * slots // (2 * n_ns)
    rows_each = -(-GRAD_ROWS // count)
    rows_each = -(-rows_each // 16) * 16
    slot_rows = -(-capacity // 8) * 8
    groups = [[e * n_ns + z * 2 + c for e in range(n_ew) for z in range(n_ns // 2)] for c in range(2)]
    slots_all = frames * slots
    shape = jax.ShapeDtypeStruct

    tall = prow * GROUP
    pixels, cells, edge_picks = call(
        table_kernel,
        (shape((pcol + 128, 4 * pcol), BF), shape((pcol, pcol), BF), shape((16, pcol + cols), BF)),
        (),
        flops=1 << 33,
    )
    own_p, p_edges = call(
        cell_layout_kernel,
        (shape((frames * rows * chans, cols), BF), shape((8, frames * rows * chans), F32)),
        (edge_picks, saved_pre),
        [pltpu.VMEM((frames * chans * rows, cols), F32)],
        flops=1 << 10,
    )
    own_g, own_edges = call(
        pixel_layout_kernel,
        (shape((frames * tall, pcol), BF), shape((8, frames * rows * chans), BF)),
        (edge_picks, cotangent, p_edges),
        [pltpu.VMEM((frames * tall * pcol // 128, 128), F32)],
        flops=1 << 33,
    )
    side_b = swap(own_edges, "ew", 1)
    side_a = swap(own_edges, "ew", 0)

    tile_tokens = tokens.reshape(slots_all, features)
    proj = proj_weight.T
    g_message = shape((3 * GROUP, frames * pcol), BF)
    p_message = shape((chans, frames * cols), BF)
    g_a, p_a, g_b, p_b, grid, picks, hidden, route, wab, w2 = call(
        functools.partial(local_kernel, capacity),
        (
            g_message,
            p_message,
            g_message,
            p_message,
            shape((frames, 2, 2 * chans, 2 * cols), BF),
            shape((frames, slots, patches), BF),
            shape((16, frames * patches), BF),
            shape((n_ns * slot_rows, slots_all), BF),
            shape((2 * chans, 8 * chans), BF),
            shape((chans, 16 * GROUP), BF),
        ),
        (
            counts.reshape(1, frames),
            own_g,
            own_p,
            vis_index.reshape(frames, slots),
            owners.reshape(frames, 1, slots),
            tile_tokens,
            mask_token,
            proj,
            up_first,
            up_second.transpose(0, 2, 1, 3),
        ),
        flops=1 << 24,
        specs=[SMEM] + [VMEM] * 9,
    )
    message_shape = shape((3 * GROUP + 16, frames * (pcol + cols)), BF)
    send_a, send_b = call(
        message_kernel,
        (message_shape, message_shape),
        (side_b, side_a, g_a, p_a, g_b, p_b),
        flops=1 << 20,
    )
    got_b = swap(send_b, "ns", 1)
    got_a = swap(send_a, "ns", 0)

    delta_mid, second_mid, first_mid, turn_mid, edge_wins, edge_pre = call(
        functools.partial(inner_kernel, n_ew),
        (
            shape((frames * 4 * chans, 2 * cols), BF),
            shape((2 * 4 * GROUP, 2 * chans), F32),
            shape((8 * chans, 2 * chans), F32),
            shape((frames, 2 * chans, 2 * cols), F32),
            shape((frames, 2, 3 * GROUP, 8 * cols), BF),
            shape((frames, 2, chans, 2 * cols), F32),
        ),
        (side_b, side_a, own_g, own_p, pixels, cells, grid, wab, w2),
        [
            pltpu.VMEM((frames * tall, pcol + 128), BF),
            pltpu.VMEM((rows * frames * chans, 2 * cols), BF),
            pltpu.VMEM((frames * tall, 8 * cols), BF),
            pltpu.VMEM((rows * frames * chans, 2 * cols), F32),
        ],
        flops=1 << 27,
        limit=16 << 20,
    )
    beyond = frames * 2 * 3 * GROUP
    half_rows = GRAD_ROWS // 2 + n_ns // 2 * slot_rows
    keep, give = call(
        functools.partial(outer_kernel, n_ew, n_ns),
        (shape((half_rows, 2 * chans), F32), shape((half_rows, 2 * chans), BF)),
        (
            got_b, got_a, pixels, cells, delta_mid, second_mid, first_mid, turn_mid, edge_wins, edge_pre,
            grid, picks, hidden, route, wab, w2, tile_tokens, mask_token,
        ),
        [
            pltpu.VMEM((beyond, pcol + 128), BF),
            pltpu.VMEM((frames * 2 * chans, 2 * cols), BF),
            pltpu.VMEM((beyond, 8 * cols), BF),
            pltpu.VMEM((frames * 2 * chans, 2 * cols), F32),
        ],
        flops=1 << 27,
        limit=24 << 20,
    )

    def exchange(blocks):
        return lax.all_to_all(blocks, ("ew", "ns"), 0, 0, axis_index_groups=groups, tiled=True)

    outgoing = call(
        functools.partial(chip_kernel, rows_each),
        shape((count // 2, rows_each + slot_rows, 2 * chans), BF),
        (keep, swap(give, "ns", 0)),
        flops=1 << 20,
    )
    arrived = exchange(outgoing)
    shares = call(
        functools.partial(sum_kernel, rows_each),
        shape((count // 2, rows_each, 2 * chans), BF),
        (arrived,),
        flops=1 << 20,
    )
    summed = exchange(shares)[: GRAD_ROWS // 2 // rows_each]
    other = swap(summed, "ns", 0)
    token_grad = call(
        functools.partial(owner_kernel, capacity, rows_each),
        shape((n_ns * capacity, features), BF),
        (arrived, proj),
        flops=1 << 27,
    )
    grad_proj, grad_first, grad_second, grad_mask = call(
        finish_kernel,
        (
            shape((chans, features), F32),
            shape((4, 4, chans, chans), F32),
            shape((4, bands, 4, chans), F32),
            shape((features,), F32),
        ),
        (summed, other, proj),
        flops=1 << 20,
    )
    return (token_grad[None, None], grad_proj.T, grad_first, grad_second.transpose(0, 2, 1, 3), grad_mask)


def solution(mesh):
    return jax.shard_map(
        functools.partial(per_device, mesh.shape["ew"], mesh.shape["ns"]),
        mesh=mesh,
        in_specs=(
            P("ns", "ew", None, None, None),
            P("ns", "ew", None, None),
            P("ns", "ew", None),
            P("ns", "ew", None, None, None),
            P(),
            P(),
            P(),
            P(),
            P(None, None, "ns", "ew"),
            P(None, None, "ns", "ew"),
        ),
        out_specs=(P("ns", "ew", None, None), P(), P(), P(), P()),
        check_vma=False,
    )
```

```python
import functools

import jax
import jax.numpy as jnp
import numpy as np
from jax import lax
from jax.experimental import pallas as pl
from jax.experimental.pallas import tpu as pltpu
from jax.sharding import PartitionSpec as P

BF = jnp.bfloat16
F32 = jnp.float32
VMEM = pl.BlockSpec(memory_space=pltpu.VMEM)
GROUP = 16
GRAD_ROWS = 1024
PROJ_AT = 512
SECOND_AT = 896
MASK_ROW = SECOND_AT + 12


def nn(a, b):
    return lax.dot_general(a, b, (((1,), (0,)), ((), ())), preferred_element_type=F32)


def nt(a, b):
    return lax.dot_general(a, b, (((1,), (1,)), ((), ())), preferred_element_type=F32)


def tn(a, b):
    return lax.dot_general(a, b, (((0,), (0,)), ((), ())), preferred_element_type=F32)


def iota(shape, dim):
    return lax.broadcasted_iota(jnp.int32, shape, dim)


def hidden_columns(cols, lanes):
    lane = lax.rem(lanes, cols)
    right = lane >= cols // 2
    own = 2 * jnp.where(right, lane - cols // 2, lane) + jnp.where(right, 1, 0)
    shifted = own + jnp.where(right, -2, 2)
    return jnp.where(lax.rem(lanes // cols, 2) == 0, own, shifted)


def table_kernel(pix_ref, cell_ref, pick_ref):
    cols = cell_ref.shape[0] // 2
    column_tables(cols, pix_ref, cell_ref)
    pick_g, pick_p = edge_tables(2 * cols, cols)
    pick_ref[:, : 2 * cols] = pick_g
    pick_ref[:, 2 * cols :] = pick_p


def column_tables(cols, pix_ref, cell_ref):
    fine = 2 * cols
    lanes = iota((1, fine), 1)
    hidden = hidden_columns(cols, lanes)
    for tap in range(4):
        pixel = 2 * hidden + tap - 1
        pixel = jnp.where(pixel < 0, fine + 6 + pixel, pixel)
        table = iota((fine + 128, fine), 0) == pixel
        pix_ref[:, tap * fine : (tap + 1) * fine] = table.astype(F32).astype(BF)
    cell = jnp.where(hidden < 0, cols + 1, hidden)
    cell_ref[...] = (iota((fine, fine), 0) == cell).astype(F32).astype(BF)


def spread(ref, wide, group):
    frames, real, rows, cols = ref.shape
    for f in range(frames):
        for o in range(group):
            value = ref[f, o].astype(F32) if o < real else jnp.zeros((rows, cols), F32)
            for h in range(cols // 128):
                wide[pl.ds(((h * frames + f) * group + o) * rows, rows), :] = value[:, h * 128 : (h + 1) * 128]


def gathered(wide, h, frames, group, rows, f, r):
    return wide[pl.ds((h * frames + f) * group * rows + r, group, stride=rows), :].astype(BF)


def edge_tables(pcol, cols):
    row, col = iota((16, pcol), 0), iota((16, pcol), 1)
    pick_g = ((row < 3) & (col == row)) | ((row >= 3) & (row < 6) & (col == row + pcol - 6))
    row, col = iota((16, cols), 0), iota((16, cols), 1)
    pick_p = ((row == 6) & (col == 0)) | ((row == 7) & (col == cols - 1))
    return pick_g.astype(F32).astype(BF), pick_p.astype(F32).astype(BF)


def layout_kernel(pick_ref, pre_ref, cot_ref, p_ref, g_ref, own_ref, pre_wide, cot_wide):
    frames, chans, rows, cols = pre_ref.shape
    prow, pcol = cot_ref.shape[2:]
    spread(pre_ref, pre_wide, chans)
    for r in range(rows):
        for f in range(frames):
            p_ref[pl.ds((r * frames + f) * chans, chans), :] = gathered(pre_wide, 0, frames, chans, rows, f, r)
    spread(cot_ref, cot_wide, GROUP)
    for f in range(frames):
        for y in range(prow):
            for h in range(pcol // 128):
                g_ref[pl.ds((f * prow + y) * GROUP, GROUP), h * 128 : (h + 1) * 128] = gathered(
                    cot_wide, h, frames, GROUP, prow, f, y
                )
    below = nt(pick_ref[:, pcol:], p_ref[...])[:8]
    line = frames * chans
    last = (rows - 1) * line
    below = jnp.concatenate([below[:, :line], below[:, last:], below[:, line:last]], axis=1)
    edges = nt(pick_ref[:, :pcol], g_ref[...])[:8]
    width = edges.shape[1]
    own_ref[...] = jnp.concatenate([edges + below[:, :width], below[:, width:]], axis=1).astype(BF)


def row_messages(g_ref, p_ref, ga_ref, pa_ref, gb_ref, pb_ref):
    deep, pcol = ga_ref.shape[0], g_ref.shape[1]
    chans, cols = pa_ref.shape[0], p_ref.shape[1]
    frames = pa_ref.shape[1] // cols
    tall = g_ref.shape[0] // frames
    high = p_ref.shape[0]

    def message(g_out, p_out, top):
        for f in range(frames):
            at = f * tall if top else (f + 1) * tall - deep
            g_out[:, f * pcol : (f + 1) * pcol] = g_ref[pl.ds(at, deep), :]
            at = f * chans if top else high - (frames - f) * chans
            p_out[:, f * cols : (f + 1) * cols] = p_ref[pl.ds(at, chans), :]

    even = lax.rem(lax.axis_index("ns"), 2) == 0

    @pl.when(even)
    def _():
        message(ga_ref, pa_ref, False)
        message(gb_ref, pb_ref, True)

    @pl.when(jnp.logical_not(even))
    def _():
        message(ga_ref, pa_ref, True)
        message(gb_ref, pb_ref, False)


def local_kernel(
    capacity, counts_ref, g_ref, p_ref, vis_ref, owners_ref, tokens_ref, mask_ref, proj_ref, first_ref, second_ref,
    ga_ref, pa_ref, gb_ref, pb_ref, grid_ref, pick_ref, hidden_ref, route_ref, wab_ref, w2_ref,
):
    row_messages(g_ref, p_ref, ga_ref, pa_ref, gb_ref, pb_ref)
    slots_all = tokens_ref.shape[0]
    frames, slots, patches = pick_ref.shape
    chans = proj_ref.shape[0]
    bands = second_ref.shape[1]
    slot_rows = -(-capacity // 8) * 8
    owners = route_ref.shape[0] // slot_rows
    eye = (iota((chans, chans), 0) == iota((chans, chans), 1)).astype(BF)
    pad = jnp.zeros((GROUP - bands, chans), F32)
    taps = []
    for b in range(4):
        for a in range(4):
            here = iota((bands, 4, chans), 1) == b
            tap = jnp.sum(jnp.where(here, second_ref[a].astype(F32), 0.0), axis=1)
            taps.append(jnp.concatenate([tap, pad], axis=0).astype(BF))
    w2_ref[...] = nt(eye, jnp.concatenate(taps, axis=0)).astype(BF)
    left = (iota((2 * chans, chans), 0) == iota((2 * chans, chans), 1)).astype(BF)
    right = (iota((2 * chans, chans), 0) == iota((2 * chans, chans), 1) + chans).astype(BF)
    for arrangement, (lo, hi) in enumerate(((1, 2), (3, 0))):
        taps_lo = jnp.concatenate([first_ref[a, lo] for a in range(4)], axis=0)
        taps_hi = jnp.concatenate([first_ref[a, hi] for a in range(4)], axis=0)
        wab_ref[:, arrangement * 4 * chans : (arrangement + 1) * 4 * chans] = (
            nt(left, taps_lo) + nt(right, taps_hi)
        ).astype(BF)
    vis = jnp.concatenate([vis_ref[f : f + 1, :] for f in range(frames)], axis=1)
    owner = jnp.concatenate([owners_ref[f] for f in range(frames)], axis=1)
    slot = iota((1, slots_all), 1)
    live = jnp.zeros((1, slots_all), jnp.int32)
    for f in range(frames):
        inside = (slot >= f * slots) & (slot < f * slots + counts_ref[:, f : f + 1])
        live = jnp.where(inside, 1, live)
    wanted = jnp.where(live > 0, vis, patches)
    square = (slots_all, slots_all)
    column = jnp.sum(
        jnp.where(iota(square, 0) == iota(square, 1), wanted.astype(F32), 0.0), axis=1, keepdims=True
    ).astype(jnp.int32)
    token_proj = nt(tokens_ref[...], proj_ref[...]).astype(BF)
    features = mask_ref.shape[0]
    mask_row = mask_ref[...].astype(F32).reshape(1, features)
    mask_proj = nt(jnp.broadcast_to(mask_row, (16, features)).astype(BF), proj_ref[...]).astype(BF)
    row0 = iota((16, patches), 0) == 0
    lane = iota((chans, 2 * chans), 1)
    for f in range(frames):
        hits = iota((slots, patches), 1) == column[f * slots : (f + 1) * slots]
        picks = hits.astype(F32)
        pick_ref[f] = picks.astype(BF)
        unseen = jnp.where(row0, 1.0 - jnp.sum(picks, axis=0, keepdims=True), 0.0).astype(BF)
        hidden_ref[:, f * patches : (f + 1) * patches] = unseen
        grid = tn(token_proj[f * slots : (f + 1) * slots], picks.astype(BF)) + tn(mask_proj, unseen)
        zero = jnp.zeros((chans, 2 * chans), F32)
        for line, (group, half_at) in enumerate(((1, 0), (0, 0), (0, 1), (1, 1))):
            pair = line // 2 * 2 * chans
            straight = grid[:, pair : pair + 2 * chans]
            turned = pltpu.roll(straight, chans, 1)
            to_left, to_right = (straight, turned) if line % 2 == 0 else (turned, straight)
            at = half_at * 2 * chans
            grid_ref[f, group, :chans, at : at + 2 * chans] = jnp.where(lane < chans, to_left, zero).astype(BF)
            grid_ref[f, group, chans:, at : at + 2 * chans] = jnp.where(lane < chans, zero, to_right).astype(BF)
    own_rows = -(-owners // 16) * 16
    hit = (iota((own_rows, slots_all), 0) == jnp.where(live > 0, owner, -1)).astype(F32)
    before = (iota(square, 0) < iota(square, 1)).astype(BF)
    earlier = nn(hit.astype(BF), before)
    place = jnp.sum(earlier * hit, axis=0, keepdims=True).astype(jnp.int32)
    block = lax.rem(owner, 2) * (owners // 2) + owner // 2
    target = jnp.where(live > 0, block * slot_rows + place, -1)
    route_ref[...] = (iota((owners * slot_rows, slots_all), 0) == target).astype(F32).astype(BF)


def side_columns(ea_ref, eb_ref, even_ew):
    ea, eb = ea_ref[...].astype(F32), eb_ref[...].astype(F32)
    return jnp.concatenate([jnp.where(even_ew, ea, eb), jnp.where(even_ew, eb, ea)], axis=0).astype(BF)


def halo_tables():
    row, col = iota((16, 128), 0), iota((16, 128), 1)
    pick_g = ((row < 3) & (col == row)) | ((row >= 11) & (row < 14) & (col == row - 8))
    pick_p = ((row == 6) & (col == 0)) | ((row == 15) & (col == 1))
    return pick_g.astype(F32).astype(BF), pick_p.astype(F32).astype(BF)


def second_backward(taps, pre, w2, drop):
    grad_hidden = nn(w2, jnp.concatenate(taps, axis=0))
    s = 0.5 + 0.5 * jnp.tanh(0.851 * pre)
    delta = grad_hidden * (s + 1.702 * pre * s * (1.0 - s))
    cols = pre.shape[1] // 2
    return jnp.where(drop, 0.0, delta).astype(BF), (pre[:, :cols] * s[:, :cols]).astype(BF)


def second_kernel_term(taps, hid):
    cols = hid.shape[1]
    zero = jnp.zeros_like(hid)
    lhs = jnp.concatenate(
        [
            jnp.concatenate([taps[0][:, :cols], taps[2][:, :cols]], axis=1),
            jnp.concatenate([taps[1][:, :cols], taps[3][:, :cols]], axis=1),
        ],
        axis=0,
    )
    rhs = jnp.concatenate(
        [jnp.concatenate([hid, zero], axis=1), jnp.concatenate([zero, hid], axis=1)], axis=0
    )
    return nt(lhs, rhs)


def outside_columns(chans, cols, n_ew, ew):
    lane = iota((chans, 2 * cols), 1)
    return ((lane == cols + cols // 2 - 1) & (ew == n_ew - 1)) | ((lane == cols + cols // 2) & (ew == 0))


def window_taps(wins, at, cols):
    return [wins[pl.ds(at, 4 * GROUP), b * 2 * cols : (b + 1) * 2 * cols] for b in range(4)]


def message_kernel(sb_ref, sa_ref, ga_ref, pa_ref, gb_ref, pb_ref, a_ref, b_ref):
    deep, span = ga_ref.shape
    corners = jnp.concatenate([sa_ref[:, :span].astype(F32), sb_ref[:, :span].astype(F32)], axis=0).astype(BF)
    for out, g, p in ((a_ref, ga_ref, pa_ref), (b_ref, gb_ref, pb_ref)):
        out[:deep, :span] = g[...]
        out[deep:, :span] = corners
        out[:, span:] = p[...]


def inner_kernel(
    n_ew, eb_ref, ea_ref, g_ref, p_ref, pix_ref, cell_ref, grid_ref, wab_ref, w2_ref,
    delta_ref, second_ref, first_ref, turn_ref, edge_ref, pre_ref, ext, wide, wins, pres,
):
    frames = grid_ref.shape[0]
    chans = w2_ref.shape[0]
    pcol, cols = g_ref.shape[1], p_ref.shape[1]
    tall = g_ref.shape[0] // frames
    rows = p_ref.shape[0] // (frames * chans)
    ew = lax.axis_index("ew")
    sides = side_columns(ea_ref, eb_ref, lax.rem(ew, 2) == 0)
    pick_g, pick_p = halo_tables()
    line = frames * chans
    ext[:, :pcol] = g_ref[...]
    ext[:, pcol:] = tn(sides[:, : frames * tall], pick_g).astype(BF)
    wide[:, :cols] = p_ref[...]
    halo = tn(sides, pick_p).astype(BF)
    wide[pl.ds(0, line), cols:] = halo[:line]
    wide[pl.ds((rows - 1) * line, line), cols:] = halo[line : 2 * line]
    wide[pl.ds(line, (rows - 2) * line), cols:] = halo[2 * line :]
    deep = 3 * GROUP
    for f in range(frames):
        block = ext[pl.ds(f * tall, tall), :]
        for b in range(4):
            lanes = slice(b * 2 * cols, (b + 1) * 2 * cols)
            wins[pl.ds(f * tall, tall), lanes] = nn(block, pix_ref[:, lanes]).astype(BF)
        edge_ref[f, 0] = wins[pl.ds(f * tall, deep), :]
        edge_ref[f, 1] = wins[pl.ds((f + 1) * tall - deep, deep), :]
    pres[...] = nn(wide[...], cell_ref[...])
    for f in range(frames):
        pre_ref[f, 0] = pres[pl.ds(f * chans, chans), :]
        pre_ref[f, 1] = pres[pl.ds((rows - 1) * line + f * chans, chans), :]
    w2 = w2_ref[...]
    wab = wab_ref[...]
    drop = outside_columns(chans, cols, n_ew, ew)
    grad_second = grad_first = None
    for f in range(frames):
        deltas = []
        for i in range(1, rows - 1):
            taps = window_taps(wins, f * tall + (2 * i - 1) * GROUP, cols)
            pre = pres[pl.ds(i * line + f * chans, chans), :]
            delta, hid = second_backward(taps, pre, w2, drop)
            deltas.append(delta)
            term = second_kernel_term(taps, hid)
            grad_second = term if grad_second is None else grad_second + term
        count = rows - 2
        for k, i in enumerate((0, 1, count - 2, count - 1)):
            delta_ref[pl.ds((f * 4 + k) * chans, chans), :] = deltas[i]
        cells = []
        for i in (0, 2):
            slab = jnp.concatenate(deltas[i : i + 4], axis=0)
            cells.append(jnp.concatenate([slab[:, :cols], slab[:, cols:]], axis=0))
        both = jnp.concatenate(cells, axis=1)
        term = nt(both, grid_ref[f, 0])
        grad_first = term if grad_first is None else grad_first + term
        turn_ref[f] = nn(wab, both)
    second_ref[...] = grad_second
    first_ref[...] = grad_first


def outer_kernel(
    n_ew, n_ns, rb_ref, ra_ref, pix_ref, cell_ref,
    delta_ref, second_ref, first_ref, turn_ref, edge_ref, pre_ref,
    grid_ref, pick_ref, hidden_ref, route_ref, wab_ref, w2_ref, tokens_ref, mask_ref,
    keep_ref, give_ref, ext, wide, wins, pres,
):
    frames, slots, patches = pick_ref.shape
    chans = w2_ref.shape[0]
    features = tokens_ref.shape[1]
    cols = pre_ref.shape[3] // 2
    pcol = 2 * cols
    deep = 3 * GROUP
    ns = lax.axis_index("ns")
    ew = lax.axis_index("ew")
    even_ns = lax.rem(ns, 2) == 0
    even_ew = lax.rem(ew, 2) == 0
    ra, rb = ra_ref[...], rb_ref[...]
    north = jnp.where(even_ns, rb, ra)
    south = jnp.where(even_ns, ra, rb)
    span = frames * pcol
    tall = span // frames

    def far_sides(message):
        a, b = message[deep : deep + 8, :span].astype(F32), message[deep + 8 :, :span].astype(F32)
        return jnp.concatenate([jnp.where(even_ew, a, b), jnp.where(even_ew, b, a)], axis=0).astype(BF)

    pick_g, pick_p = halo_tables()
    line = frames * chans
    far = (far_sides(north), far_sides(south))
    for low in range(2):
        message = south if low else north
        halo_p = tn(far[low][:, (1 - low) * line : (2 - low) * line], pick_p).astype(BF)
        for f in range(frames):
            at = (f * 2 + low) * deep
            ext[pl.ds(at, deep), :pcol] = message[:deep, f * pcol : (f + 1) * pcol]
            if low:
                ext[pl.ds(at, deep), pcol:] = tn(far[low][:, f * tall : f * tall + 128], pick_g).astype(BF)[:deep]
            else:
                end = (f + 1) * tall
                ext[pl.ds(at, deep), pcol:] = tn(far[low][:, end - 128 : end], pick_g).astype(BF)[128 - deep :]
            at = (f * 2 + low) * chans
            wide[pl.ds(at, chans), :cols] = message[:, span + f * cols : span + (f + 1) * cols]
            wide[pl.ds(at, chans), cols:] = halo_p[f * chans : (f + 1) * chans]
    block = ext[...]
    for b in range(4):
        lanes = slice(b * 2 * cols, (b + 1) * 2 * cols)
        wins[:, lanes] = nn(block, pix_ref[:, lanes]).astype(BF)
    pres[...] = nn(wide[...], cell_ref[...])
    w2 = w2_ref[...]
    wab = wab_ref[...]
    drop = outside_columns(chans, cols, n_ew, ew)
    grad_second = second_ref[...]
    grad_first = first_ref[...]
    half_lane = iota((chans, cols), 1) < cols // 2
    grids = []
    for f in range(frames):
        cells = []
        for low in range(2):
            pair = []
            for k in range(2):
                inside = k == 1 - low
                beyond = wins[pl.ds((f * 2 + low) * deep, deep), :]
                window = [edge_ref[f, low], beyond] if low else [beyond, edge_ref[f, low]]
                window = jnp.concatenate(window, axis=0)[k * 2 * GROUP : (k * 2 + 4) * GROUP]
                taps = [window[:, b * 2 * cols : (b + 1) * 2 * cols] for b in range(4)]
                pre = pre_ref[f, low] if inside else pres[pl.ds((f * 2 + low) * chans, chans), :]
                gone = drop if inside else drop | (ns == (n_ns - 1 if low else 0))
                delta, hid = second_backward(taps, pre, w2, gone)
                pair.append(delta)
                if inside:
                    grad_second = grad_second + second_kernel_term(taps, hid)
            kept = delta_ref[pl.ds((f * 4 + 2 * low) * chans, 2 * chans), :]
            slab = jnp.concatenate([kept, *pair] if low else [*pair, kept], axis=0)
            cells.append(jnp.concatenate([slab[:, :cols], slab[:, cols:]], axis=0))
        both = jnp.concatenate(cells, axis=1)
        grad_first = grad_first + nt(both, grid_ref[f, 1])
        edge = nn(wab, both)
        inner = turn_ref[f]
        parts = []
        for even, odd in ((edge[:, :cols], inner[:, :cols]), (inner[:, cols:], edge[:, cols:])):
            here = jnp.where(half_lane, even[:chans], odd[chans:])
            there = jnp.where(half_lane, odd[:chans], even[chans:])
            parts.append(here + pltpu.roll(there, cols // 2, 1))
        grids.append(jnp.concatenate(parts, axis=1).astype(BF))
    none = jnp.zeros((chans, patches), BF)
    mask_sum = nt(hidden_ref[...], jnp.concatenate(grids, axis=1))
    chosen = [nt(pick_ref[f], jnp.concatenate([grids[f], none], axis=0)) for f in range(frames)]
    chosen = jnp.concatenate(chosen, axis=0)
    placed = jnp.where(even_ns, chosen, pltpu.roll(chosen, chans, 1)).astype(BF)
    chosen = chosen.astype(BF)
    routed = nn(route_ref[...], placed)
    hi = mask_sum.astype(BF).astype(F32)
    lo = mask_sum - hi
    line = iota(hi.shape, 0)
    mask_rows = jnp.where(line == 0, hi[0:1], jnp.where(line == 1, lo[0:1], 0.0)).astype(BF)
    line = iota((16, features), 0)
    mask_row = mask_ref[...].astype(F32).reshape(1, features)
    spread_row = jnp.where(line < 2, mask_row, 0.0).astype(BF)
    grad_proj = tn(chosen[:, :chans], tokens_ref[...]) + tn(mask_rows, spread_row)
    grad_proj = [grad_proj[:, k * 128 : (k + 1) * 128] for k in range(features // 128)]
    both = jnp.concatenate([hi[0:1], lo[0:1]], axis=1)
    mark = iota(grad_second.shape, 0) == MASK_ROW - SECOND_AT
    grad_second = jnp.where(mark, both, grad_second)
    halves = (grad_first, jnp.concatenate([*grad_proj, grad_second], axis=0))
    part = routed.shape[0] // 2

    def split(mine):
        keep_ref[: GRAD_ROWS // 2, :] = halves[mine]
        keep_ref[GRAD_ROWS // 2 :, :] = routed[mine * part : (mine + 1) * part]
        give_ref[: GRAD_ROWS // 2, :] = halves[1 - mine].astype(BF)
        give_ref[GRAD_ROWS // 2 :, :] = routed[(1 - mine) * part : (2 - mine) * part].astype(BF)

    @pl.when(even_ns)
    def _():
        split(0)

    @pl.when(jnp.logical_not(even_ns))
    def _():
        split(1)


def chip_kernel(rows_each, keep_ref, got_ref, out_ref):
    count = out_ref.shape[0]
    slot_rows = out_ref.shape[1] - rows_each
    grads = GRAD_ROWS // 2
    chips = (keep_ref.shape[0] - grads) // slot_rows
    total = (keep_ref[...] + got_ref[...].astype(F32)).astype(BF)
    full = min(count, grads // rows_each)
    for d in range(full):
        out_ref[d, :rows_each, :] = total[d * rows_each : (d + 1) * rows_each]
    if full < count:

        @pl.loop(full, count)
        def _(d):
            out_ref[d, :rows_each, :] = jnp.zeros((rows_each, total.shape[1]), BF)

    for z in range(chips):
        rows = total[grads + z * slot_rows : grads + (z + 1) * slot_rows]
        for e in range(count // chips):
            out_ref[e * chips + z, rows_each:, :] = rows


def sum_kernel(rows_each, got_ref, sum_ref):
    count = got_ref.shape[0]
    if count <= 64:
        total = got_ref[0, :rows_each, :].astype(F32)
        for d in range(1, count):
            total = total + got_ref[d, :rows_each, :].astype(F32)
    else:
        total = lax.fori_loop(
            0,
            count,
            lambda d, acc: acc + got_ref[d, :rows_each, :].astype(F32),
            jnp.zeros((rows_each, got_ref.shape[2]), F32),
        )
    share = total.astype(BF)
    if count <= 64:
        for d in range(count):
            sum_ref[d] = share
    else:

        @pl.loop(0, count)
        def _(d):
            sum_ref[d] = share


def owner_kernel(capacity, rows_each, arrived_ref, proj_ref, token_ref):
    chans = proj_ref.shape[0]
    slot_rows = arrived_ref.shape[1] - rows_each
    chips = token_ref.shape[0] // (2 * capacity)
    ew = lax.axis_index("ew")
    arrived = [arrived_ref[ew * chips + z, rows_each:, :].astype(F32) for z in range(chips)]
    arrived = jnp.concatenate(arrived, axis=0).astype(BF)
    shape = (token_ref.shape[0], chips * slot_rows)
    row, col = iota(shape, 0), iota(shape, 1)
    source = (row // (2 * capacity)) * slot_rows + lax.rem(row, capacity)
    picked = nn((source == col).astype(F32).astype(BF), arrived)
    second = lax.rem(iota(picked.shape, 0) // capacity, 2) == 1
    picked = jnp.where(second, pltpu.roll(picked, chans, 1), picked)[:, :chans].astype(BF)
    token_ref[...] = nn(picked, proj_ref[...]).astype(BF)


def finish_kernel(mine_ref, other_ref, proj_ref, proj_out, first_out, second_out, mask_out):
    chans, features = proj_ref.shape
    bands = second_out.shape[1]
    rows_each = mine_ref.shape[1]
    blocks = range(GRAD_ROWS // 2 // rows_each)
    mine = jnp.concatenate([mine_ref[d] for d in blocks], axis=0)
    other = jnp.concatenate([other_ref[d] for d in blocks], axis=0)
    even = lax.rem(lax.axis_index("ns"), 2) == 0
    total = [jnp.where(even, mine, other), jnp.where(even, other, mine)]
    total = jnp.concatenate(total, axis=0).astype(F32)
    for arrangement, taps in enumerate(((1, 2), (3, 0))):
        rows = total[arrangement * 4 * chans : (arrangement + 1) * 4 * chans]
        turned = pltpu.roll(rows, chans, 1)
        for a in range(4):
            first_out[a, taps[0]] = rows[a * chans : (a + 1) * chans, :chans]
            first_out[a, taps[1]] = turned[a * chans : (a + 1) * chans, :chans]
    for k in range(features // 128):
        at = PROJ_AT + k * chans
        proj_out[:, k * 128 : (k + 1) * 128] = total[at : at + chans]
    rows = total[SECOND_AT:]
    turned = pltpu.roll(rows, chans, 1)
    for b in range(2):
        for a in range(4):
            at = (b * 4 + a) * GROUP
            second_out[a, :, b, :] = rows[at : at + bands, :chans]
            second_out[a, :, b + 2, :] = turned[at : at + bands, :chans]
    at = MASK_ROW - SECOND_AT
    mask_sum = rows[at : at + 1, :chans] + turned[at : at + 1, :chans]
    hi = mask_sum.astype(BF).astype(F32)
    mid = (mask_sum - hi).astype(BF).astype(F32)
    lo = mask_sum - hi - mid
    line = iota((16, chans), 0)
    split = jnp.where(line == 0, hi, jnp.where(line == 1, mid, jnp.where(line == 2, lo, 0.0)))
    grad_mask = jnp.sum(nn(split.astype(BF), proj_ref[...]), axis=0, keepdims=True)
    mask_out[...] = grad_mask.reshape(features)


def swap(block, axis, offset):
    count = lax.axis_size(axis)
    pairs = [(i, ((i + offset) ^ 1) - offset) for i in range(count)]
    return lax.ppermute(block, axis, [(i, j) for i, j in pairs if 0 <= j < count])


def call(kernel, outs, args, scratch=(), flops=0, limit=8 << 20, specs=None):
    return pl.pallas_call(
        kernel,
        out_shape=outs,
        in_specs=specs or [VMEM] * len(args),
        out_specs=jax.tree.map(lambda _: VMEM, outs),
        scratch_shapes=list(scratch),
        compiler_params=pltpu.CompilerParams(vmem_limit_bytes=limit),
        cost_estimate=pl.CostEstimate(flops=flops, bytes_accessed=1 << 10, transcendentals=0),
    )(*args)


def per_device(
    n_ew, n_ns, tokens, vis_index, counts, owners, mask_token, proj_weight, up_first, up_second, saved_pre, cotangent
):
    frames, slots, features = tokens.shape[2:]
    _, chans, rows, cols = saved_pre.shape
    bands, prow, pcol = cotangent.shape[1:]
    patches = rows * cols // 4
    count = n_ew * n_ns
    capacity = 3 * frames * slots // (2 * n_ns)
    rows_each = -(-GRAD_ROWS // count)
    rows_each = -(-rows_each // 16) * 16
    slot_rows = -(-capacity // 8) * 8
    groups = [[e * n_ns + z * 2 + c for e in range(n_ew) for z in range(n_ns // 2)] for c in range(2)]
    slots_all = frames * slots
    shape = jax.ShapeDtypeStruct

    tall = prow * GROUP
    pixels, cells, edge_picks = call(
        table_kernel,
        (shape((pcol + 128, 4 * pcol), BF), shape((pcol, pcol), BF), shape((16, pcol + cols), BF)),
        (),
        flops=1 << 33,
    )
    own_p, own_g, own_edges = call(
        layout_kernel,
        (
            shape((frames * rows * chans, cols), BF),
            shape((frames * tall, pcol), BF),
            shape((8, frames * rows * chans), BF),
        ),
        (edge_picks, saved_pre, cotangent),
        [
            pltpu.VMEM((frames * chans * rows, cols), F32),
            pltpu.VMEM((frames * tall * pcol // 128, 128), F32),
        ],
        flops=1 << 33,
    )
    side_b = swap(own_edges, "ew", 1)
    side_a = swap(own_edges, "ew", 0)

    tile_tokens = tokens.reshape(slots_all, features)
    proj = proj_weight.T
    g_message = shape((3 * GROUP, frames * pcol), BF)
    p_message = shape((chans, frames * cols), BF)
    g_a, p_a, g_b, p_b, grid, picks, hidden, route, wab, w2 = call(
        functools.partial(local_kernel, capacity),
        (
            g_message,
            p_message,
            g_message,
            p_message,
            shape((frames, 2, 2 * chans, 2 * cols), BF),
            shape((frames, slots, patches), BF),
            shape((16, frames * patches), BF),
            shape((n_ns * slot_rows, slots_all), BF),
            shape((2 * chans, 8 * chans), BF),
            shape((chans, 16 * GROUP), BF),
        ),
        (
            counts.reshape(1, frames),
            own_g,
            own_p,
            vis_index.reshape(frames, slots),
            owners.reshape(frames, 1, slots),
            tile_tokens,
            mask_token,
            proj,
            up_first,
            up_second.transpose(0, 2, 1, 3),
        ),
        flops=1 << 24,
    )
    message_shape = shape((3 * GROUP + 16, frames * (pcol + cols)), BF)
    send_a, send_b = call(
        message_kernel,
        (message_shape, message_shape),
        (side_b, side_a, g_a, p_a, g_b, p_b),
        flops=1 << 20,
    )
    got_b = swap(send_b, "ns", 1)
    got_a = swap(send_a, "ns", 0)

    delta_mid, second_mid, first_mid, turn_mid, edge_wins, edge_pre = call(
        functools.partial(inner_kernel, n_ew),
        (
            shape((frames * 4 * chans, 2 * cols), BF),
            shape((2 * 4 * GROUP, 2 * chans), F32),
            shape((8 * chans, 2 * chans), F32),
            shape((frames, 2 * chans, 2 * cols), F32),
            shape((frames, 2, 3 * GROUP, 8 * cols), BF),
            shape((frames, 2, chans, 2 * cols), F32),
        ),
        (side_b, side_a, own_g, own_p, pixels, cells, grid, wab, w2),
        [
            pltpu.VMEM((frames * tall, pcol + 128), BF),
            pltpu.VMEM((rows * frames * chans, 2 * cols), BF),
            pltpu.VMEM((frames * tall, 8 * cols), BF),
            pltpu.VMEM((rows * frames * chans, 2 * cols), F32),
        ],
        flops=1 << 27,
        limit=16 << 20,
    )
    beyond = frames * 2 * 3 * GROUP
    half_rows = GRAD_ROWS // 2 + n_ns // 2 * slot_rows
    keep, give = call(
        functools.partial(outer_kernel, n_ew, n_ns),
        (shape((half_rows, 2 * chans), F32), shape((half_rows, 2 * chans), BF)),
        (
            got_b, got_a, pixels, cells, delta_mid, second_mid, first_mid, turn_mid, edge_wins, edge_pre,
            grid, picks, hidden, route, wab, w2, tile_tokens, mask_token,
        ),
        [
            pltpu.VMEM((beyond, pcol + 128), BF),
            pltpu.VMEM((frames * 2 * chans, 2 * cols), BF),
            pltpu.VMEM((beyond, 8 * cols), BF),
            pltpu.VMEM((frames * 2 * chans, 2 * cols), F32),
        ],
        flops=1 << 27,
        limit=24 << 20,
    )

    def exchange(blocks):
        return lax.all_to_all(blocks, ("ew", "ns"), 0, 0, axis_index_groups=groups, tiled=True)

    outgoing = call(
        functools.partial(chip_kernel, rows_each),
        shape((count // 2, rows_each + slot_rows, 2 * chans), BF),
        (keep, swap(give, "ns", 0)),
        flops=1 << 20,
    )
    arrived = exchange(outgoing)
    shares = call(
        functools.partial(sum_kernel, rows_each),
        shape((count // 2, rows_each, 2 * chans), BF),
        (arrived,),
        flops=1 << 20,
    )
    summed = exchange(shares)[: GRAD_ROWS // 2 // rows_each]
    other = swap(summed, "ns", 0)
    token_grad = call(
        functools.partial(owner_kernel, capacity, rows_each),
        shape((n_ns * capacity, features), BF),
        (arrived, proj),
        flops=1 << 27,
    )
    grad_proj, grad_first, grad_second, grad_mask = call(
        finish_kernel,
        (
            shape((chans, features), F32),
            shape((4, 4, chans, chans), F32),
            shape((4, bands, 4, chans), F32),
            shape((features,), F32),
        ),
        (summed, other, proj),
        flops=1 << 20,
    )
    return (token_grad[None, None], grad_proj.T, grad_first, grad_second.transpose(0, 2, 1, 3), grad_mask)


def solution(mesh):
    return jax.shard_map(
        functools.partial(per_device, mesh.shape["ew"], mesh.shape["ns"]),
        mesh=mesh,
        in_specs=(
            P("ns", "ew", None, None, None),
            P("ns", "ew", None, None),
            P("ns", "ew", None),
            P("ns", "ew", None, None, None),
            P(),
            P(),
            P(),
            P(),
            P(None, None, "ns", "ew"),
            P(None, None, "ns", "ew"),
        ),
        out_specs=(P("ns", "ew", None, None), P(), P(), P(), P()),
        check_vma=False,
    )
```

```python
import functools

import jax
import jax.numpy as jnp
import numpy as np
from jax import lax
from jax.experimental import pallas as pl
from jax.experimental.pallas import tpu as pltpu
from jax.sharding import PartitionSpec as P

BF = jnp.bfloat16
F32 = jnp.float32
VMEM = pl.BlockSpec(memory_space=pltpu.VMEM)
GROUP = 16
GRAD_ROWS = 1024
PROJ_AT = 512
SECOND_AT = 896
MASK_ROW = SECOND_AT + 12


def nn(a, b):
    return lax.dot_general(a, b, (((1,), (0,)), ((), ())), preferred_element_type=F32)


def nt(a, b):
    return lax.dot_general(a, b, (((1,), (1,)), ((), ())), preferred_element_type=F32)


def tn(a, b):
    return lax.dot_general(a, b, (((0,), (0,)), ((), ())), preferred_element_type=F32)


def iota(shape, dim):
    return lax.broadcasted_iota(jnp.int32, shape, dim)


def hidden_columns(cols, lanes):
    lane = lax.rem(lanes, cols)
    right = lane >= cols // 2
    own = 2 * jnp.where(right, lane - cols // 2, lane) + jnp.where(right, 1, 0)
    shifted = own + jnp.where(right, -2, 2)
    return jnp.where(lax.rem(lanes // cols, 2) == 0, own, shifted)


def table_kernel(pix_ref, cell_ref, pick_ref):
    cols = cell_ref.shape[0] // 2
    column_tables(cols, pix_ref, cell_ref)
    pick_g, pick_p = edge_tables(2 * cols, cols)
    pick_ref[:, : 2 * cols] = pick_g
    pick_ref[:, 2 * cols :] = pick_p


def column_tables(cols, pix_ref, cell_ref):
    fine = 2 * cols
    lanes = iota((1, fine), 1)
    hidden = hidden_columns(cols, lanes)
    for tap in range(4):
        pixel = 2 * hidden + tap - 1
        pixel = jnp.where(pixel < 0, fine + 6 + pixel, pixel)
        table = iota((fine + 128, fine), 0) == pixel
        pix_ref[:, tap * fine : (tap + 1) * fine] = table.astype(F32).astype(BF)
    cell = jnp.where(hidden < 0, cols + 1, hidden)
    cell_ref[...] = (iota((fine, fine), 0) == cell).astype(F32).astype(BF)


def spread(ref, wide, group):
    frames, real, rows, cols = ref.shape
    for f in range(frames):
        for o in range(group):
            value = ref[f, o].astype(F32) if o < real else jnp.zeros((rows, cols), F32)
            for h in range(cols // 128):
                wide[pl.ds(((h * frames + f) * group + o) * rows, rows), :] = value[:, h * 128 : (h + 1) * 128]


def gathered(wide, h, frames, group, rows, f, r):
    return wide[pl.ds((h * frames + f) * group * rows + r, group, stride=rows), :].astype(BF)


def edge_tables(pcol, cols):
    row, col = iota((16, pcol), 0), iota((16, pcol), 1)
    pick_g = ((row < 3) & (col == row)) | ((row >= 3) & (row < 6) & (col == row + pcol - 6))
    row, col = iota((16, cols), 0), iota((16, cols), 1)
    pick_p = ((row == 6) & (col == 0)) | ((row == 7) & (col == cols - 1))
    return pick_g.astype(F32).astype(BF), pick_p.astype(F32).astype(BF)


def layout_kernel(pick_ref, pre_ref, cot_ref, p_ref, g_ref, own_ref, pre_wide, cot_wide):
    frames, chans, rows, cols = pre_ref.shape
    prow, pcol = cot_ref.shape[2:]
    spread(pre_ref, pre_wide, chans)
    for r in range(rows):
        for f in range(frames):
            p_ref[pl.ds((r * frames + f) * chans, chans), :] = gathered(pre_wide, 0, frames, chans, rows, f, r)
    spread(cot_ref, cot_wide, GROUP)
    for f in range(frames):
        for y in range(prow):
            for h in range(pcol // 128):
                g_ref[pl.ds((f * prow + y) * GROUP, GROUP), h * 128 : (h + 1) * 128] = gathered(
                    cot_wide, h, frames, GROUP, prow, f, y
                )
    below = nt(pick_ref[:, pcol:], p_ref[...])[:8]
    line = frames * chans
    last = (rows - 1) * line
    below = jnp.concatenate([below[:, :line], below[:, last:], below[:, line:last]], axis=1)
    edges = nt(pick_ref[:, :pcol], g_ref[...])[:8]
    width = edges.shape[1]
    own_ref[...] = jnp.concatenate([edges + below[:, :width], below[:, width:]], axis=1).astype(BF)


def row_messages(g_ref, p_ref, ga_ref, pa_ref, gb_ref, pb_ref):
    deep, pcol = ga_ref.shape[0], g_ref.shape[1]
    chans, cols = pa_ref.shape[0], p_ref.shape[1]
    frames = pa_ref.shape[1] // cols
    tall = g_ref.shape[0] // frames
    high = p_ref.shape[0]

    def message(g_out, p_out, top):
        for f in range(frames):
            at = f * tall if top else (f + 1) * tall - deep
            g_out[:, f * pcol : (f + 1) * pcol] = g_ref[pl.ds(at, deep), :]
            at = f * chans if top else high - (frames - f) * chans
            p_out[:, f * cols : (f + 1) * cols] = p_ref[pl.ds(at, chans), :]

    even = lax.rem(lax.axis_index("ns"), 2) == 0

    @pl.when(even)
    def _():
        message(ga_ref, pa_ref, False)
        message(gb_ref, pb_ref, True)

    @pl.when(jnp.logical_not(even))
    def _():
        message(ga_ref, pa_ref, True)
        message(gb_ref, pb_ref, False)


def local_kernel(
    capacity, counts_ref, g_ref, p_ref, vis_ref, owners_ref, tokens_ref, mask_ref, proj_ref, first_ref, second_ref,
    ga_ref, pa_ref, gb_ref, pb_ref, grid_ref, pick_ref, hidden_ref, route_ref, wab_ref, w2_ref,
):
    row_messages(g_ref, p_ref, ga_ref, pa_ref, gb_ref, pb_ref)
    slots_all = tokens_ref.shape[0]
    frames, slots, patches = pick_ref.shape
    chans = proj_ref.shape[0]
    bands = second_ref.shape[1]
    slot_rows = -(-capacity // 8) * 8
    owners = route_ref.shape[0] // slot_rows
    eye = (iota((chans, chans), 0) == iota((chans, chans), 1)).astype(BF)
    pad = jnp.zeros((GROUP - bands, chans), F32)
    taps = []
    for b in range(4):
        for a in range(4):
            here = iota((bands, 4, chans), 1) == b
            tap = jnp.sum(jnp.where(here, second_ref[a].astype(F32), 0.0), axis=1)
            taps.append(jnp.concatenate([tap, pad], axis=0).astype(BF))
    w2_ref[...] = nt(eye, jnp.concatenate(taps, axis=0)).astype(BF)
    left = (iota((2 * chans, chans), 0) == iota((2 * chans, chans), 1)).astype(BF)
    right = (iota((2 * chans, chans), 0) == iota((2 * chans, chans), 1) + chans).astype(BF)
    for arrangement, (lo, hi) in enumerate(((1, 2), (3, 0))):
        taps_lo = jnp.concatenate([first_ref[a, lo] for a in range(4)], axis=0)
        taps_hi = jnp.concatenate([first_ref[a, hi] for a in range(4)], axis=0)
        wab_ref[:, arrangement * 4 * chans : (arrangement + 1) * 4 * chans] = (
            nt(left, taps_lo) + nt(right, taps_hi)
        ).astype(BF)
    vis = jnp.concatenate([vis_ref[f : f + 1, :] for f in range(frames)], axis=1)
    owner = jnp.concatenate([owners_ref[f] for f in range(frames)], axis=1)
    slot = iota((1, slots_all), 1)
    live = jnp.zeros((1, slots_all), jnp.int32)
    for f in range(frames):
        inside = (slot >= f * slots) & (slot < f * slots + counts_ref[:, f : f + 1])
        live = jnp.where(inside, 1, live)
    wanted = jnp.where(live > 0, vis, patches)
    square = (slots_all, slots_all)
    column = jnp.sum(
        jnp.where(iota(square, 0) == iota(square, 1), wanted.astype(F32), 0.0), axis=1, keepdims=True
    ).astype(jnp.int32)
    token_proj = nt(tokens_ref[...], proj_ref[...]).astype(BF)
    features = mask_ref.shape[0]
    mask_row = mask_ref[...].astype(F32).reshape(1, features)
    mask_proj = nt(jnp.broadcast_to(mask_row, (16, features)).astype(BF), proj_ref[...]).astype(BF)
    row0 = iota((16, patches), 0) == 0
    lane = iota((chans, 2 * chans), 1)
    for f in range(frames):
        hits = iota((slots, patches), 1) == column[f * slots : (f + 1) * slots]
        picks = hits.astype(F32)
        pick_ref[f] = picks.astype(BF)
        unseen = jnp.where(row0, 1.0 - jnp.sum(picks, axis=0, keepdims=True), 0.0).astype(BF)
        hidden_ref[:, f * patches : (f + 1) * patches] = unseen
        grid = tn(token_proj[f * slots : (f + 1) * slots], picks.astype(BF)) + tn(mask_proj, unseen)
        zero = jnp.zeros((chans, 2 * chans), F32)
        for line, (group, half_at) in enumerate(((1, 0), (0, 0), (0, 1), (1, 1))):
            pair = line // 2 * 2 * chans
            straight = grid[:, pair : pair + 2 * chans]
            turned = pltpu.roll(straight, chans, 1)
            to_left, to_right = (straight, turned) if line % 2 == 0 else (turned, straight)
            at = half_at * 2 * chans
            grid_ref[f, group, :chans, at : at + 2 * chans] = jnp.where(lane < chans, to_left, zero).astype(BF)
            grid_ref[f, group, chans:, at : at + 2 * chans] = jnp.where(lane < chans, zero, to_right).astype(BF)
    own_rows = -(-owners // 16) * 16
    hit = (iota((own_rows, slots_all), 0) == jnp.where(live > 0, owner, -1)).astype(F32)
    before = (iota(square, 0) < iota(square, 1)).astype(BF)
    earlier = nn(hit.astype(BF), before)
    place = jnp.sum(earlier * hit, axis=0, keepdims=True).astype(jnp.int32)
    block = lax.rem(owner, 2) * (owners // 2) + owner // 2
    target = jnp.where(live > 0, block * slot_rows + place, -1)
    route_ref[...] = (iota((owners * slot_rows, slots_all), 0) == target).astype(F32).astype(BF)


def side_columns(ea_ref, eb_ref, even_ew):
    ea, eb = ea_ref[...].astype(F32), eb_ref[...].astype(F32)
    return jnp.concatenate([jnp.where(even_ew, ea, eb), jnp.where(even_ew, eb, ea)], axis=0).astype(BF)


def halo_tables():
    row, col = iota((16, 128), 0), iota((16, 128), 1)
    pick_g = ((row < 3) & (col == row)) | ((row >= 11) & (row < 14) & (col == row - 8))
    pick_p = ((row == 6) & (col == 0)) | ((row == 15) & (col == 1))
    return pick_g.astype(F32).astype(BF), pick_p.astype(F32).astype(BF)


def second_backward(taps, pre, w2, drop):
    grad_hidden = nn(w2, jnp.concatenate(taps, axis=0))
    s = 0.5 + 0.5 * jnp.tanh(0.851 * pre)
    delta = grad_hidden * (s + 1.702 * pre * s * (1.0 - s))
    cols = pre.shape[1] // 2
    return jnp.where(drop, 0.0, delta).astype(BF), (pre[:, :cols] * s[:, :cols]).astype(BF)


def second_kernel_term(taps, hid):
    cols = hid.shape[1]
    zero = jnp.zeros_like(hid)
    lhs = jnp.concatenate(
        [
            jnp.concatenate([taps[0][:, :cols], taps[2][:, :cols]], axis=1),
            jnp.concatenate([taps[1][:, :cols], taps[3][:, :cols]], axis=1),
        ],
        axis=0,
    )
    rhs = jnp.concatenate(
        [jnp.concatenate([hid, zero], axis=1), jnp.concatenate([zero, hid], axis=1)], axis=0
    )
    return nt(lhs, rhs)


def outside_columns(chans, cols, n_ew, ew):
    lane = iota((chans, 2 * cols), 1)
    return ((lane == cols + cols // 2 - 1) & (ew == n_ew - 1)) | ((lane == cols + cols // 2) & (ew == 0))


def window_taps(wins, at, cols):
    return [wins[pl.ds(at, 4 * GROUP), b * 2 * cols : (b + 1) * 2 * cols] for b in range(4)]


def message_kernel(sb_ref, sa_ref, ga_ref, pa_ref, gb_ref, pb_ref, a_ref, b_ref):
    deep, span = ga_ref.shape
    corners = jnp.concatenate([sa_ref[:, :span].astype(F32), sb_ref[:, :span].astype(F32)], axis=0).astype(BF)
    for out, g, p in ((a_ref, ga_ref, pa_ref), (b_ref, gb_ref, pb_ref)):
        out[:deep, :span] = g[...]
        out[deep:, :span] = corners
        out[:, span:] = p[...]


def inner_kernel(
    n_ew, eb_ref, ea_ref, g_ref, p_ref, pix_ref, cell_ref, grid_ref, wab_ref, w2_ref,
    delta_ref, second_ref, first_ref, turn_ref, edge_ref, pre_ref, ext, wide, wins, pres,
):
    frames = grid_ref.shape[0]
    chans = w2_ref.shape[0]
    pcol, cols = g_ref.shape[1], p_ref.shape[1]
    tall = g_ref.shape[0] // frames
    rows = p_ref.shape[0] // (frames * chans)
    ew = lax.axis_index("ew")
    sides = side_columns(ea_ref, eb_ref, lax.rem(ew, 2) == 0)
    pick_g, pick_p = halo_tables()
    line = frames * chans
    ext[:, :pcol] = g_ref[...]
    ext[:, pcol:] = tn(sides[:, : frames * tall], pick_g).astype(BF)
    wide[:, :cols] = p_ref[...]
    halo = tn(sides, pick_p).astype(BF)
    wide[pl.ds(0, line), cols:] = halo[:line]
    wide[pl.ds((rows - 1) * line, line), cols:] = halo[line : 2 * line]
    wide[pl.ds(line, (rows - 2) * line), cols:] = halo[2 * line :]
    deep = 3 * GROUP
    for f in range(frames):
        block = ext[pl.ds(f * tall, tall), :]
        for b in range(4):
            lanes = slice(b * 2 * cols, (b + 1) * 2 * cols)
            wins[pl.ds(f * tall, tall), lanes] = nn(block, pix_ref[:, lanes]).astype(BF)
        edge_ref[f, 0] = wins[pl.ds(f * tall, deep), :]
        edge_ref[f, 1] = wins[pl.ds((f + 1) * tall - deep, deep), :]
    pres[...] = nn(wide[...], cell_ref[...])
    for f in range(frames):
        pre_ref[f, 0] = pres[pl.ds(f * chans, chans), :]
        pre_ref[f, 1] = pres[pl.ds((rows - 1) * line + f * chans, chans), :]
    w2 = w2_ref[...]
    wab = wab_ref[...]
    drop = outside_columns(chans, cols, n_ew, ew)
    grad_second = grad_first = None
    for f in range(frames):
        deltas = []
        for i in range(1, rows - 1):
            taps = window_taps(wins, f * tall + (2 * i - 1) * GROUP, cols)
            pre = pres[pl.ds(i * line + f * chans, chans), :]
            delta, hid = second_backward(taps, pre, w2, drop)
            deltas.append(delta)
            term = second_kernel_term(taps, hid)
            grad_second = term if grad_second is None else grad_second + term
        count = rows - 2
        for k, i in enumerate((0, 1, count - 2, count - 1)):
            delta_ref[pl.ds((f * 4 + k) * chans, chans), :] = deltas[i]
        cells = []
        for i in (0, 2):
            slab = jnp.concatenate(deltas[i : i + 4], axis=0)
            cells.append(jnp.concatenate([slab[:, :cols], slab[:, cols:]], axis=0))
        both = jnp.concatenate(cells, axis=1)
        term = nt(both, grid_ref[f, 0])
        grad_first = term if grad_first is None else grad_first + term
        turn_ref[f] = nn(wab, both)
    second_ref[...] = grad_second
    first_ref[...] = grad_first


def outer_kernel(
    n_ew, n_ns, rb_ref, ra_ref, pix_ref, cell_ref,
    delta_ref, second_ref, first_ref, turn_ref, edge_ref, pre_ref,
    grid_ref, pick_ref, hidden_ref, route_ref, wab_ref, w2_ref, tokens_ref, mask_ref,
    keep_ref, give_ref, ext, wide, wins, pres,
):
    frames, slots, patches = pick_ref.shape
    chans = w2_ref.shape[0]
    features = tokens_ref.shape[1]
    cols = pre_ref.shape[3] // 2
    pcol = 2 * cols
    deep = 3 * GROUP
    ns = lax.axis_index("ns")
    ew = lax.axis_index("ew")
    even_ns = lax.rem(ns, 2) == 0
    even_ew = lax.rem(ew, 2) == 0
    ra, rb = ra_ref[...], rb_ref[...]
    north = jnp.where(even_ns, rb, ra)
    south = jnp.where(even_ns, ra, rb)
    span = frames * pcol
    tall = span // frames

    def far_sides(message):
        a, b = message[deep : deep + 8, :span].astype(F32), message[deep + 8 :, :span].astype(F32)
        return jnp.concatenate([jnp.where(even_ew, a, b), jnp.where(even_ew, b, a)], axis=0).astype(BF)

    pick_g, pick_p = halo_tables()
    line = frames * chans
    far = (far_sides(north), far_sides(south))
    for low in range(2):
        message = south if low else north
        halo_p = tn(far[low][:, (1 - low) * line : (2 - low) * line], pick_p).astype(BF)
        for f in range(frames):
            at = (f * 2 + low) * deep
            ext[pl.ds(at, deep), :pcol] = message[:deep, f * pcol : (f + 1) * pcol]
            if low:
                ext[pl.ds(at, deep), pcol:] = tn(far[low][:, f * tall : f * tall + 128], pick_g).astype(BF)[:deep]
            else:
                end = (f + 1) * tall
                ext[pl.ds(at, deep), pcol:] = tn(far[low][:, end - 128 : end], pick_g).astype(BF)[128 - deep :]
            at = (f * 2 + low) * chans
            wide[pl.ds(at, chans), :cols] = message[:, span + f * cols : span + (f + 1) * cols]
            wide[pl.ds(at, chans), cols:] = halo_p[f * chans : (f + 1) * chans]
    block = ext[...]
    for b in range(4):
        lanes = slice(b * 2 * cols, (b + 1) * 2 * cols)
        wins[:, lanes] = nn(block, pix_ref[:, lanes]).astype(BF)
    pres[...] = nn(wide[...], cell_ref[...])
    w2 = w2_ref[...]
    wab = wab_ref[...]
    drop = outside_columns(chans, cols, n_ew, ew)
    grad_second = second_ref[...]
    grad_first = first_ref[...]
    half_lane = iota((chans, cols), 1) < cols // 2
    grids = []
    for f in range(frames):
        cells = []
        for low in range(2):
            pair = []
            for k in range(2):
                inside = k == 1 - low
                beyond = wins[pl.ds((f * 2 + low) * deep, deep), :]
                window = [edge_ref[f, low], beyond] if low else [beyond, edge_ref[f, low]]
                window = jnp.concatenate(window, axis=0)[k * 2 * GROUP : (k * 2 + 4) * GROUP]
                taps = [window[:, b * 2 * cols : (b + 1) * 2 * cols] for b in range(4)]
                pre = pre_ref[f, low] if inside else pres[pl.ds((f * 2 + low) * chans, chans), :]
                gone = drop if inside else drop | (ns == (n_ns - 1 if low else 0))
                delta, hid = second_backward(taps, pre, w2, gone)
                pair.append(delta)
                if inside:
                    grad_second = grad_second + second_kernel_term(taps, hid)
            kept = delta_ref[pl.ds((f * 4 + 2 * low) * chans, 2 * chans), :]
            slab = jnp.concatenate([kept, *pair] if low else [*pair, kept], axis=0)
            cells.append(jnp.concatenate([slab[:, :cols], slab[:, cols:]], axis=0))
        both = jnp.concatenate(cells, axis=1)
        grad_first = grad_first + nt(both, grid_ref[f, 1])
        edge = nn(wab, both)
        inner = turn_ref[f]
        parts = []
        for even, odd in ((edge[:, :cols], inner[:, :cols]), (inner[:, cols:], edge[:, cols:])):
            here = jnp.where(half_lane, even[:chans], odd[chans:])
            there = jnp.where(half_lane, odd[:chans], even[chans:])
            parts.append(here + pltpu.roll(there, cols // 2, 1))
        grids.append(jnp.concatenate(parts, axis=1).astype(BF))
    none = jnp.zeros((chans, patches), BF)
    mask_sum = nt(hidden_ref[...], jnp.concatenate(grids, axis=1))
    chosen = [nt(pick_ref[f], jnp.concatenate([grids[f], none], axis=0)) for f in range(frames)]
    chosen = jnp.concatenate(chosen, axis=0)
    placed = jnp.where(even_ns, chosen, pltpu.roll(chosen, chans, 1)).astype(BF)
    chosen = chosen.astype(BF)
    routed = nn(route_ref[...], placed)
    hi = mask_sum.astype(BF).astype(F32)
    lo = mask_sum - hi
    line = iota(hi.shape, 0)
    mask_rows = jnp.where(line == 0, hi[0:1], jnp.where(line == 1, lo[0:1], 0.0)).astype(BF)
    line = iota((16, features), 0)
    mask_row = mask_ref[...].astype(F32).reshape(1, features)
    spread_row = jnp.where(line < 2, mask_row, 0.0).astype(BF)
    grad_proj = tn(chosen[:, :chans], tokens_ref[...]) + tn(mask_rows, spread_row)
    grad_proj = [grad_proj[:, k * 128 : (k + 1) * 128] for k in range(features // 128)]
    both = jnp.concatenate([hi[0:1], lo[0:1]], axis=1)
    mark = iota(grad_second.shape, 0) == MASK_ROW - SECOND_AT
    grad_second = jnp.where(mark, both, grad_second)
    halves = (grad_first, jnp.concatenate([*grad_proj, grad_second], axis=0))
    part = routed.shape[0] // 2

    def split(mine):
        keep_ref[: GRAD_ROWS // 2, :] = halves[mine]
        keep_ref[GRAD_ROWS // 2 :, :] = routed[mine * part : (mine + 1) * part]
        give_ref[: GRAD_ROWS // 2, :] = halves[1 - mine].astype(BF)
        give_ref[GRAD_ROWS // 2 :, :] = routed[(1 - mine) * part : (2 - mine) * part].astype(BF)

    @pl.when(even_ns)
    def _():
        split(0)

    @pl.when(jnp.logical_not(even_ns))
    def _():
        split(1)


def chip_kernel(rows_each, keep_ref, got_ref, out_ref):
    count = out_ref.shape[0]
    slot_rows = out_ref.shape[1] - rows_each
    grads = GRAD_ROWS // 2
    chips = (keep_ref.shape[0] - grads) // slot_rows
    total = (keep_ref[...] + got_ref[...].astype(F32)).astype(BF)
    full = min(count, grads // rows_each)
    for d in range(full):
        out_ref[d, :rows_each, :] = total[d * rows_each : (d + 1) * rows_each]
    if full < count:

        @pl.loop(full, count)
        def _(d):
            out_ref[d, :rows_each, :] = jnp.zeros((rows_each, total.shape[1]), BF)

    for z in range(chips):
        rows = total[grads + z * slot_rows : grads + (z + 1) * slot_rows]
        for e in range(count // chips):
            out_ref[e * chips + z, rows_each:, :] = rows


def sum_kernel(rows_each, got_ref, sum_ref):
    count = got_ref.shape[0]
    if count <= 64:
        total = got_ref[0, :rows_each, :].astype(F32)
        for d in range(1, count):
            total = total + got_ref[d, :rows_each, :].astype(F32)
    else:
        total = lax.fori_loop(
            0,
            count,
            lambda d, acc: acc + got_ref[d, :rows_each, :].astype(F32),
            jnp.zeros((rows_each, got_ref.shape[2]), F32),
        )
    share = total.astype(BF)
    if count <= 64:
        for d in range(count):
            sum_ref[d] = share
    else:

        @pl.loop(0, count)
        def _(d):
            sum_ref[d] = share


def owner_kernel(capacity, rows_each, arrived_ref, proj_ref, token_ref):
    chans = proj_ref.shape[0]
    slot_rows = arrived_ref.shape[1] - rows_each
    chips = token_ref.shape[0] // (2 * capacity)
    ew = lax.axis_index("ew")
    arrived = [arrived_ref[ew * chips + z, rows_each:, :].astype(F32) for z in range(chips)]
    arrived = jnp.concatenate(arrived, axis=0).astype(BF)
    shape = (token_ref.shape[0], chips * slot_rows)
    row, col = iota(shape, 0), iota(shape, 1)
    source = (row // (2 * capacity)) * slot_rows + lax.rem(row, capacity)
    picked = nn((source == col).astype(F32).astype(BF), arrived)
    second = lax.rem(iota(picked.shape, 0) // capacity, 2) == 1
    picked = jnp.where(second, pltpu.roll(picked, chans, 1), picked)[:, :chans].astype(BF)
    token_ref[...] = nn(picked, proj_ref[...]).astype(BF)


def finish_kernel(mine_ref, other_ref, proj_ref, proj_out, first_out, second_out, mask_out):
    chans, features = proj_ref.shape
    bands = second_out.shape[1]
    rows_each = mine_ref.shape[1]
    blocks = range(GRAD_ROWS // 2 // rows_each)
    mine = jnp.concatenate([mine_ref[d] for d in blocks], axis=0)
    other = jnp.concatenate([other_ref[d] for d in blocks], axis=0)
    even = lax.rem(lax.axis_index("ns"), 2) == 0
    total = [jnp.where(even, mine, other), jnp.where(even, other, mine)]
    total = jnp.concatenate(total, axis=0).astype(F32)
    for arrangement, taps in enumerate(((1, 2), (3, 0))):
        rows = total[arrangement * 4 * chans : (arrangement + 1) * 4 * chans]
        turned = pltpu.roll(rows, chans, 1)
        for a in range(4):
            first_out[a, taps[0]] = rows[a * chans : (a + 1) * chans, :chans]
            first_out[a, taps[1]] = turned[a * chans : (a + 1) * chans, :chans]
    for k in range(features // 128):
        at = PROJ_AT + k * chans
        proj_out[:, k * 128 : (k + 1) * 128] = total[at : at + chans]
    rows = total[SECOND_AT:]
    turned = pltpu.roll(rows, chans, 1)
    for b in range(2):
        for a in range(4):
            at = (b * 4 + a) * GROUP
            second_out[a, :, b, :] = rows[at : at + bands, :chans]
            second_out[a, :, b + 2, :] = turned[at : at + bands, :chans]
    at = MASK_ROW - SECOND_AT
    mask_sum = rows[at : at + 1, :chans] + turned[at : at + 1, :chans]
    hi = mask_sum.astype(BF).astype(F32)
    mid = (mask_sum - hi).astype(BF).astype(F32)
    lo = mask_sum - hi - mid
    line = iota((16, chans), 0)
    split = jnp.where(line == 0, hi, jnp.where(line == 1, mid, jnp.where(line == 2, lo, 0.0)))
    grad_mask = jnp.sum(nn(split.astype(BF), proj_ref[...]), axis=0, keepdims=True)
    mask_out[...] = grad_mask.reshape(features)


def swap(block, axis, offset):
    count = lax.axis_size(axis)
    pairs = [(i, ((i + offset) ^ 1) - offset) for i in range(count)]
    return lax.ppermute(block, axis, [(i, j) for i, j in pairs if 0 <= j < count])


def call(kernel, outs, args, scratch=(), flops=0, limit=8 << 20):
    return pl.pallas_call(
        kernel,
        out_shape=outs,
        in_specs=[VMEM] * len(args),
        out_specs=jax.tree.map(lambda _: VMEM, outs),
        scratch_shapes=list(scratch),
        compiler_params=pltpu.CompilerParams(vmem_limit_bytes=limit),
        cost_estimate=pl.CostEstimate(flops=flops, bytes_accessed=1 << 10, transcendentals=0),
    )(*args)


def per_device(
    n_ew, n_ns, tokens, vis_index, counts, owners, mask_token, proj_weight, up_first, up_second, saved_pre, cotangent
):
    frames, slots, features = tokens.shape[2:]
    _, chans, rows, cols = saved_pre.shape
    bands, prow, pcol = cotangent.shape[1:]
    patches = rows * cols // 4
    count = n_ew * n_ns
    capacity = 3 * frames * slots // (2 * n_ns)
    rows_each = -(-GRAD_ROWS // count)
    rows_each = -(-rows_each // 16) * 16
    slot_rows = -(-capacity // 8) * 8
    groups = [[e * n_ns + z * 2 + c for e in range(n_ew) for z in range(n_ns // 2)] for c in range(2)]
    slots_all = frames * slots
    shape = jax.ShapeDtypeStruct

    tall = prow * GROUP
    pixels, cells, edge_picks = call(
        table_kernel,
        (shape((pcol + 128, 4 * pcol), BF), shape((pcol, pcol), BF), shape((16, pcol + cols), BF)),
        (),
        flops=1 << 33,
    )
    own_p, own_g, own_edges = call(
        layout_kernel,
        (
            shape((frames * rows * chans, cols), BF),
            shape((frames * tall, pcol), BF),
            shape((8, frames * rows * chans), BF),
        ),
        (edge_picks, saved_pre, cotangent),
        [
            pltpu.VMEM((frames * chans * rows + rows, cols), F32),
            pltpu.VMEM((frames * tall * pcol // 128 + prow, 128), F32),
        ],
        flops=1 << 33,
    )
    side_b = swap(own_edges, "ew", 1)
    side_a = swap(own_edges, "ew", 0)

    tile_tokens = tokens.reshape(slots_all, features)
    proj = proj_weight.T
    g_message = shape((3 * GROUP, frames * pcol), BF)
    p_message = shape((chans, frames * cols), BF)
    g_a, p_a, g_b, p_b, grid, picks, hidden, route, wab, w2 = call(
        functools.partial(local_kernel, capacity),
        (
            g_message,
            p_message,
            g_message,
            p_message,
            shape((frames, 2, 2 * chans, 2 * cols), BF),
            shape((frames, slots, patches), BF),
            shape((16, frames * patches), BF),
            shape((n_ns * slot_rows, slots_all), BF),
            shape((2 * chans, 8 * chans), BF),
            shape((chans, 16 * GROUP), BF),
        ),
        (
            counts.reshape(1, frames),
            own_g,
            own_p,
            vis_index.reshape(frames, slots),
            owners.reshape(frames, 1, slots),
            tile_tokens,
            mask_token,
            proj,
            up_first,
            up_second.transpose(0, 2, 1, 3),
        ),
        flops=1 << 24,
    )
    message_shape = shape((3 * GROUP + 16, frames * (pcol + cols)), BF)
    send_a, send_b = call(
        message_kernel,
        (message_shape, message_shape),
        (side_b, side_a, g_a, p_a, g_b, p_b),
        flops=1 << 20,
    )
    got_b = swap(send_b, "ns", 1)
    got_a = swap(send_a, "ns", 0)

    delta_mid, second_mid, first_mid, turn_mid, edge_wins, edge_pre = call(
        functools.partial(inner_kernel, n_ew),
        (
            shape((frames * 4 * chans, 2 * cols), BF),
            shape((2 * 4 * GROUP, 2 * chans), F32),
            shape((8 * chans, 2 * chans), F32),
            shape((frames, 2 * chans, 2 * cols), F32),
            shape((frames, 2, 3 * GROUP, 8 * cols), BF),
            shape((frames, 2, chans, 2 * cols), F32),
        ),
        (side_b, side_a, own_g, own_p, pixels, cells, grid, wab, w2),
        [
            pltpu.VMEM((frames * tall, pcol + 128), BF),
            pltpu.VMEM((rows * frames * chans, 2 * cols), BF),
            pltpu.VMEM((frames * tall, 8 * cols), BF),
            pltpu.VMEM((rows * frames * chans, 2 * cols), F32),
        ],
        flops=1 << 27,
        limit=16 << 20,
    )
    beyond = frames * 2 * 3 * GROUP
    half_rows = GRAD_ROWS // 2 + n_ns // 2 * slot_rows
    keep, give = call(
        functools.partial(outer_kernel, n_ew, n_ns),
        (shape((half_rows, 2 * chans), F32), shape((half_rows, 2 * chans), BF)),
        (
            got_b, got_a, pixels, cells, delta_mid, second_mid, first_mid, turn_mid, edge_wins, edge_pre,
            grid, picks, hidden, route, wab, w2, tile_tokens, mask_token,
        ),
        [
            pltpu.VMEM((beyond, pcol + 128), BF),
            pltpu.VMEM((frames * 2 * chans, 2 * cols), BF),
            pltpu.VMEM((beyond, 8 * cols), BF),
            pltpu.VMEM((frames * 2 * chans, 2 * cols), F32),
        ],
        flops=1 << 27,
        limit=24 << 20,
    )

    def exchange(blocks):
        return lax.all_to_all(blocks, ("ew", "ns"), 0, 0, axis_index_groups=groups, tiled=True)

    outgoing = call(
        functools.partial(chip_kernel, rows_each),
        shape((count // 2, rows_each + slot_rows, 2 * chans), BF),
        (keep, swap(give, "ns", 0)),
        flops=1 << 20,
    )
    arrived = exchange(outgoing)
    shares = call(
        functools.partial(sum_kernel, rows_each),
        shape((count // 2, rows_each, 2 * chans), BF),
        (arrived,),
        flops=1 << 20,
    )
    summed = exchange(shares)[: GRAD_ROWS // 2 // rows_each]
    other = swap(summed, "ns", 0)
    token_grad = call(
        functools.partial(owner_kernel, capacity, rows_each),
        shape((n_ns * capacity, features), BF),
        (arrived, proj),
        flops=1 << 27,
    )
    grad_proj, grad_first, grad_second, grad_mask = call(
        finish_kernel,
        (
            shape((chans, features), F32),
            shape((4, 4, chans, chans), F32),
            shape((4, bands, 4, chans), F32),
            shape((features,), F32),
        ),
        (summed, other, proj),
        flops=1 << 20,
    )
    return (token_grad[None, None], grad_proj.T, grad_first, grad_second.transpose(0, 2, 1, 3), grad_mask)


def solution(mesh):
    return jax.shard_map(
        functools.partial(per_device, mesh.shape["ew"], mesh.shape["ns"]),
        mesh=mesh,
        in_specs=(
            P("ns", "ew", None, None, None),
            P("ns", "ew", None, None),
            P("ns", "ew", None),
            P("ns", "ew", None, None, None),
            P(),
            P(),
            P(),
            P(),
            P(None, None, "ns", "ew"),
            P(None, None, "ns", "ew"),
        ),
        out_specs=(P("ns", "ew", None, None), P(), P(), P(), P()),
        check_vma=False,
    )
```

```python
import functools

import jax
import jax.numpy as jnp
import numpy as np
from jax import lax
from jax.experimental import pallas as pl
from jax.experimental.pallas import tpu as pltpu
from jax.sharding import PartitionSpec as P

BF = jnp.bfloat16
F32 = jnp.float32
VMEM = pl.BlockSpec(memory_space=pltpu.VMEM)
GROUP = 16
GRAD_ROWS = 1024
PROJ_AT = 512
SECOND_AT = 896
MASK_ROW = SECOND_AT + 12


def nn(a, b):
    return lax.dot_general(a, b, (((1,), (0,)), ((), ())), preferred_element_type=F32)


def nt(a, b):
    return lax.dot_general(a, b, (((1,), (1,)), ((), ())), preferred_element_type=F32)


def tn(a, b):
    return lax.dot_general(a, b, (((0,), (0,)), ((), ())), preferred_element_type=F32)


def iota(shape, dim):
    return lax.broadcasted_iota(jnp.int32, shape, dim)


def hidden_columns(cols, lanes):
    lane = lax.rem(lanes, cols)
    right = lane >= cols // 2
    own = 2 * jnp.where(right, lane - cols // 2, lane) + jnp.where(right, 1, 0)
    shifted = own + jnp.where(right, -2, 2)
    return jnp.where(lax.rem(lanes // cols, 2) == 0, own, shifted)


def table_kernel(pix_ref, cell_ref, pick_ref):
    cols = cell_ref.shape[0] // 2
    column_tables(cols, pix_ref, cell_ref)
    pick_g, pick_p = edge_tables(2 * cols, cols)
    pick_ref[:, : 2 * cols] = pick_g
    pick_ref[:, 2 * cols :] = pick_p


def column_tables(cols, pix_ref, cell_ref):
    fine = 2 * cols
    lanes = iota((1, fine), 1)
    hidden = hidden_columns(cols, lanes)
    for tap in range(4):
        pixel = 2 * hidden + tap - 1
        pixel = jnp.where(pixel < 0, fine + 6 + pixel, pixel)
        table = iota((fine + 128, fine), 0) == pixel
        pix_ref[:, tap * fine : (tap + 1) * fine] = table.astype(F32).astype(BF)
    cell = jnp.where(hidden < 0, cols + 1, hidden)
    cell_ref[...] = (iota((fine, fine), 0) == cell).astype(F32).astype(BF)


def spread(ref, wide, group):
    frames, real, rows, cols = ref.shape
    for f in range(frames):
        for o in range(group):
            value = ref[f, o].astype(F32) if o < real else jnp.zeros((rows, cols), F32)
            for h in range(cols // 128):
                wide[pl.ds(((h * frames + f) * group + o) * rows, rows), :] = value[:, h * 128 : (h + 1) * 128]


def gathered(wide, h, frames, group, rows, f, r):
    return wide[pl.ds((h * frames + f) * group * rows + r, group, stride=rows), :].astype(BF)


def edge_tables(pcol, cols):
    row, col = iota((16, pcol), 0), iota((16, pcol), 1)
    pick_g = ((row < 3) & (col == row)) | ((row >= 3) & (row < 6) & (col == row + pcol - 6))
    row, col = iota((16, cols), 0), iota((16, cols), 1)
    pick_p = ((row == 6) & (col == 0)) | ((row == 7) & (col == cols - 1))
    return pick_g.astype(F32).astype(BF), pick_p.astype(F32).astype(BF)


def layout_kernel(pick_ref, pre_ref, cot_ref, p_ref, g_ref, own_ref, pre_wide, cot_wide):
    frames, chans, rows, cols = pre_ref.shape
    prow, pcol = cot_ref.shape[2:]
    spread(pre_ref, pre_wide, chans)
    for r in range(rows):
        for f in range(frames):
            p_ref[pl.ds((r * frames + f) * chans, chans), :] = gathered(pre_wide, 0, frames, chans, rows, f, r)
    spread(cot_ref, cot_wide, GROUP)
    for f in range(frames):
        for y in range(prow):
            for h in range(pcol // 128):
                g_ref[pl.ds((f * prow + y) * GROUP, GROUP), h * 128 : (h + 1) * 128] = gathered(
                    cot_wide, h, frames, GROUP, prow, f, y
                )
    below = nt(pick_ref[:, pcol:], p_ref[...])[:8]
    line = frames * chans
    last = (rows - 1) * line
    below = jnp.concatenate([below[:, :line], below[:, last:], below[:, line:last]], axis=1)
    edges = nt(pick_ref[:, :pcol], g_ref[...])[:8]
    width = edges.shape[1]
    own_ref[...] = jnp.concatenate([edges + below[:, :width], below[:, width:]], axis=1).astype(BF)


def row_messages(g_ref, p_ref, ga_ref, pa_ref, gb_ref, pb_ref):
    deep, pcol = ga_ref.shape[0], g_ref.shape[1]
    chans, cols = pa_ref.shape[0], p_ref.shape[1]
    frames = pa_ref.shape[1] // cols
    tall = g_ref.shape[0] // frames
    high = p_ref.shape[0]

    def message(g_out, p_out, top):
        for f in range(frames):
            at = f * tall if top else (f + 1) * tall - deep
            g_out[:, f * pcol : (f + 1) * pcol] = g_ref[pl.ds(at, deep), :]
            at = f * chans if top else high - (frames - f) * chans
            p_out[:, f * cols : (f + 1) * cols] = p_ref[pl.ds(at, chans), :]

    even = lax.rem(lax.axis_index("ns"), 2) == 0

    @pl.when(even)
    def _():
        message(ga_ref, pa_ref, False)
        message(gb_ref, pb_ref, True)

    @pl.when(jnp.logical_not(even))
    def _():
        message(ga_ref, pa_ref, True)
        message(gb_ref, pb_ref, False)


def local_kernel(
    capacity, counts_ref, g_ref, p_ref, vis_ref, owners_ref, tokens_ref, mask_ref, proj_ref, first_ref, second_ref,
    ga_ref, pa_ref, gb_ref, pb_ref, grid_ref, pick_ref, hidden_ref, route_ref, wab_ref, w2_ref,
):
    row_messages(g_ref, p_ref, ga_ref, pa_ref, gb_ref, pb_ref)
    slots_all = tokens_ref.shape[0]
    frames, slots, patches = pick_ref.shape
    chans = proj_ref.shape[0]
    bands = second_ref.shape[1]
    slot_rows = -(-capacity // 8) * 8
    owners = route_ref.shape[0] // slot_rows
    eye = (iota((chans, chans), 0) == iota((chans, chans), 1)).astype(BF)
    pad = jnp.zeros((GROUP - bands, chans), F32)
    taps = []
    for b in range(4):
        for a in range(4):
            here = iota((bands, 4, chans), 1) == b
            tap = jnp.sum(jnp.where(here, second_ref[a].astype(F32), 0.0), axis=1)
            taps.append(jnp.concatenate([tap, pad], axis=0).astype(BF))
    w2_ref[...] = nt(eye, jnp.concatenate(taps, axis=0)).astype(BF)
    left = (iota((2 * chans, chans), 0) == iota((2 * chans, chans), 1)).astype(BF)
    right = (iota((2 * chans, chans), 0) == iota((2 * chans, chans), 1) + chans).astype(BF)
    for arrangement, (lo, hi) in enumerate(((1, 2), (3, 0))):
        taps_lo = jnp.concatenate([first_ref[a, lo] for a in range(4)], axis=0)
        taps_hi = jnp.concatenate([first_ref[a, hi] for a in range(4)], axis=0)
        wab_ref[:, arrangement * 4 * chans : (arrangement + 1) * 4 * chans] = (
            nt(left, taps_lo) + nt(right, taps_hi)
        ).astype(BF)
    vis = jnp.concatenate([vis_ref[f : f + 1, :] for f in range(frames)], axis=1)
    owner = jnp.concatenate([owners_ref[f] for f in range(frames)], axis=1)
    slot = iota((1, slots_all), 1)
    live = jnp.zeros((1, slots_all), jnp.int32)
    for f in range(frames):
        inside = (slot >= f * slots) & (slot < f * slots + counts_ref[:, f : f + 1])
        live = jnp.where(inside, 1, live)
    wanted = jnp.where(live > 0, vis, patches)
    square = (slots_all, slots_all)
    column = jnp.sum(
        jnp.where(iota(square, 0) == iota(square, 1), wanted.astype(F32), 0.0), axis=1, keepdims=True
    ).astype(jnp.int32)
    token_proj = nt(tokens_ref[...], proj_ref[...]).astype(BF)
    features = mask_ref.shape[0]
    mask_row = mask_ref[...].astype(F32).reshape(1, features)
    mask_proj = nt(jnp.broadcast_to(mask_row, (16, features)).astype(BF), proj_ref[...]).astype(BF)
    row0 = iota((16, patches), 0) == 0
    lane = iota((chans, 2 * chans), 1)
    for f in range(frames):
        hits = iota((slots, patches), 1) == column[f * slots : (f + 1) * slots]
        picks = hits.astype(F32)
        pick_ref[f] = picks.astype(BF)
        unseen = jnp.where(row0, 1.0 - jnp.sum(picks, axis=0, keepdims=True), 0.0).astype(BF)
        hidden_ref[:, f * patches : (f + 1) * patches] = unseen
        grid = tn(token_proj[f * slots : (f + 1) * slots], picks.astype(BF)) + tn(mask_proj, unseen)
        zero = jnp.zeros((chans, 2 * chans), F32)
        for line, (group, half_at) in enumerate(((1, 0), (0, 0), (0, 1), (1, 1))):
            pair = line // 2 * 2 * chans
            straight = grid[:, pair : pair + 2 * chans]
            turned = pltpu.roll(straight, chans, 1)
            to_left, to_right = (straight, turned) if line % 2 == 0 else (turned, straight)
            at = half_at * 2 * chans
            grid_ref[f, group, :chans, at : at + 2 * chans] = jnp.where(lane < chans, to_left, zero).astype(BF)
            grid_ref[f, group, chans:, at : at + 2 * chans] = jnp.where(lane < chans, zero, to_right).astype(BF)
    own_rows = -(-owners // 16) * 16
    hit = (iota((own_rows, slots_all), 0) == jnp.where(live > 0, owner, -1)).astype(F32)
    before = (iota(square, 0) < iota(square, 1)).astype(BF)
    earlier = nn(hit.astype(BF), before)
    place = jnp.sum(earlier * hit, axis=0, keepdims=True).astype(jnp.int32)
    block = lax.rem(owner, 2) * (owners // 2) + owner // 2
    target = jnp.where(live > 0, block * slot_rows + place, -1)
    route = (iota((owners * slot_rows, slots_all), 0) == target).astype(F32).astype(BF)
    for f in range(frames):
        route_ref[:, f * patches : (f + 1) * patches] = nn(
            route[:, f * slots : (f + 1) * slots], pick_ref[f]
        ).astype(BF)


def side_columns(ea_ref, eb_ref, even_ew):
    ea, eb = ea_ref[...].astype(F32), eb_ref[...].astype(F32)
    return jnp.concatenate([jnp.where(even_ew, ea, eb), jnp.where(even_ew, eb, ea)], axis=0).astype(BF)


def halo_tables():
    row, col = iota((16, 128), 0), iota((16, 128), 1)
    pick_g = ((row < 3) & (col == row)) | ((row >= 11) & (row < 14) & (col == row - 8))
    pick_p = ((row == 6) & (col == 0)) | ((row == 15) & (col == 1))
    return pick_g.astype(F32).astype(BF), pick_p.astype(F32).astype(BF)


def second_backward(taps, pre, w2, drop):
    grad_hidden = nn(w2, jnp.concatenate(taps, axis=0))
    s = 0.5 + 0.5 * jnp.tanh(0.851 * pre)
    delta = grad_hidden * (s + 1.702 * pre * s * (1.0 - s))
    cols = pre.shape[1] // 2
    return jnp.where(drop, 0.0, delta).astype(BF), (pre[:, :cols] * s[:, :cols]).astype(BF)


def second_kernel_term(taps, hid):
    cols = hid.shape[1]
    zero = jnp.zeros_like(hid)
    lhs = jnp.concatenate(
        [
            jnp.concatenate([taps[0][:, :cols], taps[2][:, :cols]], axis=1),
            jnp.concatenate([taps[1][:, :cols], taps[3][:, :cols]], axis=1),
        ],
        axis=0,
    )
    rhs = jnp.concatenate(
        [jnp.concatenate([hid, zero], axis=1), jnp.concatenate([zero, hid], axis=1)], axis=0
    )
    return nt(lhs, rhs)


def outside_columns(chans, cols, n_ew, ew):
    lane = iota((chans, 2 * cols), 1)
    return ((lane == cols + cols // 2 - 1) & (ew == n_ew - 1)) | ((lane == cols + cols // 2) & (ew == 0))


def window_taps(wins, at, cols):
    return [wins[pl.ds(at, 4 * GROUP), b * 2 * cols : (b + 1) * 2 * cols] for b in range(4)]


def message_kernel(sb_ref, sa_ref, ga_ref, pa_ref, gb_ref, pb_ref, a_ref, b_ref):
    deep, span = ga_ref.shape
    corners = jnp.concatenate([sa_ref[:, :span].astype(F32), sb_ref[:, :span].astype(F32)], axis=0).astype(BF)
    for out, g, p in ((a_ref, ga_ref, pa_ref), (b_ref, gb_ref, pb_ref)):
        out[:deep, :span] = g[...]
        out[deep:, :span] = corners
        out[:, span:] = p[...]


def inner_kernel(
    n_ew, eb_ref, ea_ref, g_ref, p_ref, pix_ref, cell_ref, grid_ref, wab_ref, w2_ref,
    delta_ref, second_ref, first_ref, turn_ref, edge_ref, pre_ref, ext, wide, wins, pres,
):
    frames = grid_ref.shape[0]
    chans = w2_ref.shape[0]
    pcol, cols = g_ref.shape[1], p_ref.shape[1]
    tall = g_ref.shape[0] // frames
    rows = p_ref.shape[0] // (frames * chans)
    ew = lax.axis_index("ew")
    sides = side_columns(ea_ref, eb_ref, lax.rem(ew, 2) == 0)
    pick_g, pick_p = halo_tables()
    line = frames * chans
    ext[:, :pcol] = g_ref[...]
    ext[:, pcol:] = tn(sides[:, : frames * tall], pick_g).astype(BF)
    wide[:, :cols] = p_ref[...]
    halo = tn(sides, pick_p).astype(BF)
    wide[pl.ds(0, line), cols:] = halo[:line]
    wide[pl.ds((rows - 1) * line, line), cols:] = halo[line : 2 * line]
    wide[pl.ds(line, (rows - 2) * line), cols:] = halo[2 * line :]
    deep = 3 * GROUP
    for f in range(frames):
        block = ext[pl.ds(f * tall, tall), :]
        for b in range(4):
            lanes = slice(b * 2 * cols, (b + 1) * 2 * cols)
            wins[pl.ds(f * tall, tall), lanes] = nn(block, pix_ref[:, lanes]).astype(BF)
        edge_ref[f, 0] = wins[pl.ds(f * tall, deep), :]
        edge_ref[f, 1] = wins[pl.ds((f + 1) * tall - deep, deep), :]
    pres[...] = nn(wide[...], cell_ref[...])
    for f in range(frames):
        pre_ref[f, 0] = pres[pl.ds(f * chans, chans), :]
        pre_ref[f, 1] = pres[pl.ds((rows - 1) * line + f * chans, chans), :]
    w2 = w2_ref[...]
    wab = wab_ref[...]
    drop = outside_columns(chans, cols, n_ew, ew)
    grad_second = grad_first = None
    for f in range(frames):
        deltas = []
        for i in range(1, rows - 1):
            taps = window_taps(wins, f * tall + (2 * i - 1) * GROUP, cols)
            pre = pres[pl.ds(i * line + f * chans, chans), :]
            delta, hid = second_backward(taps, pre, w2, drop)
            deltas.append(delta)
            term = second_kernel_term(taps, hid)
            grad_second = term if grad_second is None else grad_second + term
        count = rows - 2
        for k, i in enumerate((0, 1, count - 2, count - 1)):
            delta_ref[pl.ds((f * 4 + k) * chans, chans), :] = deltas[i]
        cells = []
        for i in (0, 2):
            slab = jnp.concatenate(deltas[i : i + 4], axis=0)
            cells.append(jnp.concatenate([slab[:, :cols], slab[:, cols:]], axis=0))
        both = jnp.concatenate(cells, axis=1)
        term = nt(both, grid_ref[f, 0])
        grad_first = term if grad_first is None else grad_first + term
        turn_ref[f] = nn(wab, both)
    second_ref[...] = grad_second
    first_ref[...] = grad_first


def outer_kernel(
    n_ew, n_ns, rb_ref, ra_ref, pix_ref, cell_ref,
    delta_ref, second_ref, first_ref, turn_ref, edge_ref, pre_ref,
    grid_ref, pick_ref, hidden_ref, route_ref, wab_ref, w2_ref, tokens_ref, mask_ref,
    keep_ref, give_ref, ext, wide, wins, pres,
):
    frames, slots, patches = pick_ref.shape
    chans = w2_ref.shape[0]
    features = tokens_ref.shape[1]
    cols = pre_ref.shape[3] // 2
    pcol = 2 * cols
    deep = 3 * GROUP
    ns = lax.axis_index("ns")
    ew = lax.axis_index("ew")
    even_ns = lax.rem(ns, 2) == 0
    even_ew = lax.rem(ew, 2) == 0
    ra, rb = ra_ref[...], rb_ref[...]
    north = jnp.where(even_ns, rb, ra)
    south = jnp.where(even_ns, ra, rb)
    span = frames * pcol
    tall = span // frames

    def far_sides(message):
        a, b = message[deep : deep + 8, :span].astype(F32), message[deep + 8 :, :span].astype(F32)
        return jnp.concatenate([jnp.where(even_ew, a, b), jnp.where(even_ew, b, a)], axis=0).astype(BF)

    pick_g, pick_p = halo_tables()
    line = frames * chans
    far = (far_sides(north), far_sides(south))
    for low in range(2):
        message = south if low else north
        halo_p = tn(far[low][:, (1 - low) * line : (2 - low) * line], pick_p).astype(BF)
        for f in range(frames):
            at = (f * 2 + low) * deep
            ext[pl.ds(at, deep), :pcol] = message[:deep, f * pcol : (f + 1) * pcol]
            if low:
                ext[pl.ds(at, deep), pcol:] = tn(far[low][:, f * tall : f * tall + 128], pick_g).astype(BF)[:deep]
            else:
                end = (f + 1) * tall
                ext[pl.ds(at, deep), pcol:] = tn(far[low][:, end - 128 : end], pick_g).astype(BF)[128 - deep :]
            at = (f * 2 + low) * chans
            wide[pl.ds(at, chans), :cols] = message[:, span + f * cols : span + (f + 1) * cols]
            wide[pl.ds(at, chans), cols:] = halo_p[f * chans : (f + 1) * chans]
    block = ext[...]
    for b in range(4):
        lanes = slice(b * 2 * cols, (b + 1) * 2 * cols)
        wins[:, lanes] = nn(block, pix_ref[:, lanes]).astype(BF)
    pres[...] = nn(wide[...], cell_ref[...])
    w2 = w2_ref[...]
    wab = wab_ref[...]
    drop = outside_columns(chans, cols, n_ew, ew)
    grad_second = second_ref[...]
    grad_first = first_ref[...]
    half_lane = iota((chans, cols), 1) < cols // 2
    grids = []
    for f in range(frames):
        cells = []
        for low in range(2):
            pair = []
            for k in range(2):
                inside = k == 1 - low
                beyond = wins[pl.ds((f * 2 + low) * deep, deep), :]
                window = [edge_ref[f, low], beyond] if low else [beyond, edge_ref[f, low]]
                window = jnp.concatenate(window, axis=0)[k * 2 * GROUP : (k * 2 + 4) * GROUP]
                taps = [window[:, b * 2 * cols : (b + 1) * 2 * cols] for b in range(4)]
                pre = pre_ref[f, low] if inside else pres[pl.ds((f * 2 + low) * chans, chans), :]
                gone = drop if inside else drop | (ns == (n_ns - 1 if low else 0))
                delta, hid = second_backward(taps, pre, w2, gone)
                pair.append(delta)
                if inside:
                    grad_second = grad_second + second_kernel_term(taps, hid)
            kept = delta_ref[pl.ds((f * 4 + 2 * low) * chans, 2 * chans), :]
            slab = jnp.concatenate([kept, *pair] if low else [*pair, kept], axis=0)
            cells.append(jnp.concatenate([slab[:, :cols], slab[:, cols:]], axis=0))
        both = jnp.concatenate(cells, axis=1)
        grad_first = grad_first + nt(both, grid_ref[f, 1])
        edge = nn(wab, both)
        inner = turn_ref[f]
        parts = []
        for even, odd in ((edge[:, :cols], inner[:, :cols]), (inner[:, cols:], edge[:, cols:])):
            here = jnp.where(half_lane, even[:chans], odd[chans:])
            there = jnp.where(half_lane, odd[:chans], even[chans:])
            parts.append(here + pltpu.roll(there, cols // 2, 1))
        grids.append(jnp.concatenate(parts, axis=1).astype(BF))
    none = jnp.zeros((chans, patches), BF)
    mask_sum = nt(hidden_ref[...], jnp.concatenate(grids, axis=1))
    chosen = [nt(pick_ref[f], jnp.concatenate([grids[f], none], axis=0)) for f in range(frames)]
    chosen = jnp.concatenate(chosen, axis=0)
    chosen = chosen.astype(BF)
    grid = jnp.concatenate(grids, axis=1)
    blank = jnp.zeros_like(grid)
    placed = [jnp.where(even_ns, grid, blank), jnp.where(even_ns, blank, grid)]
    routed = nt(route_ref[...], jnp.concatenate(placed, axis=0))
    hi = mask_sum.astype(BF).astype(F32)
    lo = mask_sum - hi
    line = iota(hi.shape, 0)
    mask_rows = jnp.where(line == 0, hi[0:1], jnp.where(line == 1, lo[0:1], 0.0)).astype(BF)
    line = iota((16, features), 0)
    mask_row = mask_ref[...].astype(F32).reshape(1, features)
    spread_row = jnp.where(line < 2, mask_row, 0.0).astype(BF)
    grad_proj = tn(chosen[:, :chans], tokens_ref[...]) + tn(mask_rows, spread_row)
    grad_proj = [grad_proj[:, k * 128 : (k + 1) * 128] for k in range(features // 128)]
    both = jnp.concatenate([hi[0:1], lo[0:1]], axis=1)
    mark = iota(grad_second.shape, 0) == MASK_ROW - SECOND_AT
    grad_second = jnp.where(mark, both, grad_second)
    halves = (grad_first, jnp.concatenate([*grad_proj, grad_second], axis=0))
    part = routed.shape[0] // 2

    def split(mine):
        keep_ref[: GRAD_ROWS // 2, :] = halves[mine]
        keep_ref[GRAD_ROWS // 2 :, :] = routed[mine * part : (mine + 1) * part]
        give_ref[: GRAD_ROWS // 2, :] = halves[1 - mine].astype(BF)
        give_ref[GRAD_ROWS // 2 :, :] = routed[(1 - mine) * part : (2 - mine) * part].astype(BF)

    @pl.when(even_ns)
    def _():
        split(0)

    @pl.when(jnp.logical_not(even_ns))
    def _():
        split(1)


def chip_kernel(rows_each, keep_ref, got_ref, out_ref):
    count = out_ref.shape[0]
    slot_rows = out_ref.shape[1] - rows_each
    grads = GRAD_ROWS // 2
    chips = (keep_ref.shape[0] - grads) // slot_rows
    total = (keep_ref[...] + got_ref[...].astype(F32)).astype(BF)
    full = min(count, grads // rows_each)
    for d in range(full):
        out_ref[d, :rows_each, :] = total[d * rows_each : (d + 1) * rows_each]
    if full < count:

        @pl.loop(full, count)
        def _(d):
            out_ref[d, :rows_each, :] = jnp.zeros((rows_each, total.shape[1]), BF)

    for z in range(chips):
        rows = total[grads + z * slot_rows : grads + (z + 1) * slot_rows]
        for e in range(count // chips):
            out_ref[e * chips + z, rows_each:, :] = rows


def sum_kernel(rows_each, got_ref, sum_ref):
    count = got_ref.shape[0]
    if count <= 64:
        total = got_ref[0, :rows_each, :].astype(F32)
        for d in range(1, count):
            total = total + got_ref[d, :rows_each, :].astype(F32)
    else:
        total = lax.fori_loop(
            0,
            count,
            lambda d, acc: acc + got_ref[d, :rows_each, :].astype(F32),
            jnp.zeros((rows_each, got_ref.shape[2]), F32),
        )
    share = total.astype(BF)
    if count <= 64:
        for d in range(count):
            sum_ref[d] = share
    else:

        @pl.loop(0, count)
        def _(d):
            sum_ref[d] = share


def owner_kernel(capacity, rows_each, arrived_ref, proj_ref, token_ref):
    chans = proj_ref.shape[0]
    slot_rows = arrived_ref.shape[1] - rows_each
    chips = token_ref.shape[0] // (2 * capacity)
    ew = lax.axis_index("ew")
    arrived = [arrived_ref[ew * chips + z, rows_each:, :].astype(F32) for z in range(chips)]
    arrived = jnp.concatenate(arrived, axis=0).astype(BF)
    shape = (token_ref.shape[0], chips * slot_rows)
    row, col = iota(shape, 0), iota(shape, 1)
    source = (row // (2 * capacity)) * slot_rows + lax.rem(row, capacity)
    picked = nn((source == col).astype(F32).astype(BF), arrived)
    second = lax.rem(iota(picked.shape, 0) // capacity, 2) == 1
    picked = jnp.where(second, pltpu.roll(picked, chans, 1), picked)[:, :chans].astype(BF)
    token_ref[...] = nn(picked, proj_ref[...]).astype(BF)


def finish_kernel(mine_ref, other_ref, proj_ref, proj_out, first_out, second_out, mask_out):
    chans, features = proj_ref.shape
    bands = second_out.shape[1]
    rows_each = mine_ref.shape[1]
    blocks = range(GRAD_ROWS // 2 // rows_each)
    mine = jnp.concatenate([mine_ref[d] for d in blocks], axis=0)
    other = jnp.concatenate([other_ref[d] for d in blocks], axis=0)
    even = lax.rem(lax.axis_index("ns"), 2) == 0
    total = [jnp.where(even, mine, other), jnp.where(even, other, mine)]
    total = jnp.concatenate(total, axis=0).astype(F32)
    for arrangement, taps in enumerate(((1, 2), (3, 0))):
        rows = total[arrangement * 4 * chans : (arrangement + 1) * 4 * chans]
        turned = pltpu.roll(rows, chans, 1)
        for a in range(4):
            first_out[a, taps[0]] = rows[a * chans : (a + 1) * chans, :chans]
            first_out[a, taps[1]] = turned[a * chans : (a + 1) * chans, :chans]
    for k in range(features // 128):
        at = PROJ_AT + k * chans
        proj_out[:, k * 128 : (k + 1) * 128] = total[at : at + chans]
    rows = total[SECOND_AT:]
    turned = pltpu.roll(rows, chans, 1)
    for b in range(2):
        for a in range(4):
            at = (b * 4 + a) * GROUP
            second_out[a, :, b, :] = rows[at : at + bands, :chans]
            second_out[a, :, b + 2, :] = turned[at : at + bands, :chans]
    at = MASK_ROW - SECOND_AT
    mask_sum = rows[at : at + 1, :chans] + turned[at : at + 1, :chans]
    hi = mask_sum.astype(BF).astype(F32)
    mid = (mask_sum - hi).astype(BF).astype(F32)
    lo = mask_sum - hi - mid
    line = iota((16, chans), 0)
    split = jnp.where(line == 0, hi, jnp.where(line == 1, mid, jnp.where(line == 2, lo, 0.0)))
    grad_mask = jnp.sum(nn(split.astype(BF), proj_ref[...]), axis=0, keepdims=True)
    mask_out[...] = grad_mask.reshape(features)


def swap(block, axis, offset):
    count = lax.axis_size(axis)
    pairs = [(i, ((i + offset) ^ 1) - offset) for i in range(count)]
    return lax.ppermute(block, axis, [(i, j) for i, j in pairs if 0 <= j < count])


def call(kernel, outs, args, scratch=(), flops=0, limit=8 << 20):
    return pl.pallas_call(
        kernel,
        out_shape=outs,
        in_specs=[VMEM] * len(args),
        out_specs=jax.tree.map(lambda _: VMEM, outs),
        scratch_shapes=list(scratch),
        compiler_params=pltpu.CompilerParams(vmem_limit_bytes=limit),
        cost_estimate=pl.CostEstimate(flops=flops, bytes_accessed=1 << 10, transcendentals=0),
    )(*args)


def per_device(
    n_ew, n_ns, tokens, vis_index, counts, owners, mask_token, proj_weight, up_first, up_second, saved_pre, cotangent
):
    frames, slots, features = tokens.shape[2:]
    _, chans, rows, cols = saved_pre.shape
    bands, prow, pcol = cotangent.shape[1:]
    patches = rows * cols // 4
    count = n_ew * n_ns
    capacity = 3 * frames * slots // (2 * n_ns)
    rows_each = -(-GRAD_ROWS // count)
    rows_each = -(-rows_each // 16) * 16
    slot_rows = -(-capacity // 8) * 8
    groups = [[e * n_ns + z * 2 + c for e in range(n_ew) for z in range(n_ns // 2)] for c in range(2)]
    slots_all = frames * slots
    shape = jax.ShapeDtypeStruct

    tall = prow * GROUP
    pixels, cells, edge_picks = call(
        table_kernel,
        (shape((pcol + 128, 4 * pcol), BF), shape((pcol, pcol), BF), shape((16, pcol + cols), BF)),
        (),
        flops=1 << 33,
    )
    own_p, own_g, own_edges = call(
        layout_kernel,
        (
            shape((frames * rows * chans, cols), BF),
            shape((frames * tall, pcol), BF),
            shape((8, frames * rows * chans), BF),
        ),
        (edge_picks, saved_pre, cotangent),
        [
            pltpu.VMEM((frames * chans * rows + rows, cols), F32),
            pltpu.VMEM((frames * tall * pcol // 128 + prow, 128), F32),
        ],
        flops=1 << 33,
    )
    side_b = swap(own_edges, "ew", 1)
    side_a = swap(own_edges, "ew", 0)

    tile_tokens = tokens.reshape(slots_all, features)
    proj = proj_weight.T
    g_message = shape((3 * GROUP, frames * pcol), BF)
    p_message = shape((chans, frames * cols), BF)
    g_a, p_a, g_b, p_b, grid, picks, hidden, route, wab, w2 = call(
        functools.partial(local_kernel, capacity),
        (
            g_message,
            p_message,
            g_message,
            p_message,
            shape((frames, 2, 2 * chans, 2 * cols), BF),
            shape((frames, slots, patches), BF),
            shape((16, frames * patches), BF),
            shape((n_ns * slot_rows, frames * patches), BF),
            shape((2 * chans, 8 * chans), BF),
            shape((chans, 16 * GROUP), BF),
        ),
        (
            counts.reshape(1, frames),
            own_g,
            own_p,
            vis_index.reshape(frames, slots),
            owners.reshape(frames, 1, slots),
            tile_tokens,
            mask_token,
            proj,
            up_first,
            up_second.transpose(0, 2, 1, 3),
        ),
        flops=1 << 24,
    )
    message_shape = shape((3 * GROUP + 16, frames * (pcol + cols)), BF)
    send_a, send_b = call(
        message_kernel,
        (message_shape, message_shape),
        (side_b, side_a, g_a, p_a, g_b, p_b),
        flops=1 << 20,
    )
    got_b = swap(send_b, "ns", 1)
    got_a = swap(send_a, "ns", 0)

    delta_mid, second_mid, first_mid, turn_mid, edge_wins, edge_pre = call(
        functools.partial(inner_kernel, n_ew),
        (
            shape((frames * 4 * chans, 2 * cols), BF),
            shape((2 * 4 * GROUP, 2 * chans), F32),
            shape((8 * chans, 2 * chans), F32),
            shape((frames, 2 * chans, 2 * cols), F32),
            shape((frames, 2, 3 * GROUP, 8 * cols), BF),
            shape((frames, 2, chans, 2 * cols), F32),
        ),
        (side_b, side_a, own_g, own_p, pixels, cells, grid, wab, w2),
        [
            pltpu.VMEM((frames * tall, pcol + 128), BF),
            pltpu.VMEM((rows * frames * chans, 2 * cols), BF),
            pltpu.VMEM((frames * tall, 8 * cols), BF),
            pltpu.VMEM((rows * frames * chans, 2 * cols), F32),
        ],
        flops=1 << 27,
        limit=16 << 20,
    )
    beyond = frames * 2 * 3 * GROUP
    half_rows = GRAD_ROWS // 2 + n_ns // 2 * slot_rows
    keep, give = call(
        functools.partial(outer_kernel, n_ew, n_ns),
        (shape((half_rows, 2 * chans), F32), shape((half_rows, 2 * chans), BF)),
        (
            got_b, got_a, pixels, cells, delta_mid, second_mid, first_mid, turn_mid, edge_wins, edge_pre,
            grid, picks, hidden, route, wab, w2, tile_tokens, mask_token,
        ),
        [
            pltpu.VMEM((beyond, pcol + 128), BF),
            pltpu.VMEM((frames * 2 * chans, 2 * cols), BF),
            pltpu.VMEM((beyond, 8 * cols), BF),
            pltpu.VMEM((frames * 2 * chans, 2 * cols), F32),
        ],
        flops=1 << 27,
        limit=24 << 20,
    )

    def exchange(blocks):
        return lax.all_to_all(blocks, ("ew", "ns"), 0, 0, axis_index_groups=groups, tiled=True)

    outgoing = call(
        functools.partial(chip_kernel, rows_each),
        shape((count // 2, rows_each + slot_rows, 2 * chans), BF),
        (keep, swap(give, "ns", 0)),
        flops=1 << 20,
    )
    arrived = exchange(outgoing)
    shares = call(
        functools.partial(sum_kernel, rows_each),
        shape((count // 2, rows_each, 2 * chans), BF),
        (arrived,),
        flops=1 << 20,
    )
    summed = exchange(shares)[: GRAD_ROWS // 2 // rows_each]
    other = swap(summed, "ns", 0)
    token_grad = call(
        functools.partial(owner_kernel, capacity, rows_each),
        shape((n_ns * capacity, features), BF),
        (arrived, proj),
        flops=1 << 27,
    )
    grad_proj, grad_first, grad_second, grad_mask = call(
        finish_kernel,
        (
            shape((chans, features), F32),
            shape((4, 4, chans, chans), F32),
            shape((4, bands, 4, chans), F32),
            shape((features,), F32),
        ),
        (summed, other, proj),
        flops=1 << 20,
    )
    return (token_grad[None, None], grad_proj.T, grad_first, grad_second.transpose(0, 2, 1, 3), grad_mask)


def solution(mesh):
    return jax.shard_map(
        functools.partial(per_device, mesh.shape["ew"], mesh.shape["ns"]),
        mesh=mesh,
        in_specs=(
            P("ns", "ew", None, None, None),
            P("ns", "ew", None, None),
            P("ns", "ew", None),
            P("ns", "ew", None, None, None),
            P(),
            P(),
            P(),
            P(),
            P(None, None, "ns", "ew"),
            P(None, None, "ns", "ew"),
        ),
        out_specs=(P("ns", "ew", None, None), P(), P(), P(), P()),
        check_vma=False,
    )
```

```python
import functools

import jax
import jax.numpy as jnp
import numpy as np
from jax import lax
from jax.experimental import pallas as pl
from jax.experimental.pallas import tpu as pltpu
from jax.sharding import PartitionSpec as P

BF = jnp.bfloat16
F32 = jnp.float32
VMEM = pl.BlockSpec(memory_space=pltpu.VMEM)
GROUP = 16
GRAD_ROWS = 1024
PROJ_AT = 512
SECOND_AT = 896
MASK_ROW = SECOND_AT + 12


def nn(a, b):
    return lax.dot_general(a, b, (((1,), (0,)), ((), ())), preferred_element_type=F32)


def nt(a, b):
    return lax.dot_general(a, b, (((1,), (1,)), ((), ())), preferred_element_type=F32)


def tn(a, b):
    return lax.dot_general(a, b, (((0,), (0,)), ((), ())), preferred_element_type=F32)


def iota(shape, dim):
    return lax.broadcasted_iota(jnp.int32, shape, dim)


def hidden_columns(cols, lanes):
    lane = lax.rem(lanes, cols)
    right = lane >= cols // 2
    own = 2 * jnp.where(right, lane - cols // 2, lane) + jnp.where(right, 1, 0)
    shifted = own + jnp.where(right, -2, 2)
    return jnp.where(lax.rem(lanes // cols, 2) == 0, own, shifted)


def table_kernel(pix_ref, cell_ref, pick_ref):
    cols = cell_ref.shape[0] // 2
    column_tables(cols, pix_ref, cell_ref)
    pick_g, pick_p = edge_tables(2 * cols, cols)
    pick_ref[:, : 2 * cols] = pick_g
    pick_ref[:, 2 * cols :] = pick_p


def column_tables(cols, pix_ref, cell_ref):
    fine = 2 * cols
    lanes = iota((1, fine), 1)
    hidden = hidden_columns(cols, lanes)
    for tap in range(4):
        pixel = 2 * hidden + tap - 1
        pixel = jnp.where(pixel < 0, fine + 6 + pixel, pixel)
        table = iota((fine + 128, fine), 0) == pixel
        pix_ref[:, tap * fine : (tap + 1) * fine] = table.astype(F32).astype(BF)
    cell = jnp.where(hidden < 0, cols + 1, hidden)
    cell_ref[...] = (iota((fine, fine), 0) == cell).astype(F32).astype(BF)


def spread(ref, wide, group):
    frames, real, rows, cols = ref.shape
    for f in range(frames):
        for o in range(group):
            value = ref[f, o].astype(F32) if o < real else jnp.zeros((rows, cols), F32)
            for h in range(cols // 128):
                wide[pl.ds(((h * frames + f) * group + o) * rows, rows), :] = value[:, h * 128 : (h + 1) * 128]


def gathered(wide, h, frames, group, rows, f, r):
    return wide[pl.ds((h * frames + f) * group * rows + r, group, stride=rows), :].astype(BF)


def edge_tables(pcol, cols):
    row, col = iota((16, pcol), 0), iota((16, pcol), 1)
    pick_g = ((row < 3) & (col == row)) | ((row >= 3) & (row < 6) & (col == row + pcol - 6))
    row, col = iota((16, cols), 0), iota((16, cols), 1)
    pick_p = ((row == 6) & (col == 0)) | ((row == 7) & (col == cols - 1))
    return pick_g.astype(F32).astype(BF), pick_p.astype(F32).astype(BF)


def layout_kernel(pick_ref, pre_ref, cot_ref, p_ref, g_ref, own_ref, pre_wide, cot_wide):
    frames, chans, rows, cols = pre_ref.shape
    prow, pcol = cot_ref.shape[2:]
    spread(pre_ref, pre_wide, chans)
    for r in range(rows):
        for f in range(frames):
            p_ref[pl.ds((r * frames + f) * chans, chans), :] = gathered(pre_wide, 0, frames, chans, rows, f, r)
    spread(cot_ref, cot_wide, GROUP)
    for f in range(frames):
        for y in range(prow):
            for h in range(pcol // 128):
                g_ref[pl.ds((f * prow + y) * GROUP, GROUP), h * 128 : (h + 1) * 128] = gathered(
                    cot_wide, h, frames, GROUP, prow, f, y
                )
    below = nt(pick_ref[:, pcol:], p_ref[...])[:8]
    line = frames * chans
    last = (rows - 1) * line
    below = jnp.concatenate([below[:, :line], below[:, last:], below[:, line:last]], axis=1)
    edges = nt(pick_ref[:, :pcol], g_ref[...])[:8]
    width = edges.shape[1]
    own_ref[...] = jnp.concatenate([edges + below[:, :width], below[:, width:]], axis=1).astype(BF)


def row_messages(g_ref, p_ref, ga_ref, pa_ref, gb_ref, pb_ref):
    deep, pcol = ga_ref.shape[0], g_ref.shape[1]
    chans, cols = pa_ref.shape[0], p_ref.shape[1]
    frames = pa_ref.shape[1] // cols
    tall = g_ref.shape[0] // frames
    high = p_ref.shape[0]

    def message(g_out, p_out, top):
        for f in range(frames):
            at = f * tall if top else (f + 1) * tall - deep
            g_out[:, f * pcol : (f + 1) * pcol] = g_ref[pl.ds(at, deep), :]
            at = f * chans if top else high - (frames - f) * chans
            p_out[:, f * cols : (f + 1) * cols] = p_ref[pl.ds(at, chans), :]

    even = lax.rem(lax.axis_index("ns"), 2) == 0

    @pl.when(even)
    def _():
        message(ga_ref, pa_ref, False)
        message(gb_ref, pb_ref, True)

    @pl.when(jnp.logical_not(even))
    def _():
        message(ga_ref, pa_ref, True)
        message(gb_ref, pb_ref, False)


def local_kernel(
    capacity, counts_ref, g_ref, p_ref, vis_ref, owners_ref, tokens_ref, mask_ref, proj_ref, first_ref, second_ref,
    ga_ref, pa_ref, gb_ref, pb_ref, grid_ref, pick_ref, hidden_ref, route_ref, wab_ref, w2_ref,
):
    row_messages(g_ref, p_ref, ga_ref, pa_ref, gb_ref, pb_ref)
    slots_all = tokens_ref.shape[0]
    frames, slots, patches = pick_ref.shape
    chans = proj_ref.shape[0]
    bands = second_ref.shape[1]
    slot_rows = -(-capacity // 8) * 8
    owners = route_ref.shape[0] // slot_rows
    eye = (iota((chans, chans), 0) == iota((chans, chans), 1)).astype(BF)
    pad = jnp.zeros((GROUP - bands, chans), F32)
    taps = []
    for b in range(4):
        for a in range(4):
            here = iota((bands, 4, chans), 1) == b
            tap = jnp.sum(jnp.where(here, second_ref[a].astype(F32), 0.0), axis=1)
            taps.append(jnp.concatenate([tap, pad], axis=0).astype(BF))
    w2_ref[...] = nt(eye, jnp.concatenate(taps, axis=0)).astype(BF)
    left = (iota((2 * chans, chans), 0) == iota((2 * chans, chans), 1)).astype(BF)
    right = (iota((2 * chans, chans), 0) == iota((2 * chans, chans), 1) + chans).astype(BF)
    for arrangement, (lo, hi) in enumerate(((1, 2), (3, 0))):
        taps_lo = jnp.concatenate([first_ref[a, lo] for a in range(4)], axis=0)
        taps_hi = jnp.concatenate([first_ref[a, hi] for a in range(4)], axis=0)
        wab_ref[:, arrangement * 4 * chans : (arrangement + 1) * 4 * chans] = (
            nt(left, taps_lo) + nt(right, taps_hi)
        ).astype(BF)
    vis = jnp.concatenate([vis_ref[f : f + 1, :] for f in range(frames)], axis=1)
    owner = jnp.concatenate([owners_ref[f] for f in range(frames)], axis=1)
    slot = iota((1, slots_all), 1)
    live = jnp.zeros((1, slots_all), jnp.int32)
    for f in range(frames):
        inside = (slot >= f * slots) & (slot < f * slots + counts_ref[:, f : f + 1])
        live = jnp.where(inside, 1, live)
    wanted = jnp.where(live > 0, vis, patches)
    square = (slots_all, slots_all)
    column = jnp.sum(
        jnp.where(iota(square, 0) == iota(square, 1), wanted.astype(F32), 0.0), axis=1, keepdims=True
    ).astype(jnp.int32)
    token_proj = nt(tokens_ref[...], proj_ref[...]).astype(BF)
    features = mask_ref.shape[0]
    mask_row = mask_ref[...].astype(F32).reshape(1, features)
    mask_proj = nt(jnp.broadcast_to(mask_row, (16, features)).astype(BF), proj_ref[...]).astype(BF)
    row0 = iota((16, patches), 0) == 0
    lane = iota((chans, 2 * chans), 1)
    for f in range(frames):
        hits = iota((slots, patches), 1) == column[f * slots : (f + 1) * slots]
        picks = hits.astype(F32)
        pick_ref[f] = picks.astype(BF)
        unseen = jnp.where(row0, 1.0 - jnp.sum(picks, axis=0, keepdims=True), 0.0).astype(BF)
        hidden_ref[:, f * patches : (f + 1) * patches] = unseen
        grid = tn(token_proj[f * slots : (f + 1) * slots], picks.astype(BF)) + tn(mask_proj, unseen)
        zero = jnp.zeros((chans, 2 * chans), F32)
        for line, (group, half_at) in enumerate(((1, 0), (0, 0), (0, 1), (1, 1))):
            pair = line // 2 * 2 * chans
            straight = grid[:, pair : pair + 2 * chans]
            turned = pltpu.roll(straight, chans, 1)
            to_left, to_right = (straight, turned) if line % 2 == 0 else (turned, straight)
            at = half_at * 2 * chans
            grid_ref[f, group, :chans, at : at + 2 * chans] = jnp.where(lane < chans, to_left, zero).astype(BF)
            grid_ref[f, group, chans:, at : at + 2 * chans] = jnp.where(lane < chans, zero, to_right).astype(BF)
    own_rows = -(-owners // 16) * 16
    hit = (iota((own_rows, slots_all), 0) == jnp.where(live > 0, owner, -1)).astype(F32)
    before = (iota(square, 0) < iota(square, 1)).astype(BF)
    earlier = nn(hit.astype(BF), before)
    place = jnp.sum(earlier * hit, axis=0, keepdims=True).astype(jnp.int32)
    block = lax.rem(owner, 2) * (owners // 2) + owner // 2
    target = jnp.where(live > 0, block * slot_rows + place, -1)
    route_ref[...] = (iota((owners * slot_rows, slots_all), 0) == target).astype(F32).astype(BF)


def scene_side(ref, n_ew):
    ew = lax.axis_index("ew")
    return jnp.where((ew == 0) | (ew == n_ew - 1), 0.0, ref[...].astype(F32))


def side_columns(ea_ref, eb_ref, even_ew, n_ew):
    ea, eb = ea_ref[...].astype(F32), scene_side(eb_ref, n_ew)
    return jnp.concatenate([jnp.where(even_ew, ea, eb), jnp.where(even_ew, eb, ea)], axis=0).astype(BF)


def halo_tables():
    row, col = iota((16, 128), 0), iota((16, 128), 1)
    pick_g = ((row < 3) & (col == row)) | ((row >= 11) & (row < 14) & (col == row - 8))
    pick_p = ((row == 6) & (col == 0)) | ((row == 15) & (col == 1))
    return pick_g.astype(F32).astype(BF), pick_p.astype(F32).astype(BF)


def second_backward(taps, pre, w2, drop):
    grad_hidden = nn(w2, jnp.concatenate(taps, axis=0))
    s = 0.5 + 0.5 * jnp.tanh(0.851 * pre)
    delta = grad_hidden * (s + 1.702 * pre * s * (1.0 - s))
    cols = pre.shape[1] // 2
    return jnp.where(drop, 0.0, delta).astype(BF), (pre[:, :cols] * s[:, :cols]).astype(BF)


def second_kernel_term(taps, hid):
    cols = hid.shape[1]
    zero = jnp.zeros_like(hid)
    lhs = jnp.concatenate(
        [
            jnp.concatenate([taps[0][:, :cols], taps[2][:, :cols]], axis=1),
            jnp.concatenate([taps[1][:, :cols], taps[3][:, :cols]], axis=1),
        ],
        axis=0,
    )
    rhs = jnp.concatenate(
        [jnp.concatenate([hid, zero], axis=1), jnp.concatenate([zero, hid], axis=1)], axis=0
    )
    return nt(lhs, rhs)


def outside_columns(chans, cols, n_ew, ew):
    lane = iota((chans, 2 * cols), 1)
    return ((lane == cols + cols // 2 - 1) & (ew == n_ew - 1)) | ((lane == cols + cols // 2) & (ew == 0))


def window_taps(wins, at, cols):
    return [wins[pl.ds(at, 4 * GROUP), b * 2 * cols : (b + 1) * 2 * cols] for b in range(4)]


def message_kernel(n_ew, sb_ref, sa_ref, ga_ref, pa_ref, gb_ref, pb_ref, a_ref, b_ref):
    deep, span = ga_ref.shape
    corners = jnp.concatenate([sa_ref[:, :span].astype(F32), scene_side(sb_ref, n_ew)[:, :span]], axis=0).astype(BF)
    for out, g, p in ((a_ref, ga_ref, pa_ref), (b_ref, gb_ref, pb_ref)):
        out[:deep, :span] = g[...]
        out[deep:, :span] = corners
        out[:, span:] = p[...]


def inner_kernel(
    n_ew, eb_ref, ea_ref, g_ref, p_ref, pix_ref, cell_ref, grid_ref, wab_ref, w2_ref,
    delta_ref, second_ref, first_ref, turn_ref, edge_ref, pre_ref, ext, wide, wins, pres,
):
    frames = grid_ref.shape[0]
    chans = w2_ref.shape[0]
    pcol, cols = g_ref.shape[1], p_ref.shape[1]
    tall = g_ref.shape[0] // frames
    rows = p_ref.shape[0] // (frames * chans)
    ew = lax.axis_index("ew")
    sides = side_columns(ea_ref, eb_ref, lax.rem(ew, 2) == 0, n_ew)
    pick_g, pick_p = halo_tables()
    line = frames * chans
    ext[:, :pcol] = g_ref[...]
    ext[:, pcol:] = tn(sides[:, : frames * tall], pick_g).astype(BF)
    wide[:, :cols] = p_ref[...]
    halo = tn(sides, pick_p).astype(BF)
    wide[pl.ds(0, line), cols:] = halo[:line]
    wide[pl.ds((rows - 1) * line, line), cols:] = halo[line : 2 * line]
    wide[pl.ds(line, (rows - 2) * line), cols:] = halo[2 * line :]
    deep = 3 * GROUP
    for f in range(frames):
        block = ext[pl.ds(f * tall, tall), :]
        for b in range(4):
            lanes = slice(b * 2 * cols, (b + 1) * 2 * cols)
            wins[pl.ds(f * tall, tall), lanes] = nn(block, pix_ref[:, lanes]).astype(BF)
        edge_ref[f, 0] = wins[pl.ds(f * tall, deep), :]
        edge_ref[f, 1] = wins[pl.ds((f + 1) * tall - deep, deep), :]
    pres[...] = nn(wide[...], cell_ref[...])
    for f in range(frames):
        pre_ref[f, 0] = pres[pl.ds(f * chans, chans), :]
        pre_ref[f, 1] = pres[pl.ds((rows - 1) * line + f * chans, chans), :]
    w2 = w2_ref[...]
    wab = wab_ref[...]
    drop = outside_columns(chans, cols, n_ew, ew)
    grad_second = grad_first = None
    for f in range(frames):
        deltas = []
        for i in range(1, rows - 1):
            taps = window_taps(wins, f * tall + (2 * i - 1) * GROUP, cols)
            pre = pres[pl.ds(i * line + f * chans, chans), :]
            delta, hid = second_backward(taps, pre, w2, drop)
            deltas.append(delta)
            term = second_kernel_term(taps, hid)
            grad_second = term if grad_second is None else grad_second + term
        count = rows - 2
        for k, i in enumerate((0, 1, count - 2, count - 1)):
            delta_ref[pl.ds((f * 4 + k) * chans, chans), :] = deltas[i]
        cells = []
        for i in (0, 2):
            slab = jnp.concatenate(deltas[i : i + 4], axis=0)
            cells.append(jnp.concatenate([slab[:, :cols], slab[:, cols:]], axis=0))
        both = jnp.concatenate(cells, axis=1)
        term = nt(both, grid_ref[f, 0])
        grad_first = term if grad_first is None else grad_first + term
        turn_ref[f] = nn(wab, both)
    second_ref[...] = grad_second
    first_ref[...] = grad_first


def outer_kernel(
    n_ew, n_ns, rb_ref, ra_ref, pix_ref, cell_ref,
    delta_ref, second_ref, first_ref, turn_ref, edge_ref, pre_ref,
    grid_ref, pick_ref, hidden_ref, route_ref, wab_ref, w2_ref, tokens_ref, mask_ref,
    keep_ref, give_ref, ext, wide, wins, pres,
):
    frames, slots, patches = pick_ref.shape
    chans = w2_ref.shape[0]
    features = tokens_ref.shape[1]
    cols = pre_ref.shape[3] // 2
    pcol = 2 * cols
    deep = 3 * GROUP
    ns = lax.axis_index("ns")
    ew = lax.axis_index("ew")
    even_ns = lax.rem(ns, 2) == 0
    even_ew = lax.rem(ew, 2) == 0
    ra, rb = ra_ref[...], rb_ref[...]
    north = jnp.where(even_ns, rb, ra)
    south = jnp.where(even_ns, ra, rb)
    span = frames * pcol
    tall = span // frames

    def far_sides(message):
        a, b = message[deep : deep + 8, :span].astype(F32), message[deep + 8 :, :span].astype(F32)
        return jnp.concatenate([jnp.where(even_ew, a, b), jnp.where(even_ew, b, a)], axis=0).astype(BF)

    pick_g, pick_p = halo_tables()
    line = frames * chans
    far = (far_sides(north), far_sides(south))
    for low in range(2):
        message = south if low else north
        halo_p = tn(far[low][:, (1 - low) * line : (2 - low) * line], pick_p).astype(BF)
        for f in range(frames):
            at = (f * 2 + low) * deep
            ext[pl.ds(at, deep), :pcol] = message[:deep, f * pcol : (f + 1) * pcol]
            if low:
                ext[pl.ds(at, deep), pcol:] = tn(far[low][:, f * tall : f * tall + 128], pick_g).astype(BF)[:deep]
            else:
                end = (f + 1) * tall
                ext[pl.ds(at, deep), pcol:] = tn(far[low][:, end - 128 : end], pick_g).astype(BF)[128 - deep :]
            at = (f * 2 + low) * chans
            wide[pl.ds(at, chans), :cols] = message[:, span + f * cols : span + (f + 1) * cols]
            wide[pl.ds(at, chans), cols:] = halo_p[f * chans : (f + 1) * chans]
    block = ext[...]
    for b in range(4):
        lanes = slice(b * 2 * cols, (b + 1) * 2 * cols)
        wins[:, lanes] = nn(block, pix_ref[:, lanes]).astype(BF)
    pres[...] = nn(wide[...], cell_ref[...])
    w2 = w2_ref[...]
    wab = wab_ref[...]
    drop = outside_columns(chans, cols, n_ew, ew)
    grad_second = second_ref[...]
    grad_first = first_ref[...]
    half_lane = iota((chans, cols), 1) < cols // 2
    grids = []
    for f in range(frames):
        cells = []
        for low in range(2):
            pair = []
            for k in range(2):
                inside = k == 1 - low
                beyond = wins[pl.ds((f * 2 + low) * deep, deep), :]
                window = [edge_ref[f, low], beyond] if low else [beyond, edge_ref[f, low]]
                window = jnp.concatenate(window, axis=0)[k * 2 * GROUP : (k * 2 + 4) * GROUP]
                taps = [window[:, b * 2 * cols : (b + 1) * 2 * cols] for b in range(4)]
                pre = pre_ref[f, low] if inside else pres[pl.ds((f * 2 + low) * chans, chans), :]
                gone = drop if inside else drop | (ns == (n_ns - 1 if low else 0))
                delta, hid = second_backward(taps, pre, w2, gone)
                pair.append(delta)
                if inside:
                    grad_second = grad_second + second_kernel_term(taps, hid)
            kept = delta_ref[pl.ds((f * 4 + 2 * low) * chans, 2 * chans), :]
            slab = jnp.concatenate([kept, *pair] if low else [*pair, kept], axis=0)
            cells.append(jnp.concatenate([slab[:, :cols], slab[:, cols:]], axis=0))
        both = jnp.concatenate(cells, axis=1)
        grad_first = grad_first + nt(both, grid_ref[f, 1])
        edge = nn(wab, both)
        inner = turn_ref[f]
        parts = []
        for even, odd in ((edge[:, :cols], inner[:, :cols]), (inner[:, cols:], edge[:, cols:])):
            here = jnp.where(half_lane, even[:chans], odd[chans:])
            there = jnp.where(half_lane, odd[:chans], even[chans:])
            parts.append(here + pltpu.roll(there, cols // 2, 1))
        grids.append(jnp.concatenate(parts, axis=1).astype(BF))
    none = jnp.zeros((chans, patches), BF)
    mask_sum = nt(hidden_ref[...], jnp.concatenate(grids, axis=1))
    chosen = [nt(pick_ref[f], jnp.concatenate([grids[f], none], axis=0)) for f in range(frames)]
    chosen = jnp.concatenate(chosen, axis=0)
    placed = jnp.where(even_ns, chosen, pltpu.roll(chosen, chans, 1)).astype(BF)
    chosen = chosen.astype(BF)
    routed = nn(route_ref[...], placed)
    hi = mask_sum.astype(BF).astype(F32)
    lo = mask_sum - hi
    line = iota(hi.shape, 0)
    mask_rows = jnp.where(line == 0, hi[0:1], jnp.where(line == 1, lo[0:1], 0.0)).astype(BF)
    line = iota((16, features), 0)
    mask_row = mask_ref[...].astype(F32).reshape(1, features)
    spread_row = jnp.where(line < 2, mask_row, 0.0).astype(BF)
    grad_proj = tn(chosen[:, :chans], tokens_ref[...]) + tn(mask_rows, spread_row)
    grad_proj = [grad_proj[:, k * 128 : (k + 1) * 128] for k in range(features // 128)]
    both = jnp.concatenate([hi[0:1], lo[0:1]], axis=1)
    mark = iota(grad_second.shape, 0) == MASK_ROW - SECOND_AT
    grad_second = jnp.where(mark, both, grad_second)
    halves = (grad_first, jnp.concatenate([*grad_proj, grad_second], axis=0))
    part = routed.shape[0] // 2

    def split(mine):
        keep_ref[: GRAD_ROWS // 2, :] = halves[mine]
        keep_ref[GRAD_ROWS // 2 :, :] = routed[mine * part : (mine + 1) * part]
        give_ref[: GRAD_ROWS // 2, :] = halves[1 - mine].astype(BF)
        give_ref[GRAD_ROWS // 2 :, :] = routed[(1 - mine) * part : (2 - mine) * part].astype(BF)

    @pl.when(even_ns)
    def _():
        split(0)

    @pl.when(jnp.logical_not(even_ns))
    def _():
        split(1)


def chip_kernel(rows_each, keep_ref, got_ref, out_ref):
    count = out_ref.shape[0]
    slot_rows = out_ref.shape[1] - rows_each
    grads = GRAD_ROWS // 2
    chips = (keep_ref.shape[0] - grads) // slot_rows
    total = (keep_ref[...] + got_ref[...].astype(F32)).astype(BF)
    full = min(count, grads // rows_each)
    for d in range(full):
        out_ref[d, :rows_each, :] = total[d * rows_each : (d + 1) * rows_each]
    if full < count:

        @pl.loop(full, count)
        def _(d):
            out_ref[d, :rows_each, :] = jnp.zeros((rows_each, total.shape[1]), BF)

    for z in range(chips):
        rows = total[grads + z * slot_rows : grads + (z + 1) * slot_rows]
        for e in range(count // chips):
            out_ref[e * chips + z, rows_each:, :] = rows


def sum_kernel(rows_each, got_ref, sum_ref):
    count = got_ref.shape[0]
    if count <= 64:
        total = got_ref[0, :rows_each, :].astype(F32)
        for d in range(1, count):
            total = total + got_ref[d, :rows_each, :].astype(F32)
    else:
        total = lax.fori_loop(
            0,
            count,
            lambda d, acc: acc + got_ref[d, :rows_each, :].astype(F32),
            jnp.zeros((rows_each, got_ref.shape[2]), F32),
        )
    share = total.astype(BF)
    if count <= 64:
        for d in range(count):
            sum_ref[d] = share
    else:

        @pl.loop(0, count)
        def _(d):
            sum_ref[d] = share


def owner_kernel(capacity, rows_each, arrived_ref, proj_ref, token_ref):
    chans = proj_ref.shape[0]
    slot_rows = arrived_ref.shape[1] - rows_each
    chips = token_ref.shape[0] // (2 * capacity)
    ew = lax.axis_index("ew")
    arrived = [arrived_ref[ew * chips + z, rows_each:, :].astype(F32) for z in range(chips)]
    arrived = jnp.concatenate(arrived, axis=0).astype(BF)
    shape = (token_ref.shape[0], chips * slot_rows)
    row, col = iota(shape, 0), iota(shape, 1)
    source = (row // (2 * capacity)) * slot_rows + lax.rem(row, capacity)
    picked = nn((source == col).astype(F32).astype(BF), arrived)
    second = lax.rem(iota(picked.shape, 0) // capacity, 2) == 1
    picked = jnp.where(second, pltpu.roll(picked, chans, 1), picked)[:, :chans].astype(BF)
    token_ref[...] = nn(picked, proj_ref[...]).astype(BF)


def finish_kernel(mine_ref, other_ref, proj_ref, proj_out, first_out, second_out, mask_out):
    chans, features = proj_ref.shape
    bands = second_out.shape[1]
    rows_each = mine_ref.shape[1]
    blocks = range(GRAD_ROWS // 2 // rows_each)
    mine = jnp.concatenate([mine_ref[d] for d in blocks], axis=0)
    other = jnp.concatenate([other_ref[d] for d in blocks], axis=0)
    even = lax.rem(lax.axis_index("ns"), 2) == 0
    total = [jnp.where(even, mine, other), jnp.where(even, other, mine)]
    total = jnp.concatenate(total, axis=0).astype(F32)
    for arrangement, taps in enumerate(((1, 2), (3, 0))):
        rows = total[arrangement * 4 * chans : (arrangement + 1) * 4 * chans]
        turned = pltpu.roll(rows, chans, 1)
        for a in range(4):
            first_out[a, taps[0]] = rows[a * chans : (a + 1) * chans, :chans]
            first_out[a, taps[1]] = turned[a * chans : (a + 1) * chans, :chans]
    for k in range(features // 128):
        at = PROJ_AT + k * chans
        proj_out[:, k * 128 : (k + 1) * 128] = total[at : at + chans]
    rows = total[SECOND_AT:]
    turned = pltpu.roll(rows, chans, 1)
    for b in range(2):
        for a in range(4):
            at = (b * 4 + a) * GROUP
            second_out[a, :, b, :] = rows[at : at + bands, :chans]
            second_out[a, :, b + 2, :] = turned[at : at + bands, :chans]
    at = MASK_ROW - SECOND_AT
    mask_sum = rows[at : at + 1, :chans] + turned[at : at + 1, :chans]
    hi = mask_sum.astype(BF).astype(F32)
    mid = (mask_sum - hi).astype(BF).astype(F32)
    lo = mask_sum - hi - mid
    line = iota((16, chans), 0)
    split = jnp.where(line == 0, hi, jnp.where(line == 1, mid, jnp.where(line == 2, lo, 0.0)))
    grad_mask = jnp.sum(nn(split.astype(BF), proj_ref[...]), axis=0, keepdims=True)
    mask_out[...] = grad_mask.reshape(features)


def swap(block, axis, offset, ring=False):
    count = lax.axis_size(axis)
    pairs = [(i, ((i + offset) ^ 1) - offset) for i in range(count)]
    if ring and count % 2 == 0:
        pairs = [(i, j % count) for i, j in pairs]
    return lax.ppermute(block, axis, [(i, j) for i, j in pairs if 0 <= j < count])


def call(kernel, outs, args, scratch=(), flops=0, limit=8 << 20):
    return pl.pallas_call(
        kernel,
        out_shape=outs,
        in_specs=[VMEM] * len(args),
        out_specs=jax.tree.map(lambda _: VMEM, outs),
        scratch_shapes=list(scratch),
        compiler_params=pltpu.CompilerParams(vmem_limit_bytes=limit),
        cost_estimate=pl.CostEstimate(flops=flops, bytes_accessed=1 << 10, transcendentals=0),
    )(*args)


def per_device(
    n_ew, n_ns, tokens, vis_index, counts, owners, mask_token, proj_weight, up_first, up_second, saved_pre, cotangent
):
    frames, slots, features = tokens.shape[2:]
    _, chans, rows, cols = saved_pre.shape
    bands, prow, pcol = cotangent.shape[1:]
    patches = rows * cols // 4
    count = n_ew * n_ns
    capacity = 3 * frames * slots // (2 * n_ns)
    rows_each = -(-GRAD_ROWS // count)
    rows_each = -(-rows_each // 16) * 16
    slot_rows = -(-capacity // 8) * 8
    groups = [[e * n_ns + z * 2 + c for e in range(n_ew) for z in range(n_ns // 2)] for c in range(2)]
    slots_all = frames * slots
    shape = jax.ShapeDtypeStruct

    tall = prow * GROUP
    pixels, cells, edge_picks = call(
        table_kernel,
        (shape((pcol + 128, 4 * pcol), BF), shape((pcol, pcol), BF), shape((16, pcol + cols), BF)),
        (),
        flops=1 << 33,
    )
    own_p, own_g, own_edges = call(
        layout_kernel,
        (
            shape((frames * rows * chans, cols), BF),
            shape((frames * tall, pcol), BF),
            shape((8, frames * rows * chans), BF),
        ),
        (edge_picks, saved_pre, cotangent),
        [
            pltpu.VMEM((frames * chans * rows + rows, cols), F32),
            pltpu.VMEM((frames * tall * pcol // 128 + prow, 128), F32),
        ],
        flops=1 << 33,
    )
    side_b = swap(own_edges, "ew", 1, ring=True)
    side_a = swap(own_edges, "ew", 0)

    tile_tokens = tokens.reshape(slots_all, features)
    proj = proj_weight.T
    g_message = shape((3 * GROUP, frames * pcol), BF)
    p_message = shape((chans, frames * cols), BF)
    g_a, p_a, g_b, p_b, grid, picks, hidden, route, wab, w2 = call(
        functools.partial(local_kernel, capacity),
        (
            g_message,
            p_message,
            g_message,
            p_message,
            shape((frames, 2, 2 * chans, 2 * cols), BF),
            shape((frames, slots, patches), BF),
            shape((16, frames * patches), BF),
            shape((n_ns * slot_rows, slots_all), BF),
            shape((2 * chans, 8 * chans), BF),
            shape((chans, 16 * GROUP), BF),
        ),
        (
            counts.reshape(1, frames),
            own_g,
            own_p,
            vis_index.reshape(frames, slots),
            owners.reshape(frames, 1, slots),
            tile_tokens,
            mask_token,
            proj,
            up_first,
            up_second.transpose(0, 2, 1, 3),
        ),
        flops=1 << 24,
    )
    message_shape = shape((3 * GROUP + 16, frames * (pcol + cols)), BF)
    send_a, send_b = call(
        functools.partial(message_kernel, n_ew),
        (message_shape, message_shape),
        (side_b, side_a, g_a, p_a, g_b, p_b),
        flops=1 << 20,
    )
    got_b = swap(send_b, "ns", 1)
    got_a = swap(send_a, "ns", 0)

    delta_mid, second_mid, first_mid, turn_mid, edge_wins, edge_pre = call(
        functools.partial(inner_kernel, n_ew),
        (
            shape((frames * 4 * chans, 2 * cols), BF),
            shape((2 * 4 * GROUP, 2 * chans), F32),
            shape((8 * chans, 2 * chans), F32),
            shape((frames, 2 * chans, 2 * cols), F32),
            shape((frames, 2, 3 * GROUP, 8 * cols), BF),
            shape((frames, 2, chans, 2 * cols), F32),
        ),
        (side_b, side_a, own_g, own_p, pixels, cells, grid, wab, w2),
        [
            pltpu.VMEM((frames * tall, pcol + 128), BF),
            pltpu.VMEM((rows * frames * chans, 2 * cols), BF),
            pltpu.VMEM((frames * tall, 8 * cols), BF),
            pltpu.VMEM((rows * frames * chans, 2 * cols), F32),
        ],
        flops=1 << 27,
        limit=16 << 20,
    )
    beyond = frames * 2 * 3 * GROUP
    half_rows = GRAD_ROWS // 2 + n_ns // 2 * slot_rows
    keep, give = call(
        functools.partial(outer_kernel, n_ew, n_ns),
        (shape((half_rows, 2 * chans), F32), shape((half_rows, 2 * chans), BF)),
        (
            got_b, got_a, pixels, cells, delta_mid, second_mid, first_mid, turn_mid, edge_wins, edge_pre,
            grid, picks, hidden, route, wab, w2, tile_tokens, mask_token,
        ),
        [
            pltpu.VMEM((beyond, pcol + 128), BF),
            pltpu.VMEM((frames * 2 * chans, 2 * cols), BF),
            pltpu.VMEM((beyond, 8 * cols), BF),
            pltpu.VMEM((frames * 2 * chans, 2 * cols), F32),
        ],
        flops=1 << 27,
        limit=24 << 20,
    )

    def exchange(blocks):
        return lax.all_to_all(blocks, ("ew", "ns"), 0, 0, axis_index_groups=groups, tiled=True)

    outgoing = call(
        functools.partial(chip_kernel, rows_each),
        shape((count // 2, rows_each + slot_rows, 2 * chans), BF),
        (keep, swap(give, "ns", 0)),
        flops=1 << 20,
    )
    arrived = exchange(outgoing)
    shares = call(
        functools.partial(sum_kernel, rows_each),
        shape((count // 2, rows_each, 2 * chans), BF),
        (arrived,),
        flops=1 << 20,
    )
    summed = exchange(shares)[: GRAD_ROWS // 2 // rows_each]
    other = swap(summed, "ns", 0)
    token_grad = call(
        functools.partial(owner_kernel, capacity, rows_each),
        shape((n_ns * capacity, features), BF),
        (arrived, proj),
        flops=1 << 27,
    )
    grad_proj, grad_first, grad_second, grad_mask = call(
        finish_kernel,
        (
            shape((chans, features), F32),
            shape((4, 4, chans, chans), F32),
            shape((4, bands, 4, chans), F32),
            shape((features,), F32),
        ),
        (summed, other, proj),
        flops=1 << 20,
    )
    return (token_grad[None, None], grad_proj.T, grad_first, grad_second.transpose(0, 2, 1, 3), grad_mask)


def solution(mesh):
    return jax.shard_map(
        functools.partial(per_device, mesh.shape["ew"], mesh.shape["ns"]),
        mesh=mesh,
        in_specs=(
            P("ns", "ew", None, None, None),
            P("ns", "ew", None, None),
            P("ns", "ew", None),
            P("ns", "ew", None, None, None),
            P(),
            P(),
            P(),
            P(),
            P(None, None, "ns", "ew"),
            P(None, None, "ns", "ew"),
        ),
        out_specs=(P("ns", "ew", None, None), P(), P(), P(), P()),
        check_vma=False,
    )
```

```python
import functools

import jax
import jax.numpy as jnp
import numpy as np
from jax import lax
from jax.experimental import pallas as pl
from jax.experimental.pallas import tpu as pltpu
from jax.sharding import PartitionSpec as P

BF = jnp.bfloat16
F32 = jnp.float32
VMEM = pl.BlockSpec(memory_space=pltpu.VMEM)
GROUP = 16
GRAD_ROWS = 1024
PROJ_AT = 512
SECOND_AT = 896
MASK_ROW = SECOND_AT + 12


def nn(a, b):
    return lax.dot_general(a, b, (((1,), (0,)), ((), ())), preferred_element_type=F32)


def nt(a, b):
    return lax.dot_general(a, b, (((1,), (1,)), ((), ())), preferred_element_type=F32)


def tn(a, b):
    return lax.dot_general(a, b, (((0,), (0,)), ((), ())), preferred_element_type=F32)


def iota(shape, dim):
    return lax.broadcasted_iota(jnp.int32, shape, dim)


def hidden_columns(cols, lanes):
    lane = lax.rem(lanes, cols)
    right = lane >= cols // 2
    own = 2 * jnp.where(right, lane - cols // 2, lane) + jnp.where(right, 1, 0)
    shifted = own + jnp.where(right, -2, 2)
    return jnp.where(lax.rem(lanes // cols, 2) == 0, own, shifted)


def table_kernel(pix_ref, cell_ref, pick_ref):
    cols = cell_ref.shape[0] // 2
    column_tables(cols, pix_ref, cell_ref)
    pick_g, pick_p = edge_tables(2 * cols, cols)
    pick_ref[:, : 2 * cols] = pick_g
    pick_ref[:, 2 * cols :] = pick_p


def column_tables(cols, pix_ref, cell_ref):
    fine = 2 * cols
    lanes = iota((1, fine), 1)
    hidden = hidden_columns(cols, lanes)
    for tap in range(4):
        pixel = 2 * hidden + tap - 1
        pixel = jnp.where(pixel < 0, fine + 6 + pixel, pixel)
        table = iota((fine + 128, fine), 0) == pixel
        pix_ref[:, tap * fine : (tap + 1) * fine] = table.astype(F32).astype(BF)
    cell = jnp.where(hidden < 0, cols + 1, hidden)
    cell_ref[...] = (iota((fine, fine), 0) == cell).astype(F32).astype(BF)


def spread(ref, wide, group):
    frames, real, rows, cols = ref.shape
    for f in range(frames):
        for o in range(group):
            value = ref[f, o].astype(F32) if o < real else jnp.zeros((rows, cols), F32)
            for h in range(cols // 128):
                wide[pl.ds(((h * frames + f) * group + o) * rows, rows), :] = value[:, h * 128 : (h + 1) * 128]


def gathered(wide, h, frames, group, rows, f, r):
    return wide[pl.ds((h * frames + f) * group * rows + r, group, stride=rows), :].astype(BF)


def edge_tables(pcol, cols):
    row, col = iota((16, pcol), 0), iota((16, pcol), 1)
    pick_g = ((row < 3) & (col == row)) | ((row >= 3) & (row < 6) & (col == row + pcol - 6))
    row, col = iota((16, cols), 0), iota((16, cols), 1)
    pick_p = ((row == 6) & (col == 0)) | ((row == 7) & (col == cols - 1))
    return pick_g.astype(F32).astype(BF), pick_p.astype(F32).astype(BF)


def layout_kernel(pick_ref, pre_ref, cot_ref, p_ref, g_ref, own_ref, pre_wide, cot_wide):
    frames, chans, rows, cols = pre_ref.shape
    prow, pcol = cot_ref.shape[2:]
    spread(pre_ref, pre_wide, chans)
    for r in range(rows):
        for f in range(frames):
            p_ref[pl.ds((r * frames + f) * chans, chans), :] = gathered(pre_wide, 0, frames, chans, rows, f, r)
    spread(cot_ref, cot_wide, GROUP)
    for f in range(frames):
        for y in range(prow):
            for h in range(pcol // 128):
                g_ref[pl.ds((f * prow + y) * GROUP, GROUP), h * 128 : (h + 1) * 128] = gathered(
                    cot_wide, h, frames, GROUP, prow, f, y
                )
    below = nt(pick_ref[:, pcol:], p_ref[...])[:8]
    line = frames * chans
    last = (rows - 1) * line
    below = jnp.concatenate([below[:, :line], below[:, last:], below[:, line:last]], axis=1)
    edges = nt(pick_ref[:, :pcol], g_ref[...])[:8]
    width = edges.shape[1]
    own_ref[...] = jnp.concatenate([edges + below[:, :width], below[:, width:]], axis=1).astype(BF)


def row_messages(g_ref, p_ref, ga_ref, pa_ref, gb_ref, pb_ref):
    deep, pcol = ga_ref.shape[0], g_ref.shape[1]
    chans, cols = pa_ref.shape[0], p_ref.shape[1]
    frames = pa_ref.shape[1] // cols
    tall = g_ref.shape[0] // frames
    high = p_ref.shape[0]

    def message(g_out, p_out, top):
        for f in range(frames):
            at = f * tall if top else (f + 1) * tall - deep
            g_out[:, f * pcol : (f + 1) * pcol] = g_ref[pl.ds(at, deep), :]
            at = f * chans if top else high - (frames - f) * chans
            p_out[:, f * cols : (f + 1) * cols] = p_ref[pl.ds(at, chans), :]

    even = lax.rem(lax.axis_index("ns"), 2) == 0

    @pl.when(even)
    def _():
        message(ga_ref, pa_ref, False)
        message(gb_ref, pb_ref, True)

    @pl.when(jnp.logical_not(even))
    def _():
        message(ga_ref, pa_ref, True)
        message(gb_ref, pb_ref, False)


def local_kernel(
    capacity, counts_ref, g_ref, p_ref, vis_ref, owners_ref, tokens_ref, mask_ref, proj_ref, first_ref, second_ref,
    ga_ref, pa_ref, gb_ref, pb_ref, grid_ref, pick_ref, hidden_ref, route_ref, wab_ref, w2_ref,
):
    row_messages(g_ref, p_ref, ga_ref, pa_ref, gb_ref, pb_ref)
    slots_all = tokens_ref.shape[0]
    frames, slots, patches = pick_ref.shape
    chans = proj_ref.shape[0]
    bands = second_ref.shape[1]
    slot_rows = -(-capacity // 8) * 8
    owners = route_ref.shape[0] // slot_rows
    eye = (iota((chans, chans), 0) == iota((chans, chans), 1)).astype(BF)
    pad = jnp.zeros((GROUP - bands, chans), F32)
    taps = []
    for b in range(4):
        for a in range(4):
            here = iota((bands, 4, chans), 1) == b
            tap = jnp.sum(jnp.where(here, second_ref[a].astype(F32), 0.0), axis=1)
            taps.append(jnp.concatenate([tap, pad], axis=0).astype(BF))
    w2_ref[...] = nt(eye, jnp.concatenate(taps, axis=0)).astype(BF)
    left = (iota((2 * chans, chans), 0) == iota((2 * chans, chans), 1)).astype(BF)
    right = (iota((2 * chans, chans), 0) == iota((2 * chans, chans), 1) + chans).astype(BF)
    for arrangement, (lo, hi) in enumerate(((1, 2), (3, 0))):
        taps_lo = jnp.concatenate([first_ref[a, lo] for a in range(4)], axis=0)
        taps_hi = jnp.concatenate([first_ref[a, hi] for a in range(4)], axis=0)
        wab_ref[:, arrangement * 4 * chans : (arrangement + 1) * 4 * chans] = (
            nt(left, taps_lo) + nt(right, taps_hi)
        ).astype(BF)
    vis = jnp.concatenate([vis_ref[f : f + 1, :] for f in range(frames)], axis=1)
    owner = jnp.concatenate([owners_ref[f] for f in range(frames)], axis=1)
    slot = iota((1, slots_all), 1)
    live = jnp.zeros((1, slots_all), jnp.int32)
    for f in range(frames):
        inside = (slot >= f * slots) & (slot < f * slots + counts_ref[:, f : f + 1])
        live = jnp.where(inside, 1, live)
    wanted = jnp.where(live > 0, vis, patches)
    square = (slots_all, slots_all)
    column = jnp.sum(
        jnp.where(iota(square, 0) == iota(square, 1), wanted.astype(F32), 0.0), axis=1, keepdims=True
    ).astype(jnp.int32)
    token_proj = nt(tokens_ref[...], proj_ref[...]).astype(BF)
    features = mask_ref.shape[0]
    mask_row = mask_ref[...].astype(F32).reshape(1, features)
    mask_proj = nt(jnp.broadcast_to(mask_row, (16, features)).astype(BF), proj_ref[...]).astype(BF)
    row0 = iota((16, patches), 0) == 0
    lane = iota((chans, 2 * chans), 1)
    for f in range(frames):
        hits = iota((slots, patches), 1) == column[f * slots : (f + 1) * slots]
        picks = hits.astype(F32)
        pick_ref[f] = picks.astype(BF)
        unseen = jnp.where(row0, 1.0 - jnp.sum(picks, axis=0, keepdims=True), 0.0).astype(BF)
        hidden_ref[:, f * patches : (f + 1) * patches] = unseen
        grid = tn(token_proj[f * slots : (f + 1) * slots], picks.astype(BF)) + tn(mask_proj, unseen)
        zero = jnp.zeros((chans, 2 * chans), F32)
        for line, (group, half_at) in enumerate(((1, 0), (0, 0), (0, 1), (1, 1))):
            pair = line // 2 * 2 * chans
            straight = grid[:, pair : pair + 2 * chans]
            turned = pltpu.roll(straight, chans, 1)
            to_left, to_right = (straight, turned) if line % 2 == 0 else (turned, straight)
            at = half_at * 2 * chans
            grid_ref[f, group, :chans, at : at + 2 * chans] = jnp.where(lane < chans, to_left, zero).astype(BF)
            grid_ref[f, group, chans:, at : at + 2 * chans] = jnp.where(lane < chans, zero, to_right).astype(BF)
    own_rows = -(-owners // 16) * 16
    hit = (iota((own_rows, slots_all), 0) == jnp.where(live > 0, owner, -1)).astype(F32)
    before = (iota(square, 0) < iota(square, 1)).astype(BF)
    earlier = nn(hit.astype(BF), before)
    place = jnp.sum(earlier * hit, axis=0, keepdims=True).astype(jnp.int32)
    block = lax.rem(owner, 2) * (owners // 2) + owner // 2
    target = jnp.where(live > 0, block * slot_rows + place, -1)
    route_ref[...] = (iota((owners * slot_rows, slots_all), 0) == target).astype(F32).astype(BF)


def scene_side(ref, n_ew):
    ew = lax.axis_index("ew")
    return jnp.where((ew == 0) | (ew == n_ew - 1), 0.0, ref[...].astype(F32))


def side_columns(ea_ref, eb_ref, even_ew, n_ew):
    ea, eb = ea_ref[...].astype(F32), scene_side(eb_ref, n_ew)
    return jnp.concatenate([jnp.where(even_ew, ea, eb), jnp.where(even_ew, eb, ea)], axis=0).astype(BF)


def halo_tables():
    row, col = iota((16, 128), 0), iota((16, 128), 1)
    pick_g = ((row < 3) & (col == row)) | ((row >= 11) & (row < 14) & (col == row - 8))
    pick_p = ((row == 6) & (col == 0)) | ((row == 15) & (col == 1))
    return pick_g.astype(F32).astype(BF), pick_p.astype(F32).astype(BF)


def second_backward(taps, pre, w2, drop):
    grad_hidden = nn(w2, jnp.concatenate(taps, axis=0))
    s = 0.5 + 0.5 * jnp.tanh(0.851 * pre)
    delta = grad_hidden * (s + 1.702 * pre * s * (1.0 - s))
    cols = pre.shape[1] // 2
    return jnp.where(drop, 0.0, delta).astype(BF), (pre[:, :cols] * s[:, :cols]).astype(BF)


def second_kernel_term(taps, hid):
    cols = hid.shape[1]
    zero = jnp.zeros_like(hid)
    lhs = jnp.concatenate(
        [
            jnp.concatenate([taps[0][:, :cols], taps[2][:, :cols]], axis=1),
            jnp.concatenate([taps[1][:, :cols], taps[3][:, :cols]], axis=1),
        ],
        axis=0,
    )
    rhs = jnp.concatenate(
        [jnp.concatenate([hid, zero], axis=1), jnp.concatenate([zero, hid], axis=1)], axis=0
    )
    return nt(lhs, rhs)


def outside_columns(chans, cols, n_ew, ew):
    lane = iota((chans, 2 * cols), 1)
    return ((lane == cols + cols // 2 - 1) & (ew == n_ew - 1)) | ((lane == cols + cols // 2) & (ew == 0))


def window_taps(wins, at, cols):
    return [wins[pl.ds(at, 4 * GROUP), b * 2 * cols : (b + 1) * 2 * cols] for b in range(4)]


def message_kernel(n_ew, sb_ref, sa_ref, ga_ref, pa_ref, gb_ref, pb_ref, a_ref, b_ref):
    deep, span = ga_ref.shape
    corners = jnp.concatenate([sa_ref[:, :span].astype(F32), scene_side(sb_ref, n_ew)[:, :span]], axis=0).astype(BF)
    for out, g, p in ((a_ref, ga_ref, pa_ref), (b_ref, gb_ref, pb_ref)):
        out[:deep, :span] = g[...]
        out[deep:, :span] = corners
        out[:, span:] = p[...]


def inner_kernel(
    n_ew, eb_ref, ea_ref, g_ref, p_ref, pix_ref, cell_ref, grid_ref, wab_ref, w2_ref,
    delta_ref, second_ref, first_ref, turn_ref, edge_ref, pre_ref, ext, wide, wins, pres,
):
    frames = grid_ref.shape[0]
    chans = w2_ref.shape[0]
    pcol, cols = g_ref.shape[1], p_ref.shape[1]
    tall = g_ref.shape[0] // frames
    rows = p_ref.shape[0] // (frames * chans)
    ew = lax.axis_index("ew")
    sides = side_columns(ea_ref, eb_ref, lax.rem(ew, 2) == 0, n_ew)
    pick_g, pick_p = halo_tables()
    line = frames * chans
    ext[:, :pcol] = g_ref[...]
    ext[:, pcol:] = tn(sides[:, : frames * tall], pick_g).astype(BF)
    wide[:, :cols] = p_ref[...]
    halo = tn(sides, pick_p).astype(BF)
    wide[pl.ds(0, line), cols:] = halo[:line]
    wide[pl.ds((rows - 1) * line, line), cols:] = halo[line : 2 * line]
    wide[pl.ds(line, (rows - 2) * line), cols:] = halo[2 * line :]
    deep = 3 * GROUP
    for f in range(frames):
        block = ext[pl.ds(f * tall, tall), :]
        for b in range(4):
            lanes = slice(b * 2 * cols, (b + 1) * 2 * cols)
            wins[pl.ds(f * tall, tall), lanes] = nn(block, pix_ref[:, lanes]).astype(BF)
        edge_ref[f, 0] = wins[pl.ds(f * tall, deep), :]
        edge_ref[f, 1] = wins[pl.ds((f + 1) * tall - deep, deep), :]
    pres[...] = nn(wide[...], cell_ref[...])
    for f in range(frames):
        pre_ref[f, 0] = pres[pl.ds(f * chans, chans), :]
        pre_ref[f, 1] = pres[pl.ds((rows - 1) * line + f * chans, chans), :]
    w2 = w2_ref[...]
    wab = wab_ref[...]
    drop = outside_columns(chans, cols, n_ew, ew)
    grad_second = grad_first = None
    for f in range(frames):
        deltas = []
        for i in range(1, rows - 1):
            taps = window_taps(wins, f * tall + (2 * i - 1) * GROUP, cols)
            pre = pres[pl.ds(i * line + f * chans, chans), :]
            delta, hid = second_backward(taps, pre, w2, drop)
            deltas.append(delta)
            term = second_kernel_term(taps, hid)
            grad_second = term if grad_second is None else grad_second + term
        count = rows - 2
        for k, i in enumerate((0, 1, count - 2, count - 1)):
            delta_ref[pl.ds((f * 4 + k) * chans, chans), :] = deltas[i]
        cells = []
        for i in (0, 2):
            slab = jnp.concatenate(deltas[i : i + 4], axis=0)
            cells.append(jnp.concatenate([slab[:, :cols], slab[:, cols:]], axis=0))
        both = jnp.concatenate(cells, axis=1)
        term = nt(both, grid_ref[f, 0])
        grad_first = term if grad_first is None else grad_first + term
        turn_ref[f] = nn(wab, both)
    second_ref[...] = grad_second
    first_ref[...] = grad_first


def outer_kernel(
    n_ew, n_ns, rb_ref, ra_ref, pix_ref, cell_ref,
    delta_ref, second_ref, first_ref, turn_ref, edge_ref, pre_ref,
    grid_ref, pick_ref, hidden_ref, route_ref, wab_ref, w2_ref, tokens_ref, mask_ref,
    keep_ref, give_ref, ext, wide, wins, pres,
):
    frames, slots, patches = pick_ref.shape
    chans = w2_ref.shape[0]
    features = tokens_ref.shape[1]
    cols = pre_ref.shape[3] // 2
    pcol = 2 * cols
    deep = 3 * GROUP
    ns = lax.axis_index("ns")
    ew = lax.axis_index("ew")
    even_ns = lax.rem(ns, 2) == 0
    even_ew = lax.rem(ew, 2) == 0
    ra, rb = ra_ref[...], rb_ref[...]
    rb = jnp.where((ns == 0) | (ns == n_ns - 1), jnp.zeros_like(rb), rb)
    north = jnp.where(even_ns, rb, ra)
    south = jnp.where(even_ns, ra, rb)
    span = frames * pcol
    tall = span // frames

    def far_sides(message):
        a, b = message[deep : deep + 8, :span].astype(F32), message[deep + 8 :, :span].astype(F32)
        return jnp.concatenate([jnp.where(even_ew, a, b), jnp.where(even_ew, b, a)], axis=0).astype(BF)

    pick_g, pick_p = halo_tables()
    line = frames * chans
    far = (far_sides(north), far_sides(south))
    for low in range(2):
        message = south if low else north
        halo_p = tn(far[low][:, (1 - low) * line : (2 - low) * line], pick_p).astype(BF)
        for f in range(frames):
            at = (f * 2 + low) * deep
            ext[pl.ds(at, deep), :pcol] = message[:deep, f * pcol : (f + 1) * pcol]
            if low:
                ext[pl.ds(at, deep), pcol:] = tn(far[low][:, f * tall : f * tall + 128], pick_g).astype(BF)[:deep]
            else:
                end = (f + 1) * tall
                ext[pl.ds(at, deep), pcol:] = tn(far[low][:, end - 128 : end], pick_g).astype(BF)[128 - deep :]
            at = (f * 2 + low) * chans
            wide[pl.ds(at, chans), :cols] = message[:, span + f * cols : span + (f + 1) * cols]
            wide[pl.ds(at, chans), cols:] = halo_p[f * chans : (f + 1) * chans]
    block = ext[...]
    for b in range(4):
        lanes = slice(b * 2 * cols, (b + 1) * 2 * cols)
        wins[:, lanes] = nn(block, pix_ref[:, lanes]).astype(BF)
    pres[...] = nn(wide[...], cell_ref[...])
    w2 = w2_ref[...]
    wab = wab_ref[...]
    drop = outside_columns(chans, cols, n_ew, ew)
    grad_second = second_ref[...]
    grad_first = first_ref[...]
    half_lane = iota((chans, cols), 1) < cols // 2
    grids = []
    for f in range(frames):
        cells = []
        for low in range(2):
            pair = []
            for k in range(2):
                inside = k == 1 - low
                beyond = wins[pl.ds((f * 2 + low) * deep, deep), :]
                window = [edge_ref[f, low], beyond] if low else [beyond, edge_ref[f, low]]
                window = jnp.concatenate(window, axis=0)[k * 2 * GROUP : (k * 2 + 4) * GROUP]
                taps = [window[:, b * 2 * cols : (b + 1) * 2 * cols] for b in range(4)]
                pre = pre_ref[f, low] if inside else pres[pl.ds((f * 2 + low) * chans, chans), :]
                gone = drop if inside else drop | (ns == (n_ns - 1 if low else 0))
                delta, hid = second_backward(taps, pre, w2, gone)
                pair.append(delta)
                if inside:
                    grad_second = grad_second + second_kernel_term(taps, hid)
            kept = delta_ref[pl.ds((f * 4 + 2 * low) * chans, 2 * chans), :]
            slab = jnp.concatenate([kept, *pair] if low else [*pair, kept], axis=0)
            cells.append(jnp.concatenate([slab[:, :cols], slab[:, cols:]], axis=0))
        both = jnp.concatenate(cells, axis=1)
        grad_first = grad_first + nt(both, grid_ref[f, 1])
        edge = nn(wab, both)
        inner = turn_ref[f]
        parts = []
        for even, odd in ((edge[:, :cols], inner[:, :cols]), (inner[:, cols:], edge[:, cols:])):
            here = jnp.where(half_lane, even[:chans], odd[chans:])
            there = jnp.where(half_lane, odd[:chans], even[chans:])
            parts.append(here + pltpu.roll(there, cols // 2, 1))
        grids.append(jnp.concatenate(parts, axis=1).astype(BF))
    none = jnp.zeros((chans, patches), BF)
    mask_sum = nt(hidden_ref[...], jnp.concatenate(grids, axis=1))
    chosen = [nt(pick_ref[f], jnp.concatenate([grids[f], none], axis=0)) for f in range(frames)]
    chosen = jnp.concatenate(chosen, axis=0)
    placed = jnp.where(even_ns, chosen, pltpu.roll(chosen, chans, 1)).astype(BF)
    chosen = chosen.astype(BF)
    routed = nn(route_ref[...], placed)
    hi = mask_sum.astype(BF).astype(F32)
    lo = mask_sum - hi
    line = iota(hi.shape, 0)
    mask_rows = jnp.where(line == 0, hi[0:1], jnp.where(line == 1, lo[0:1], 0.0)).astype(BF)
    line = iota((16, features), 0)
    mask_row = mask_ref[...].astype(F32).reshape(1, features)
    spread_row = jnp.where(line < 2, mask_row, 0.0).astype(BF)
    grad_proj = tn(chosen[:, :chans], tokens_ref[...]) + tn(mask_rows, spread_row)
    grad_proj = [grad_proj[:, k * 128 : (k + 1) * 128] for k in range(features // 128)]
    both = jnp.concatenate([hi[0:1], lo[0:1]], axis=1)
    mark = iota(grad_second.shape, 0) == MASK_ROW - SECOND_AT
    grad_second = jnp.where(mark, both, grad_second)
    halves = (grad_first, jnp.concatenate([*grad_proj, grad_second], axis=0))
    part = routed.shape[0] // 2

    def split(mine):
        keep_ref[: GRAD_ROWS // 2, :] = halves[mine]
        keep_ref[GRAD_ROWS // 2 :, :] = routed[mine * part : (mine + 1) * part]
        give_ref[: GRAD_ROWS // 2, :] = halves[1 - mine].astype(BF)
        give_ref[GRAD_ROWS // 2 :, :] = routed[(1 - mine) * part : (2 - mine) * part].astype(BF)

    @pl.when(even_ns)
    def _():
        split(0)

    @pl.when(jnp.logical_not(even_ns))
    def _():
        split(1)


def chip_kernel(rows_each, keep_ref, got_ref, out_ref):
    count = out_ref.shape[0]
    slot_rows = out_ref.shape[1] - rows_each
    grads = GRAD_ROWS // 2
    chips = (keep_ref.shape[0] - grads) // slot_rows
    total = (keep_ref[...] + got_ref[...].astype(F32)).astype(BF)
    full = min(count, grads // rows_each)
    for d in range(full):
        out_ref[d, :rows_each, :] = total[d * rows_each : (d + 1) * rows_each]
    if full < count:

        @pl.loop(full, count)
        def _(d):
            out_ref[d, :rows_each, :] = jnp.zeros((rows_each, total.shape[1]), BF)

    for z in range(chips):
        rows = total[grads + z * slot_rows : grads + (z + 1) * slot_rows]
        for e in range(count // chips):
            out_ref[e * chips + z, rows_each:, :] = rows


def sum_kernel(rows_each, got_ref, sum_ref):
    count = got_ref.shape[0]
    if count <= 64:
        total = got_ref[0, :rows_each, :].astype(F32)
        for d in range(1, count):
            total = total + got_ref[d, :rows_each, :].astype(F32)
    else:
        total = lax.fori_loop(
            0,
            count,
            lambda d, acc: acc + got_ref[d, :rows_each, :].astype(F32),
            jnp.zeros((rows_each, got_ref.shape[2]), F32),
        )
    share = total.astype(BF)
    if count <= 64:
        for d in range(count):
            sum_ref[d] = share
    else:

        @pl.loop(0, count)
        def _(d):
            sum_ref[d] = share


def owner_kernel(capacity, rows_each, arrived_ref, proj_ref, token_ref):
    chans = proj_ref.shape[0]
    slot_rows = arrived_ref.shape[1] - rows_each
    chips = token_ref.shape[0] // (2 * capacity)
    ew = lax.axis_index("ew")
    arrived = [arrived_ref[ew * chips + z, rows_each:, :].astype(F32) for z in range(chips)]
    arrived = jnp.concatenate(arrived, axis=0).astype(BF)
    shape = (token_ref.shape[0], chips * slot_rows)
    row, col = iota(shape, 0), iota(shape, 1)
    source = (row // (2 * capacity)) * slot_rows + lax.rem(row, capacity)
    picked = nn((source == col).astype(F32).astype(BF), arrived)
    second = lax.rem(iota(picked.shape, 0) // capacity, 2) == 1
    picked = jnp.where(second, pltpu.roll(picked, chans, 1), picked)[:, :chans].astype(BF)
    token_ref[...] = nn(picked, proj_ref[...]).astype(BF)


def finish_kernel(mine_ref, other_ref, proj_ref, proj_out, first_out, second_out, mask_out):
    chans, features = proj_ref.shape
    bands = second_out.shape[1]
    rows_each = mine_ref.shape[1]
    blocks = range(GRAD_ROWS // 2 // rows_each)
    mine = jnp.concatenate([mine_ref[d] for d in blocks], axis=0)
    other = jnp.concatenate([other_ref[d] for d in blocks], axis=0)
    even = lax.rem(lax.axis_index("ns"), 2) == 0
    total = [jnp.where(even, mine, other), jnp.where(even, other, mine)]
    total = jnp.concatenate(total, axis=0).astype(F32)
    for arrangement, taps in enumerate(((1, 2), (3, 0))):
        rows = total[arrangement * 4 * chans : (arrangement + 1) * 4 * chans]
        turned = pltpu.roll(rows, chans, 1)
        for a in range(4):
            first_out[a, taps[0]] = rows[a * chans : (a + 1) * chans, :chans]
            first_out[a, taps[1]] = turned[a * chans : (a + 1) * chans, :chans]
    for k in range(features // 128):
        at = PROJ_AT + k * chans
        proj_out[:, k * 128 : (k + 1) * 128] = total[at : at + chans]
    rows = total[SECOND_AT:]
    turned = pltpu.roll(rows, chans, 1)
    for b in range(2):
        for a in range(4):
            at = (b * 4 + a) * GROUP
            second_out[a, :, b, :] = rows[at : at + bands, :chans]
            second_out[a, :, b + 2, :] = turned[at : at + bands, :chans]
    at = MASK_ROW - SECOND_AT
    mask_sum = rows[at : at + 1, :chans] + turned[at : at + 1, :chans]
    hi = mask_sum.astype(BF).astype(F32)
    mid = (mask_sum - hi).astype(BF).astype(F32)
    lo = mask_sum - hi - mid
    line = iota((16, chans), 0)
    split = jnp.where(line == 0, hi, jnp.where(line == 1, mid, jnp.where(line == 2, lo, 0.0)))
    grad_mask = jnp.sum(nn(split.astype(BF), proj_ref[...]), axis=0, keepdims=True)
    mask_out[...] = grad_mask.reshape(features)


def swap(block, axis, offset, ring=False):
    count = lax.axis_size(axis)
    pairs = [(i, ((i + offset) ^ 1) - offset) for i in range(count)]
    if ring and count % 2 == 0:
        pairs = [(i, j % count) for i, j in pairs]
    return lax.ppermute(block, axis, [(i, j) for i, j in pairs if 0 <= j < count])


def call(kernel, outs, args, scratch=(), flops=0, limit=8 << 20):
    return pl.pallas_call(
        kernel,
        out_shape=outs,
        in_specs=[VMEM] * len(args),
        out_specs=jax.tree.map(lambda _: VMEM, outs),
        scratch_shapes=list(scratch),
        compiler_params=pltpu.CompilerParams(vmem_limit_bytes=limit),
        cost_estimate=pl.CostEstimate(flops=flops, bytes_accessed=1 << 10, transcendentals=0),
    )(*args)


def per_device(
    n_ew, n_ns, tokens, vis_index, counts, owners, mask_token, proj_weight, up_first, up_second, saved_pre, cotangent
):
    frames, slots, features = tokens.shape[2:]
    _, chans, rows, cols = saved_pre.shape
    bands, prow, pcol = cotangent.shape[1:]
    patches = rows * cols // 4
    count = n_ew * n_ns
    capacity = 3 * frames * slots // (2 * n_ns)
    rows_each = -(-GRAD_ROWS // count)
    rows_each = -(-rows_each // 16) * 16
    slot_rows = -(-capacity // 8) * 8
    groups = [[e * n_ns + z * 2 + c for e in range(n_ew) for z in range(n_ns // 2)] for c in range(2)]
    slots_all = frames * slots
    shape = jax.ShapeDtypeStruct

    tall = prow * GROUP
    pixels, cells, edge_picks = call(
        table_kernel,
        (shape((pcol + 128, 4 * pcol), BF), shape((pcol, pcol), BF), shape((16, pcol + cols), BF)),
        (),
        flops=1 << 33,
    )
    own_p, own_g, own_edges = call(
        layout_kernel,
        (
            shape((frames * rows * chans, cols), BF),
            shape((frames * tall, pcol), BF),
            shape((8, frames * rows * chans), BF),
        ),
        (edge_picks, saved_pre, cotangent),
        [
            pltpu.VMEM((frames * chans * rows + rows, cols), F32),
            pltpu.VMEM((frames * tall * pcol // 128 + prow, 128), F32),
        ],
        flops=1 << 33,
    )
    side_b = swap(own_edges, "ew", 1, ring=True)
    side_a = swap(own_edges, "ew", 0)

    tile_tokens = tokens.reshape(slots_all, features)
    proj = proj_weight.T
    g_message = shape((3 * GROUP, frames * pcol), BF)
    p_message = shape((chans, frames * cols), BF)
    g_a, p_a, g_b, p_b, grid, picks, hidden, route, wab, w2 = call(
        functools.partial(local_kernel, capacity),
        (
            g_message,
            p_message,
            g_message,
            p_message,
            shape((frames, 2, 2 * chans, 2 * cols), BF),
            shape((frames, slots, patches), BF),
            shape((16, frames * patches), BF),
            shape((n_ns * slot_rows, slots_all), BF),
            shape((2 * chans, 8 * chans), BF),
            shape((chans, 16 * GROUP), BF),
        ),
        (
            counts.reshape(1, frames),
            own_g,
            own_p,
            vis_index.reshape(frames, slots),
            owners.reshape(frames, 1, slots),
            tile_tokens,
            mask_token,
            proj,
            up_first,
            up_second.transpose(0, 2, 1, 3),
        ),
        flops=1 << 24,
    )
    message_shape = shape((3 * GROUP + 16, frames * (pcol + cols)), BF)
    send_a, send_b = call(
        functools.partial(message_kernel, n_ew),
        (message_shape, message_shape),
        (side_b, side_a, g_a, p_a, g_b, p_b),
        flops=1 << 20,
    )
    got_b = swap(send_b, "ns", 1, ring=True)
    got_a = swap(send_a, "ns", 0)

    delta_mid, second_mid, first_mid, turn_mid, edge_wins, edge_pre = call(
        functools.partial(inner_kernel, n_ew),
        (
            shape((frames * 4 * chans, 2 * cols), BF),
            shape((2 * 4 * GROUP, 2 * chans), F32),
            shape((8 * chans, 2 * chans), F32),
            shape((frames, 2 * chans, 2 * cols), F32),
            shape((frames, 2, 3 * GROUP, 8 * cols), BF),
            shape((frames, 2, chans, 2 * cols), F32),
        ),
        (side_b, side_a, own_g, own_p, pixels, cells, grid, wab, w2),
        [
            pltpu.VMEM((frames * tall, pcol + 128), BF),
            pltpu.VMEM((rows * frames * chans, 2 * cols), BF),
            pltpu.VMEM((frames * tall, 8 * cols), BF),
            pltpu.VMEM((rows * frames * chans, 2 * cols), F32),
        ],
        flops=1 << 27,
        limit=16 << 20,
    )
    beyond = frames * 2 * 3 * GROUP
    half_rows = GRAD_ROWS // 2 + n_ns // 2 * slot_rows
    keep, give = call(
        functools.partial(outer_kernel, n_ew, n_ns),
        (shape((half_rows, 2 * chans), F32), shape((half_rows, 2 * chans), BF)),
        (
            got_b, got_a, pixels, cells, delta_mid, second_mid, first_mid, turn_mid, edge_wins, edge_pre,
            grid, picks, hidden, route, wab, w2, tile_tokens, mask_token,
        ),
        [
            pltpu.VMEM((beyond, pcol + 128), BF),
            pltpu.VMEM((frames * 2 * chans, 2 * cols), BF),
            pltpu.VMEM((beyond, 8 * cols), BF),
            pltpu.VMEM((frames * 2 * chans, 2 * cols), F32),
        ],
        flops=1 << 27,
        limit=24 << 20,
    )

    def exchange(blocks):
        return lax.all_to_all(blocks, ("ew", "ns"), 0, 0, axis_index_groups=groups, tiled=True)

    outgoing = call(
        functools.partial(chip_kernel, rows_each),
        shape((count // 2, rows_each + slot_rows, 2 * chans), BF),
        (keep, swap(give, "ns", 0)),
        flops=1 << 20,
    )
    arrived = exchange(outgoing)
    shares = call(
        functools.partial(sum_kernel, rows_each),
        shape((count // 2, rows_each, 2 * chans), BF),
        (arrived,),
        flops=1 << 20,
    )
    summed = exchange(shares)[: GRAD_ROWS // 2 // rows_each]
    other = swap(summed, "ns", 0)
    token_grad = call(
        functools.partial(owner_kernel, capacity, rows_each),
        shape((n_ns * capacity, features), BF),
        (arrived, proj),
        flops=1 << 27,
    )
    grad_proj, grad_first, grad_second, grad_mask = call(
        finish_kernel,
        (
            shape((chans, features), F32),
            shape((4, 4, chans, chans), F32),
            shape((4, bands, 4, chans), F32),
            shape((features,), F32),
        ),
        (summed, other, proj),
        flops=1 << 20,
    )
    return (token_grad[None, None], grad_proj.T, grad_first, grad_second.transpose(0, 2, 1, 3), grad_mask)


def solution(mesh):
    return jax.shard_map(
        functools.partial(per_device, mesh.shape["ew"], mesh.shape["ns"]),
        mesh=mesh,
        in_specs=(
            P("ns", "ew", None, None, None),
            P("ns", "ew", None, None),
            P("ns", "ew", None),
            P("ns", "ew", None, None, None),
            P(),
            P(),
            P(),
            P(),
            P(None, None, "ns", "ew"),
            P(None, None, "ns", "ew"),
        ),
        out_specs=(P("ns", "ew", None, None), P(), P(), P(), P()),
        check_vma=False,
    )
```
